32 devices in a mesh: dp: 8 (over z, x), group: 4 (over y, core).
Axes of the slice: x: 2, y: 2, z: 4, core: 2. Of those that a mesh axis runs over, the one named last changes fastest.
Arguments:
- series_in: bfloat16 [73728, 512], P(('dp', 'group')), may hold values from -6 to 6
- block_kinds: int32 [384], P(('dp', 'group')), may hold values from 0 to 2, as said below
- out_grad: bfloat16 [73728, 512], P(('dp', 'group')), may hold values from -6 to 6
- fine_shrink: bfloat16 [6144, 512], P('dp'), may hold values from -0.078125 to 0.078125
- coarse_shrink: bfloat16 [8192, 512], P('dp'), may hold values from -0.0625 to 0.0625
- fine_isometric: bfloat16 [8192, 512], P('dp'), may hold values from -0.0625 to 0.0625
- coarse_isometric: bfloat16 [6144, 512], P('dp'), may hold values from -0.078125 to 0.078125
- fine_grow: bfloat16 [512, 6144], P('dp'), may hold values from -0.25 to 0.25
- coarse_grow: bfloat16 [512, 8192], P('dp'), may hold values from -0.25 to 0.25
- merge_weight: bfloat16 [1024, 512], P('dp'), may hold values from -0.1875 to 0.1875
- expand_weight: bfloat16 [512, 2048], P('dp'), may hold values from -0.25 to 0.25
- contract_weight: bfloat16 [2048, 512], P('dp'), may hold values from -0.125 to 0.125
- trend_weight: bfloat16 [512, 512], P('dp'), may hold values from -1.25 to 1.25
- branch_gain: bfloat16 [512], P('dp'), may hold values from 0.099609375 to 1.8984375
- middle_gain: bfloat16 [512], P('dp'), may hold values from 0.099609375 to 1.8984375
- output_gain: bfloat16 [512], P('dp'), may hold values from 0.099609375 to 1.8984375
Outputs:
- series_out: bfloat16 [73728, 512], P(('dp', 'group'))
- series_grad: bfloat16 [73728, 512], P(('dp', 'group'))
- fine_shrink_grad: float32 [6144, 512], P('dp')
- coarse_shrink_grad: float32 [8192, 512], P('dp')
- fine_isometric_grad: float32 [8192, 512], P('dp')
- coarse_isometric_grad: float32 [6144, 512], P('dp')
- fine_grow_grad: float32 [512, 6144], P('dp')
- coarse_grow_grad: float32 [512, 8192], P('dp')
- merge_grad: float32 [1024, 512], P('dp')
- expand_grad: float32 [512, 2048], P('dp')
- contract_grad: float32 [2048, 512], P('dp')
- trend_grad: float32 [512, 512], P('dp')
- branch_gain_grad: float32 [512], P('dp')
- middle_gain_grad: float32 [512], P('dp')
- output_gain_grad: float32 [512], P('dp')
The draws below stay inside these ranges and needn't reach their ends.
Inputs may be any that keep to these rules, and one draw needn't show every extreme that they name: `block_kinds`: 0 starts an hourly series of one block, 1 starts a fifteen-minute series of four blocks, 2 continues the series of the block before; every aligned group of four blocks begins a series.
All inputs are finite; a program needn't handle non-finite values.
Results may differ from the reference program's by a relative error of at most 0.02.
Values may be sent and summed in bfloat16 or wider, within the bound.
No kernel may reach another device: no remote copies, remote signals or barrier semaphores. Data moves between devices by JAX's collectives and lax.ppermute only.
A program may use at most 320 MiB of HBM per device.

```python
import jax
import jax.numpy as jnp
from jax import lax

D = 512
FF = 2048
HOUR = 192
S1 = 12
S2 = 16
WINDOW = 25
NBLK = 384
TOKENS = 73728


def draw_block_kinds(key, part):
    key = jax.random.fold_in(key, 7)
    groups = NBLK // 4
    picks = jax.random.randint(key, (groups,), 0, 2)
    picks = picks.at[0].set(1).at[groups - 1].set(0)
    quarter = jnp.array([1, 2, 2, 2], jnp.int32)
    hourly = jnp.zeros((4,), jnp.int32)
    layout = jnp.where(picks[:, None] == 1, quarter[None, :], hourly[None, :])
    return layout.reshape(-1).astype(jnp.int32)


def shard_levels(key, extent, cuts, least, top_value):
    level = 1.0
    for dim, blocks in cuts:
        draws = jax.random.uniform(jax.random.fold_in(jax.random.fold_in(key, 6), dim), (blocks,), jnp.float32, least / len(cuts), top_value / len(cuts))
        level = level * jnp.repeat(jnp.exp(draws), extent[dim] // blocks).reshape((-1,) + (1,) * (len(extent) - 1 - dim))
    return level


def noise(stream_key, shape, deviation, limit, split=(), kind=jnp.bfloat16):
    values = deviation * jax.random.normal(stream_key, shape, jnp.float32)
    if split:
        values = values * shard_levels(stream_key, shape, split, -0.22, 0.18)
    return jnp.clip(values, -limit, limit).astype(kind)


def setup_inputs(seed: int = 0) -> dict:
    key_of = jax.random.split(jax.random.key(seed), 17)
    series_in = noise(key_of[0], (TOKENS, D), 1.0, 6.0, ((0, 32),))
    block_kinds = draw_block_kinds(jax.random.fold_in(key_of[16], 71), 0)
    out_grad = noise(key_of[2], (TOKENS, D), 1.0, 6.0, ((0, 32),))
    fine_shrink = noise(key_of[3], (S1 * D, D), (S1 * D) ** -0.5, 0.078125, ((0, 8),))
    coarse_shrink = noise(key_of[4], (S2 * D, D), (S2 * D) ** -0.5, 0.0625, ((0, 8),))
    fine_isometric = noise(key_of[5], ((HOUR // S1) * D, D), ((HOUR // S1) * D) ** -0.5, 0.0625, ((0, 8),))
    coarse_isometric = noise(key_of[6], ((HOUR // S2) * D, D), ((HOUR // S2) * D) ** -0.5, 0.078125, ((0, 8),))
    fine_grow = noise(key_of[7], (D, S1 * D), D ** -0.5, 0.25, ((0, 8),))
    coarse_grow = noise(key_of[8], (D, S2 * D), D ** -0.5, 0.25, ((0, 8),))
    merge_weight = noise(key_of[9], (2 * D, D), (2 * D) ** -0.5, 0.1875, ((0, 8),))
    expand_weight = noise(key_of[10], (D, FF), D ** -0.5, 0.25, ((0, 8),))
    contract_weight = noise(key_of[11], (FF, D), FF ** -0.5, 0.125, ((0, 8),))
    trend_weight = noise(key_of[12], (D, D), (D // WINDOW) ** -0.5, 1.25, ((0, 8),))
    branch_gain = jnp.clip(1.0 + 0.18 * jax.random.normal(key_of[13], (D,), jnp.float32), 0.099609375, 1.8984375).astype(jnp.bfloat16)
    middle_gain = jnp.clip(1.0 + 0.18 * jax.random.normal(key_of[14], (D,), jnp.float32), 0.099609375, 1.8984375).astype(jnp.bfloat16)
    output_gain = jnp.clip(1.0 + 0.18 * jax.random.normal(key_of[15], (D,), jnp.float32), 0.099609375, 1.8984375).astype(jnp.bfloat16)
    return dict(series_in=series_in, block_kinds=block_kinds, out_grad=out_grad, fine_shrink=fine_shrink, coarse_shrink=coarse_shrink, fine_isometric=fine_isometric, coarse_isometric=coarse_isometric, fine_grow=fine_grow, coarse_grow=coarse_grow, merge_weight=merge_weight, expand_weight=expand_weight, contract_weight=contract_weight, trend_weight=trend_weight, branch_gain=branch_gain, middle_gain=middle_gain, output_gain=output_gain)


@jax.custom_vjp
def low(v):
    return lax.optimization_barrier(v.astype(jnp.bfloat16)).astype(jnp.float32)

@jax.custom_vjp
def low_back(v):
    return v

def low_keep(v):
    return (low(v), None)

def low_pass(kept, grad):
    return (grad,)

def back_keep(v):
    return (v, None)

def back_low(kept, grad):
    return (low(grad),)
low.defvjp(low_keep, low_pass)
low_back.defvjp(back_keep, back_low)

def precise_dot(left, right):
    return jnp.dot(left, right, precision=lax.Precision.HIGHEST, preferred_element_type=jnp.float32)

def layer_norm(values, gain):
    center = lax.optimization_barrier(jnp.mean(values, axis=-1, keepdims=True))
    centered = values - center
    spread = lax.optimization_barrier(jnp.mean(centered * centered, axis=-1, keepdims=True))
    return centered * lax.rsqrt(spread + 1e-05) * gain

def previous_block(blocks, follows):
    earlier = jnp.concatenate([jnp.zeros_like(blocks[:1]), blocks[:-1]], axis=0)
    return earlier * follows.astype(blocks.dtype)[:, None, None]

def moving_average(blocks, follows):
    half_window = WINDOW // 2
    block_len = blocks.shape[1]
    leading = jnp.concatenate([follows[1:], jnp.zeros_like(follows[:1])])
    before_rim = previous_block(blocks, follows)[:, block_len - half_window:] + (1.0 - follows)[:, None, None] * blocks[:, :1]
    following = jnp.concatenate([blocks[1:], jnp.zeros_like(blocks[:1])], axis=0) * leading[:, None, None]
    after_rim = following[:, :half_window] + (1.0 - leading)[:, None, None] * blocks[:, block_len - 1:]
    padded = jnp.concatenate([before_rim, blocks, after_rim], axis=1)
    running = padded[:, 0:block_len]
    for offset in range(1, WINDOW):
        running = running + padded[:, offset:offset + block_len]
    return running / WINDOW

def unfold(lowered, follows):
    positions = lowered.shape[1]
    extended = jnp.concatenate([previous_block(lowered, follows), lowered], axis=1)
    return jnp.concatenate([extended[:, 1 + offset:1 + offset + positions] for offset in range(positions)], axis=2)

def branch(season_low, season, follows, shrink, isometric, grow, gain, stride):
    block_count, block_len, feature_width = season.shape
    positions = block_len // stride
    shrunk = jnp.tanh(low_back(precise_dot(season_low.reshape(block_count, positions, stride * feature_width), shrink)))
    shrunk_low = low(shrunk)
    isolocal = jnp.tanh(low_back(precise_dot(unfold(shrunk_low, follows), isometric)))
    mixed_out = layer_norm(isolocal + shrunk, gain)
    upward = jnp.tanh(low_back(precise_dot(low(mixed_out), grow))).reshape(block_count, block_len, feature_width)
    return layer_norm(upward + season, gain)

def layer(values, kinds, fine_shrink, coarse_shrink, fine_isometric, coarse_isometric, fine_grow, coarse_grow, merge_weight, expand_weight, contract_weight, trend_weight, branch_gain, middle_gain, output_gain):
    block_count = kinds.shape[0]
    follows = (kinds == 2).astype(values.dtype)
    blocks = values.reshape(block_count, HOUR, D)
    trend = moving_average(blocks, follows)
    season = blocks - trend
    season_low = low(season)
    fine = branch(season_low, season, follows, fine_shrink, fine_isometric, fine_grow, branch_gain, S1)
    coarse = branch(season_low, season, follows, coarse_shrink, coarse_isometric, coarse_grow, branch_gain, S2)
    joined = low(jnp.concatenate([fine, coarse], axis=2))
    merged = low_back(precise_dot(joined, merge_weight))
    middle = layer_norm(merged, middle_gain)
    hidden = jax.nn.gelu(low_back(precise_dot(low(middle), expand_weight)), approximate=False)
    lifted = low_back(precise_dot(low(hidden), contract_weight))
    seasonal = layer_norm(middle + lifted, output_gain)
    projected = low_back(precise_dot(low(trend), trend_weight))
    return seasonal + projected

def reference(series_in, block_kinds, out_grad, fine_shrink, coarse_shrink, fine_isometric, coarse_isometric, fine_grow, coarse_grow, merge_weight, expand_weight, contract_weight, trend_weight, branch_gain, middle_gain, output_gain):
    params = tuple((item.astype(jnp.float32) for item in (fine_shrink, coarse_shrink, fine_isometric, coarse_isometric, fine_grow, coarse_grow, merge_weight, expand_weight, contract_weight, trend_weight, branch_gain, middle_gain, output_gain)))
    inputs = series_in.astype(jnp.float32).reshape(-1, 4 * HOUR, D)
    kind_rows = block_kinds.reshape(-1, 4)
    cotangents = out_grad.astype(jnp.float32).reshape(-1, 4, HOUR, D)

    def step(running, group_item):
        values, kind_row, cotangent = group_item
        result, pullback = jax.vjp(lambda v, *p: layer(v, kind_row, *p), values, *params)
        grads = pullback(cotangent)
        running = tuple((a + b for a, b in zip(running, grads[1:])))
        return (running, (result.reshape(4 * HOUR, D).astype(jnp.bfloat16), grads[0].astype(jnp.bfloat16)))
    zeros = tuple((jnp.zeros_like(item) for item in params))
    sums, (outputs, input_grads) = lax.scan(step, zeros, (inputs, kind_rows, cotangents))
    return (outputs.reshape(-1, D), input_grads.reshape(-1, D), sums[0], sums[1], sums[2], sums[3], sums[4], sums[5], sums[6], sums[7], sums[8], sums[9], sums[10], sums[11], sums[12])
```

```python
import jax
import jax.numpy as jnp
from jax import lax
from jax.experimental import pallas as pl
from jax.experimental.pallas import tpu as pltpu
from jax.sharding import PartitionSpec as P

S1 = 12
S2 = 16
WINDOW = 25
HALF = WINDOW // 2
GROUP = 4
BF = jnp.bfloat16
F32 = jnp.float32


def layer_norm(values, gain):
    center = jnp.mean(values, axis=-1, keepdims=True)
    centered = values - center
    spread = jnp.mean(centered * centered, axis=-1, keepdims=True)
    return centered * lax.rsqrt(spread + 1e-05) * gain


def exact_gelu(values):
    return jax.nn.gelu(values, approximate=False)


def previous_block(blocks, follows):
    earlier = jnp.concatenate([jnp.zeros_like(blocks[:1]), blocks[:-1]], axis=0)
    return earlier * follows.astype(blocks.dtype)[:, None, None]


def average_matrix(kinds, block_len):
    follows = (kinds == 2).reshape(-1, GROUP)
    groups = follows.shape[0]
    length = GROUP * block_len
    first = jnp.zeros((groups, GROUP), jnp.int32)
    last = jnp.zeros((groups, GROUP), jnp.int32)
    start = jnp.zeros((groups,), jnp.int32)
    firsts = []
    for b in range(GROUP):
        start = jnp.where(follows[:, b], start, b * block_len) if b else jnp.zeros_like(start)
        firsts.append(start)
    stop = jnp.full((groups,), length - 1, jnp.int32)
    lasts = []
    for b in reversed(range(GROUP)):
        if b < GROUP - 1:
            stop = jnp.where(follows[:, b + 1], stop, (b + 1) * block_len - 1)
        lasts.append(stop)
    first = jnp.repeat(jnp.stack(firsts, 1), block_len, axis=1)
    last = jnp.repeat(jnp.stack(lasts[::-1], 1), block_len, axis=1)
    i = lax.broadcasted_iota(jnp.int32, (groups, length, length), 1)
    j = lax.broadcasted_iota(jnp.int32, (groups, length, length), 2)
    first = first[:, :, None]
    last = last[:, :, None]
    inside = (jnp.abs(i - j) <= HALF) & (j >= first) & (j <= last)
    count = inside.astype(jnp.int32)
    count = count + jnp.where(j == first, jnp.maximum(first - i + HALF, 0), 0)
    count = count + jnp.where(j == last, jnp.maximum(i + HALF - last, 0), 0)
    return count.astype(BF)


def unfold(lowered, follows):
    positions = lowered.shape[1]
    extended = jnp.concatenate([previous_block(lowered, follows), lowered], axis=1)
    return jnp.concatenate(
        [extended[:, 1 + offset : 1 + offset + positions] for offset in range(positions)], axis=2
    )


def plain_dot(left, right):
    return jnp.dot(left, right, preferred_element_type=F32)


def weight_dot(inputs, grads):
    return lax.dot_general(inputs, grads, (((0,), (0,)), ((), ())), preferred_element_type=F32)


def back_dot(grads, weight):
    return lax.dot_general(grads, weight, (((1,), (1,)), ((), ())), preferred_element_type=F32)


def branch_forward(season_low, season, follows, shrink, isometric, grow, gain, stride):
    block_count, block_len, feature_width = season.shape
    positions = block_len // stride
    shrink_rows = season_low.reshape(block_count * positions, stride * feature_width)
    shrunk = jnp.tanh(plain_dot(shrink_rows, shrink))
    shrunk_low = shrunk.astype(BF).reshape(block_count, positions, feature_width)
    stacked = unfold(shrunk_low, follows).reshape(
        block_count * positions, positions * feature_width
    )
    isolocal = jnp.tanh(plain_dot(stacked, isometric))
    mixed_out, mixed_pull = jax.vjp(layer_norm, isolocal + shrunk, gain)
    mixed_low = mixed_out.astype(BF)
    upward = jnp.tanh(plain_dot(mixed_low, grow)).reshape(block_count, block_len, feature_width)
    result, result_pull = jax.vjp(layer_norm, upward + season, gain)
    saved = (
        shrink_rows,
        shrunk,
        shrunk_low,
        stacked,
        isolocal,
        mixed_pull,
        mixed_low,
        upward,
        result_pull,
    )
    return (result, saved)


def branch_backward(saved, result_grad, follows, shrink, isometric, grow, stride):
    (
        shrink_rows,
        shrunk,
        shrunk_low,
        stacked,
        isolocal,
        mixed_pull,
        mixed_low,
        upward,
        result_pull,
    ) = saved
    block_count, block_len, feature_width = result_grad.shape
    positions = block_len // stride
    summed, gain_first = result_pull(result_grad)
    grow_pre = (
        (summed * (1.0 - upward * upward))
        .reshape(block_count * positions, stride * feature_width)
        .astype(BF)
    )
    grow_grad = weight_dot(mixed_low, grow_pre).astype(BF)
    mixed_back = back_dot(grow_pre, grow)
    joint_grad, gain_second = mixed_pull(mixed_back)
    iso_pre = (joint_grad * (1.0 - isolocal * isolocal)).astype(BF)
    isometric_grad = weight_dot(stacked, iso_pre).astype(BF)
    stack_back = back_dot(iso_pre, isometric).reshape(
        block_count, positions, positions * feature_width
    )
    ignored, unfold_pull = jax.vjp(
        lambda values: unfold(values, follows), shrunk_low.astype(F32)
    )
    (shrunk_back,) = unfold_pull(stack_back)
    shrunk_total = shrunk_back.reshape(block_count * positions, feature_width) + joint_grad
    shrink_pre = (shrunk_total * (1.0 - shrunk * shrunk)).astype(BF)
    shrink_grad = weight_dot(shrink_rows, shrink_pre).astype(BF)
    season_back = (
        back_dot(shrink_pre, shrink).reshape(block_count, block_len, feature_width) + summed
    )
    return (season_back, shrink_grad, isometric_grad, grow_grad, gain_first + gain_second)


CORE_SWAP = ((0, 1), (1, 0), (2, 3), (3, 2))
Y_SWAP = ((0, 2), (2, 0), (1, 3), (3, 1))


def swap_core(v):
    return lax.ppermute(v, "group", CORE_SWAP)


def swap_y(v):
    return lax.ppermute(v, "group", Y_SWAP)


class Ring:
    def __init__(self, n):
        self.n = n
        order = list(range(0, n, 2)) + list(range(n - 1, 0, -2))
        self.right = [(order[k], order[(k + 1) % n]) for k in range(n)]
        self.left = [(b, a) for a, b in self.right]
        d = lax.axis_index("dp")
        self.me = d
        self.pos = jnp.where(d % 2 == 0, d // 2, n - 1 - d // 2)

    def index(self, offset):
        r = (self.pos + offset) % self.n
        return jnp.where(r < self.n // 2, 2 * r, 2 * (self.n - 1 - r) + 1)

    def steps(self, long_right):
        longer, shorter = self.n // 2, self.n - 1 - self.n // 2
        return (longer, shorter) if long_right else (shorter, longer)

    def go_right(self, v):
        return lax.ppermute(v, "dp", self.right)

    def go_left(self, v):
        return lax.ppermute(v, "dp", self.left)


def gather_pieces(ring, own, split_y, long_right):
    to_right, to_left = ring.steps(long_right)
    found = []

    def spread(piece):
        if split_y:
            other = swap_y(piece)
            return [piece, other, swap_core(piece), swap_core(other)]
        return [piece, swap_core(piece)]

    right = left = own
    for k in range(1, max(to_right, to_left) + 1):
        if k <= to_right:
            right = ring.go_right(right)
            found.append((-k, spread(right)))
        if k <= to_left:
            left = ring.go_left(left)
            found.append((k, spread(left)))
    return found


def place(name, shards, found, parts, ring, core, y, split_y):
    n = ring.n
    offsets = [offset for offset, _ in found]
    where = jnp.stack([ring.me, core, y] + [ring.index(offset) for offset in offsets])
    buffers = [b for _, bufs in found for b in bufs]
    count = len(buffers) // len(offsets)
    whole = [
        jax.ShapeDtypeStruct((shard.shape[0] * n, shard.shape[1]), shard.dtype) for shard in shards
    ]

    def body(where_ref, *refs):
        own = refs[: len(shards)]
        pieces = refs[len(shards) : len(shards) + len(buffers)]
        outs = refs[len(shards) + len(buffers) : -1]
        sems = refs[-1]
        me, c, h = where_ref[0], where_ref[1], where_ref[2]
        for t, shard in enumerate(shards):
            rows = shard.shape[0]
            start = pl.multiple_of(me * rows, rows)
            pltpu.make_async_copy(own[t], outs[t].at[pl.ds(start, rows)], sems.at[t]).start()
        for o in range(len(offsets)):
            source = where_ref[3 + o]
            for b in range(count):
                if split_y:
                    cc, hh = (c if b < 2 else 1 - c), (h if b % 2 == 0 else 1 - h)
                else:
                    cc, hh = (c if b == 0 else 1 - c), None
                piece = pieces[o * count + b]
                for t, cuts in enumerate(parts):
                    rows = shards[t].shape[0]
                    for r0, nr, c0, nc, fn, align_r, align_c in cuts:
                        row, col = fn(cc, hh)
                        row = pl.multiple_of(source * rows + row, align_r)
                        if not isinstance(col, int):
                            col = pl.multiple_of(col, align_c)
                        pltpu.make_async_copy(
                            piece.at[pl.ds(r0, nr), pl.ds(c0, nc)],
                            outs[t].at[pl.ds(row, nr), pl.ds(col, nc)],
                            sems.at[t],
                        ).start()
        for t in range(len(shards)):
            pltpu.make_async_copy(outs[t], outs[t], sems.at[t]).wait()

    total = sum(w.shape[0] * w.shape[1] * 4 for w in whole)
    return pl.pallas_call(
        body,
        out_shape=whole,
        grid_spec=pltpu.PrefetchScalarGridSpec(
            num_scalar_prefetch=1,
            grid=(),
            in_specs=[pl.BlockSpec(memory_space=pl.ANY)] * (len(shards) + len(buffers)),
            out_specs=[pl.BlockSpec(memory_space=pltpu.VMEM)] * len(whole),
            scratch_shapes=[pltpu.SemaphoreType.DMA((len(shards),))],
        ),
        cost_estimate=pl.CostEstimate(flops=0, bytes_accessed=total, transcendentals=0),
        compiler_params=pltpu.CompilerParams(vmem_limit_bytes=40 * 1024 * 1024),
        name=name,
    )(where, *shards, *buffers)


def cut(v, index, size, axis):
    return lax.dynamic_slice_in_dim(v, index, size, axis=axis)


def gather_row_pair(name, ring, first, second, core, y, split_y, long_right):
    share = 4 if split_y else 2
    ra, rb = first.shape[0] // share, second.shape[0] // share
    slot = core * 2 + y if split_y else core
    own = jnp.concatenate([cut(first, slot * ra, ra, 0), cut(second, slot * rb, rb, 0)], axis=0)
    width = first.shape[1]
    found = gather_pieces(ring, own, split_y, long_right)

    def at(rows):
        if split_y:
            return lambda c, h: ((c * 2 + h) * rows, 0)
        return lambda c, h: (c * rows, 0)

    parts = [[(0, ra, 0, width, at(ra), ra, 1)], [(ra, rb, 0, width, at(rb), rb, 1)]]
    return place(name, [first, second], found, parts, ring, core, y, split_y)


def gather_column_pair(name, ring, first, second, core, y, split_y, long_right):
    share = 4 if split_y else 2
    ca, cb = first.shape[1] // share, second.shape[1] // share
    slot = core * 2 + y if split_y else core
    own = jnp.concatenate([cut(first, slot * ca, ca, 1), cut(second, slot * cb, cb, 1)], axis=1)
    rows = first.shape[0]
    found = gather_pieces(ring, own, split_y, long_right)

    def at(cols):
        if split_y:
            return lambda c, h: (0, (c * 2 + h) * cols)
        return lambda c, h: (0, c * cols)

    parts = [[(0, rows, 0, ca, at(ca), rows, ca)], [(0, rows, ca, cb, at(cb), rows, cb)]]
    return place(name, [first, second], found, parts, ring, core, y, split_y)


def gather_rest(name, ring, merge, contract, trend, expand, core, y, long_right):
    half = merge.shape[1] // 2
    wide = expand.shape[1] // 2
    chunks = wide // half
    stack = [cut(v, core * half, half, 1) for v in (merge, contract, trend)]
    stack += [cut(expand, core * wide + j * half, half, 1) for j in range(chunks)]
    own = jnp.concatenate(stack, axis=0)
    found = gather_pieces(ring, own, False, long_right)
    parts, start = [], 0
    for v in (merge, contract, trend):
        rows = v.shape[0]
        parts.append([(start, rows, 0, half, lambda c, h: (0, c * half), rows, half)])
        start += rows
    rows = expand.shape[0]
    cuts = []
    for j in range(chunks):
        cuts.append(
            (start, rows, 0, half, lambda c, h, j=j: (0, c * wide + j * half), rows, half)
        )
        start += rows
    parts.append(cuts)
    return place(name, [merge, contract, trend, expand], found, parts, ring, core, y, False)


def reduce_tensor(ring, grad, by_rows, core, y, split_y, long_right):
    n = ring.n
    rows, cols = grad.shape[0] // n, grad.shape[1]
    if by_rows:
        full = grad.reshape(n, 2, rows // 2, cols)
        take = lambda v, c: lax.dynamic_index_in_dim(v, c, axis=1, keepdims=False)
        give = take(full, 1 - core)
        keep = take(full, core)
        got = swap_core(give)
        if split_y:
            quarter = rows // 4
            piece = lambda v, h: cut(v, h * quarter, quarter, 1)
        axis = 0
    else:
        half = cols // 2
        full = grad.reshape(n, rows, cols)
        take = lambda v, c: cut(v, c * half, half, 2)
        give = take(full, 1 - core)
        keep = take(full, core)
        got = swap_core(give)
        if split_y:
            quarter = half // 2
            piece = lambda v, h: cut(v, h * quarter, quarter, 2)
        axis = 1
    terms = [keep, got]
    if split_y:
        give_y = (piece(keep, 1 - y).astype(F32) + piece(got, 1 - y).astype(F32)).astype(BF)
        got_y = swap_y(give_y)
        terms = [piece(keep, y), piece(got, y), got_y]

    def local(offset):
        at = ring.me if offset == 0 else ring.index(offset)
        total = None
        for t in terms:
            v = lax.dynamic_index_in_dim(t, at, axis=0, keepdims=False).astype(F32)
            total = v if total is None else total + v
        return total

    to_right, to_left = ring.steps(long_right)
    longest = max(to_right, to_left)
    right = left = None
    for k in range(longest, 0, -1):
        if k <= to_right:
            part = local(k)
            if right is not None:
                part = part + right.astype(F32)
            right = ring.go_right(part.astype(BF))
        if k <= to_left:
            part = local(-k)
            if left is not None:
                part = part + left.astype(F32)
            left = ring.go_left(part.astype(BF))
    mine = (local(0) + right.astype(F32) + left.astype(F32)).astype(BF)
    other = swap_y(mine)
    if split_y:
        half_sum = jnp.where(
            y == 0,
            jnp.concatenate([mine, other], axis=axis),
            jnp.concatenate([other, mine], axis=axis),
        )
    else:
        half_sum = (mine.astype(F32) + other.astype(F32)).astype(BF)
    sibling = swap_core(half_sum)
    return jnp.where(
        core == 0,
        jnp.concatenate([half_sum, sibling], axis=axis),
        jnp.concatenate([sibling, half_sum], axis=axis),
    ).astype(F32)


def add_over(v, axis, size):
    step = 1
    while step < size:
        v = v + lax.ppermute(v, axis, [(i, i ^ step) for i in range(size)])
        step *= 2
    return v


def on_device(
    n,
    series_in,
    block_kinds,
    out_grad,
    fine_shrink,
    coarse_shrink,
    fine_isometric,
    coarse_isometric,
    fine_grow,
    coarse_grow,
    merge_weight,
    expand_weight,
    contract_weight,
    trend_weight,
    branch_gain,
    middle_gain,
    output_gain,
):
    ring = Ring(n)
    member = lax.axis_index("group")
    core, y = member % 2, member // 2
    me = ring.me
    block_count = block_kinds.shape[0]
    feature_width = series_in.shape[1]
    block_len = series_in.shape[0] // block_count
    share = branch_gain.shape[0]

    gains = jnp.stack([branch_gain, middle_gain, output_gain]).astype(F32)
    gains = lax.dynamic_update_slice(
        jnp.zeros((3, feature_width), F32), gains, (jnp.int32(0), me * share)
    )
    gains = add_over(gains, "dp", n)
    gain_branch, gain_middle, gain_output = gains[0], gains[1], gains[2]

    f_shrink, c_shrink = gather_row_pair(
        "place_shrink", ring, fine_shrink, coarse_shrink, core, y, True, False
    )
    f_grow, c_grow = gather_column_pair(
        "place_grow", ring, fine_grow, coarse_grow, core, y, True, False
    )
    f_iso, c_iso = gather_row_pair(
        "place_iso", ring, fine_isometric, coarse_isometric, core, y, False, True
    )
    merge_full, contract_full, trend_full, expand_full = gather_rest(
        "place_rest",
        ring,
        merge_weight,
        contract_weight,
        trend_weight,
        expand_weight,
        core,
        y,
        False,
    )

    follows = (block_kinds == 2).astype(F32)
    blocks = series_in.astype(F32).reshape(block_count, block_len, feature_width)
    counts = average_matrix(block_kinds, block_len)
    grouped = series_in.reshape(-1, GROUP * block_len, feature_width)
    trend = jnp.einsum("gij,gjd->gid", counts, grouped, preferred_element_type=F32)
    trend = (trend * (1.0 / WINDOW)).reshape(block_count, block_len, feature_width)
    season = blocks - trend
    season_low = season.astype(BF)
    fine_out, fine_saved = branch_forward(
        season_low, season, follows, f_shrink, f_iso, f_grow, gain_branch, S1
    )
    coarse_out, coarse_saved = branch_forward(
        season_low, season, follows, c_shrink, c_iso, c_grow, gain_branch, S2
    )
    joined = (
        jnp.concatenate([fine_out, coarse_out], axis=2).astype(BF).reshape(-1, 2 * feature_width)
    )
    merged = plain_dot(joined, merge_full)
    middle, middle_pull = jax.vjp(layer_norm, merged, gain_middle)
    middle_low = middle.astype(BF)
    hidden, gelu_pull = jax.vjp(exact_gelu, plain_dot(middle_low, expand_full))
    hidden_low = hidden.astype(BF)
    lifted = plain_dot(hidden_low, contract_full)
    seasonal, output_pull = jax.vjp(layer_norm, middle + lifted, gain_output)
    trend_low = trend.reshape(-1, feature_width).astype(BF)
    projected = plain_dot(trend_low, trend_full)
    series_out = (seasonal + projected).astype(BF)
    trend_grad = weight_dot(trend_low, out_grad).astype(BF)
    trend_back = back_dot(out_grad, trend_full)
    summed_grad, output_gain_raw = output_pull(out_grad.astype(F32))
    lifted_low = summed_grad.astype(BF)
    contract_grad = weight_dot(hidden_low, lifted_low).astype(BF)
    (hidden_pre_grad,) = gelu_pull(back_dot(lifted_low, contract_full))
    hidden_grad_low = hidden_pre_grad.astype(BF)
    expand_grad = weight_dot(middle_low, hidden_grad_low).astype(BF)
    middle_back = summed_grad + back_dot(hidden_grad_low, expand_full)
    merged_grad, middle_gain_raw = middle_pull(middle_back)
    merged_low = merged_grad.astype(BF)
    merge_grad = weight_dot(joined, merged_low).astype(BF)
    joined_back = back_dot(merged_low, merge_full).reshape(
        block_count, block_len, 2 * feature_width
    )
    fine_season, fine_shrink_g, fine_iso_g, fine_grow_g, fine_gain_g = branch_backward(
        fine_saved, joined_back[:, :, :feature_width], follows, f_shrink, f_iso, f_grow, S1
    )
    coarse_season, coarse_shrink_g, coarse_iso_g, coarse_grow_g, coarse_gain_g = branch_backward(
        coarse_saved, joined_back[:, :, feature_width:], follows, c_shrink, c_iso, c_grow, S2
    )
    season_grad = fine_season + coarse_season
    trend_total = trend_back.reshape(block_count, block_len, feature_width) - season_grad
    spread = (trend_total * (1.0 / WINDOW)).astype(BF)
    averaged = jnp.einsum(
        "gij,gid->gjd",
        counts,
        spread.reshape(grouped.shape),
        preferred_element_type=F32,
    )
    series_grad = (season_grad + averaged.reshape(season_grad.shape)).reshape(
        -1, feature_width
    ).astype(BF)

    def reduced(grad, by_rows, split_y, long_right):
        return reduce_tensor(ring, grad, by_rows, core, y, split_y, long_right)

    contract_share = reduced(contract_grad, True, False, True)
    expand_share = reduced(expand_grad, False, False, False)
    merge_share = reduced(merge_grad, True, False, False)
    trend_share = reduced(trend_grad, True, False, False)
    fine_grow_share = reduced(fine_grow_g, False, True, True)
    coarse_grow_share = reduced(coarse_grow_g, False, True, False)
    fine_iso_share = reduced(fine_iso_g, True, True, True)
    coarse_iso_share = reduced(coarse_iso_g, True, True, False)
    fine_shrink_share = reduced(fine_shrink_g, True, False, True)
    coarse_shrink_share = reduced(coarse_shrink_g, True, False, False)

    gain_grads = jnp.stack([fine_gain_g + coarse_gain_g, middle_gain_raw, output_gain_raw])
    gain_grads = add_over(add_over(gain_grads, "dp", n), "group", 4)
    gain_grads = lax.dynamic_slice(gain_grads, (jnp.int32(0), me * share), (3, share))
    return (
        series_out,
        series_grad,
        fine_shrink_share,
        coarse_shrink_share,
        fine_iso_share,
        coarse_iso_share,
        fine_grow_share,
        coarse_grow_share,
        merge_share,
        expand_share,
        contract_share,
        trend_share,
        gain_grads[0],
        gain_grads[1],
        gain_grads[2],
    )


def solution(mesh):
    n = mesh.shape["dp"]
    rows = P(("dp", "group"), None)
    weight = P("dp", None)
    return jax.shard_map(
        lambda *args: on_device(n, *args),
        mesh=mesh,
        in_specs=(rows, P(("dp", "group")), rows) + (weight,) * 10 + (P("dp"),) * 3,
        out_specs=(rows, rows) + (weight,) * 10 + (P("dp"),) * 3,
        check_vma=False,
    )
```

```python
import functools
import math

import jax
import jax.numpy as jnp
from jax import lax
from jax.experimental import pallas as pl
from jax.experimental.pallas import tpu as pltpu
from jax.sharding import PartitionSpec as P

STRIDES = (12, 16)
WINDOW = 25
HALF = WINDOW // 2
GROUP = 4
BF = jnp.bfloat16
F32 = jnp.float32
MIB = 1024 * 1024
CORE_SWAP = ((0, 1), (1, 0), (2, 3), (3, 2))
Y_SWAP = ((0, 2), (2, 0), (1, 3), (3, 1))


class Layout:
    def __init__(self, n, width, block_len, ff):
        self.n, self.width, self.block_len = n, width, block_len
        self.length = GROUP * block_len
        self.taps = tuple(block_len // s for s in STRIDES)
        self.shrink = tuple(s * width for s in STRIDES)
        self.iso = tuple(p * width for p in self.taps)
        self.si_half = (self.shrink[0] + self.iso[0]) // (2 * n)
        self.k = width // n
        self.g_half = max(STRIDES) // 2 * self.k
        self.chunks = ff // width
        self.merge, self.contract = 2 * width // n, ff // n
        self.f_half = max(self.contract + self.merge, self.k * (1 + self.chunks))
        self.npos = tuple(GROUP * p for p in self.taps)

    def si_parts(self, b):
        s, i = self.shrink[b] // self.n, self.iso[b] // self.n
        return [(0, s // 2, 0, s), (s // 2, i // 2, self.shrink[b], i)]

    def g_parts(self, b):
        return [(j * self.k, self.k, j) for j in range(STRIDES[b] // 2)]

    def f_parts(self, h):
        base = self.g_half
        if h == 0:
            return [
                (base, self.contract, "contract", 0),
                (base + self.contract, self.merge, "merge", 0),
            ]
        found = [(base, self.k, "trend", 0)]
        for j in range(self.chunks):
            found.append((base + (1 + j) * self.k, self.k, "expand", j))
        return found


def held(*values):
    return lax.optimization_barrier(values)


class Ring:
    def __init__(self, n):
        self.n = n
        order = list(range(0, n, 2)) + list(range(n - 1, 0, -2))
        self.right = [(order[k], order[(k + 1) % n]) for k in range(n)]
        self.left = [(b, a) for a, b in self.right]
        d = lax.axis_index("dp")
        self.me = d
        self.pos = jnp.where(d % 2 == 0, d // 2, n - 1 - d // 2)

    def index(self, offset):
        if offset == 0:
            return self.me
        r = (self.pos + offset) % self.n
        return jnp.where(r < self.n // 2, 2 * r, 2 * (self.n - 1 - r) + 1)


def slot(sends, work=None, given=()):
    names = list(sends)
    tied = held(*[sends[k][0] for k in names], *given)
    moved = [sends[k][1](v) for k, v in zip(names, tied)]
    done = tuple(work(*tied[len(names) :])) if work is not None else ()
    out = held(*moved, *done)
    return dict(zip(names, out[: len(names)])), out[len(names) :]


def swap_core(v):
    return lax.ppermute(v, "group", CORE_SWAP)


def swap_y(v):
    return lax.ppermute(v, "group", Y_SWAP)


def dot(a, b):
    return jnp.dot(a, b, preferred_element_type=F32)


def dot_t(a, b):
    return lax.dot_general(a, b, (((1,), (1,)), ((), ())), preferred_element_type=F32)


def dot_w(a, b):
    return lax.dot_general(a, b, (((0,), (0,)), ((), ())), preferred_element_type=F32)


def normal(v):
    center = jnp.mean(v, axis=-1, keepdims=True)
    centered = v - center
    inverse = lax.rsqrt(jnp.mean(centered * centered, axis=-1, keepdims=True) + 1e-05)
    return centered * inverse, inverse


def normal_back(grad, hat, inverse, gain):
    g = grad * gain
    a = jnp.mean(g, axis=-1, keepdims=True)
    b = jnp.mean(g * hat, axis=-1, keepdims=True)
    return inverse * (g - a - hat * b)


def erf_pair(h):
    x = jnp.abs(h) * (1.0 / math.sqrt(2.0))
    d = 1.0 + 0.3275911 * x
    t = pl.reciprocal(d, approx=True)
    t = t * (2.0 - d * t)
    e = jnp.exp(-0.5 * h * h)
    p = t * (
        0.254829592
        + t * (-0.284496736 + t * (1.421413741 + t * (-1.453152027 + t * 1.061405429)))
    )
    q = 0.5 * p * e
    return jnp.where(h >= 0, 1.0 - q, q), h * e * (1.0 / math.sqrt(2.0 * math.pi))


def over(parts, first, rows):
    for part in parts:
        lo, hi = max(first, part[0]), min(first + rows, part[0] + part[1])
        if lo < hi:
            yield lo - first, hi - lo, lo - part[0], part


def start_copy(piece, row, rows, whole, at, sem):
    at = at if isinstance(at, int) else pl.multiple_of(at, 16)
    pltpu.make_async_copy(
        piece.at[pl.ds(row, rows)], whole.at[pl.ds(at, rows)], sem
    ).start()


def wait_rows(whole, first, rows, sem):
    view = whole.at[pl.ds(first, rows)]
    pltpu.make_async_copy(view, view, sem).wait()


class Pieces:
    def __init__(self):
        self.meta, self.arrays = [], []

    def add(self, source, other, first, array):
        self.meta.append((source, other, first, array.shape[0]))
        self.arrays.append(array)


def load_si(lay, b, where, meta, refs, whole, sems):
    core = where[1]
    for (source, other, first, rows), ref in zip(meta, refs):
        src = where[2 + source]
        h = 1 - core if other else core
        for row, count, inside, part in over(lay.si_parts(b), first, rows):
            _, half, base, shard = part
            at = base + src * shard + h * half + inside
            start_copy(ref, row, count, whole, at, sems.at[0 if base == 0 else 1])


def load_g(lay, b, where, meta, refs, whole, sem):
    core = where[1]
    for (source, other, first, rows), ref in zip(meta, refs):
        src = where[2 + source]
        h = 1 - core if other else core
        for row, count, inside, part in over(lay.g_parts(b), first, rows):
            at = (h * (STRIDES[b] // 2) + part[2]) * lay.width + src * lay.k + inside
            start_copy(ref, row, count, whole, at, sem)


def load_f(lay, c, where, meta, refs, wholes, sems):
    names = ("merge", "contract", "trend", "expand")
    for (source, other, first, rows), ref in zip(meta, refs):
        src = where[2 + source]
        h = 1 - c if other else c
        for row, count, inside, part in over(lay.f_parts(h), first, rows):
            t = names.index(part[2])
            at = part[3] * lay.width + src * part[1] + inside
            start_copy(ref, row, count, wholes[t], at, sems.at[t])


def any_spec():
    return pl.BlockSpec(memory_space=pl.ANY)


def vmem_spec():
    return pl.BlockSpec(memory_space=pltpu.VMEM)


def smem_spec():
    return pl.BlockSpec(memory_space=pltpu.SMEM)


def cost(flops, moved):
    return pl.CostEstimate(flops=int(flops), bytes_accessed=int(moved), transcendentals=0)


def by_branch(where, body):
    for b in range(2):
        pl.when(where[0] == b)(functools.partial(body, b))


def tap_rows(x, age, k):
    if k == 0:
        return x
    return jnp.where(age >= k, pltpu.roll(x, k, 0), 0.0)


def shrink_forward(lay, where, si, season_low, age, gain):
    n, width = lay.n, lay.width
    groups = season_low.shape[0]
    most = groups * max(lay.npos)
    count = len(si.arrays)

    def kernel(where, age_ref, gain_ref, season_ref, *refs):
        pieces, (shrunk_ref, iso_ref, mixed_ref, whole, sems) = refs[:count], refs[count:]

        def body(b):
            load_si(lay, b, where, si.meta, pieces, whole, sems)
            npos = lay.npos[b]
            m = groups * npos
            wait_rows(whole, 0, lay.shrink[b], sems.at[0])
            z = jnp.zeros((m, width), F32)
            for s in range(STRIDES[b]):
                x = season_ref[:, s * npos : (s + 1) * npos, :].reshape(m, width)
                z += dot(x, whole[s * width : (s + 1) * width])
            shrunk = jnp.tanh(z)
            shrunk_ref[:m] = shrunk
            low = shrunk.astype(BF).astype(F32)
            wait_rows(whole, lay.shrink[b], lay.iso[b], sems.at[1])
            taps = lay.taps[b]
            base = lay.shrink[b]
            age = age_ref[:m]
            e = jnp.zeros((m, width), F32)
            for k in range(taps):
                at = base + (taps - 1 - k) * width
                e += dot(tap_rows(low, age, k).astype(BF), whole[at : at + width])
            iso = jnp.tanh(e)
            iso_ref[:m] = iso
            hat, _ = normal(iso + shrunk)
            mixed_ref[:m] = (hat * gain_ref[...]).astype(BF)

        by_branch(where, body)

    total = lay.shrink[0] + lay.iso[0]
    return pl.pallas_call(
        kernel,
        out_shape=[
            jax.ShapeDtypeStruct((most, width), F32),
            jax.ShapeDtypeStruct((most, width), F32),
            jax.ShapeDtypeStruct((most, width), BF),
        ],
        in_specs=[smem_spec(), vmem_spec(), vmem_spec(), vmem_spec()] + [any_spec()] * count,
        out_specs=[vmem_spec()] * 3,
        scratch_shapes=[pltpu.VMEM((total, width), BF), pltpu.SemaphoreType.DMA((2,))],
        compiler_params=pltpu.CompilerParams(vmem_limit_bytes=44 * MIB),
        cost_estimate=cost(2 * most * width * total, 2 * total * width),
        name="shrink_forward",
    )(where, age, gain, season_low, *si.arrays)


def grow_forward(lay, where, gf, part, mixed, season, order, gain):
    width = lay.width
    groups = season.shape[0] // 2
    length = lay.length
    count = len(gf.arrays)

    def kernel(where, gain_ref, order_ref, mixed_ref, season_ref, *refs):
        pieces, (out_ref, up_ref, whole, rows_ref, sem) = refs[:count], refs[count:]

        def body(b):
            load_g(lay, b, where, gf.meta, pieces, whole, sem)
            npos = lay.npos[b]
            m = groups * npos
            x = mixed_ref[part * m : (part + 1) * m]
            wait_rows(whole, 0, STRIDES[b] * width, sem)
            for s in range(STRIDES[b]):
                cut = slice(s * npos, (s + 1) * npos)
                up = jnp.tanh(dot(x, whole[s * width : (s + 1) * width]))
                up_ref[:, cut, :] = up.reshape(groups, npos, width)
                hat, _ = normal(up + season_ref[:, cut, :].reshape(m, width))
                rows_ref[:, cut, :] = (hat * gain_ref[...]).astype(BF).reshape(groups, npos, width)

        by_branch(where, body)
        for g in range(groups):
            out_ref[g] = dot_w(order_ref[...], rows_ref[g]).astype(BF)

    most = max(STRIDES) * width
    return pl.pallas_call(
        kernel,
        grid=(1,),
        out_shape=[
            jax.ShapeDtypeStruct((groups, length, width), BF),
            jax.ShapeDtypeStruct((groups, length, width), F32),
        ],
        in_specs=[
            smem_spec(),
            vmem_spec(),
            vmem_spec(),
            vmem_spec(),
            pl.BlockSpec((groups, length, width), lambda g: (part, 0, 0)),
        ]
        + [any_spec()] * count,
        out_specs=[vmem_spec()] * 2,
        scratch_shapes=[
            pltpu.VMEM((most, width), BF),
            pltpu.VMEM((groups, length, width), BF),
            pltpu.SemaphoreType.DMA,
        ],
        compiler_params=pltpu.CompilerParams(vmem_limit_bytes=52 * MIB),
        cost_estimate=cost(
            2 * groups * length * width * (width + length), 2 * most * width + 14 * groups * length * width
        ),
        name="grow_forward",
    )(where, gain, order, mixed, season, *gf.arrays)


def grow_backward(lay, where, gf, part, grad, up, season, order, gain):
    width = lay.width
    groups = season.shape[0] // 2
    length = lay.length
    count = len(gf.arrays)
    most = groups * max(lay.npos)

    def kernel(where, gain_ref, order_ref, grad_ref, up_ref, season_ref, *refs):
        pieces, rest = refs[:count], refs[count:]
        (pre_ref, back_ref, sum_ref, gain_grad_ref, whole, rows_ref, sem) = rest

        def order_rows():
            for g in range(groups):
                rows_ref[g] = dot(order_ref[...], grad_ref[g]).astype(BF)

        def body(b):
            load_g(lay, b, where, gf.meta, pieces, whole, sem)
            order_rows()
            npos = lay.npos[b]
            m = groups * npos
            wait_rows(whole, 0, STRIDES[b] * width, sem)
            total = jnp.zeros((m, width), F32)
            gains = jnp.zeros((1, width), F32)
            for s in range(STRIDES[b]):
                cut = slice(s * npos, (s + 1) * npos)
                up = up_ref[:, cut, :].reshape(m, width)
                hat, inverse = normal(up + season_ref[:, cut, :].reshape(m, width))
                g = rows_ref[:, cut, :].reshape(m, width).astype(F32)
                gains += jnp.sum(g * hat, axis=0, keepdims=True)
                d = normal_back(g, hat, inverse, gain_ref[...])
                sum_ref[:, cut, :] = d.reshape(groups, npos, width)
                pre = (d * (1.0 - up * up)).astype(BF)
                pre_ref[:, cut, :] = pre.reshape(groups, npos, width)
                total += dot_t(pre, whole[s * width : (s + 1) * width])
            back_ref[:m] = total
            gain_grad_ref[...] = gains

        by_branch(where, body)

    whole_rows = max(STRIDES) * width
    return pl.pallas_call(
        kernel,
        grid=(1,),
        out_shape=[
            jax.ShapeDtypeStruct((groups, length, width), BF),
            jax.ShapeDtypeStruct((most, width), F32),
            jax.ShapeDtypeStruct((groups, length, width), F32),
            jax.ShapeDtypeStruct((1, width), F32),
        ],
        in_specs=[
            smem_spec(),
            vmem_spec(),
            vmem_spec(),
            vmem_spec(),
            vmem_spec(),
            pl.BlockSpec((groups, length, width), lambda g: (part, 0, 0)),
        ]
        + [any_spec()] * count,
        out_specs=[vmem_spec()] * 4,
        scratch_shapes=[
            pltpu.VMEM((whole_rows, width), BF),
            pltpu.VMEM((groups, length, width), BF),
            pltpu.SemaphoreType.DMA,
        ],
        compiler_params=pltpu.CompilerParams(vmem_limit_bytes=58 * MIB),
        cost_estimate=cost(
            2 * groups * length * width * (width + length),
            2 * whole_rows * width + 18 * groups * length * width,
        ),
        name="grow_backward",
    )(where, gain, order, grad, up, season, *gf.arrays)


def grow_weight(lay, where, places, mixed, pre_own, pre_other):
    n, width, k = lay.n, lay.width, lay.k
    groups = pre_own.shape[0]

    def kernel(where, places_ref, mixed_ref, own_ref, other_ref, out_ref):
        def body(b):
            npos = lay.npos[b]
            m = groups * npos
            x0, x1 = mixed_ref[:m], mixed_ref[m : 2 * m]
            steps = STRIDES[b] // 2
            for s in range(STRIDES[b]):
                cut = slice(s * npos, (s + 1) * npos)
                d = dot_w(x0, own_ref[:, cut, :].reshape(m, width))
                d += dot_w(x1, other_ref[:, cut, :].reshape(m, width))
                side = jnp.where(where[1] == s // steps, 0, 1)
                at = (s % steps) * k
                for shard in range(n):
                    out_ref[side, places_ref[shard], at : at + k, :] = d[
                        shard * k : (shard + 1) * k
                    ].astype(BF)
            rest = lay.g_half - steps * k
            if rest:
                out_ref[:, :, steps * k :, :] = jnp.zeros((2, n, rest, width), BF)

        by_branch(where, body)

    return pl.pallas_call(
        kernel,
        out_shape=jax.ShapeDtypeStruct((2, n, lay.g_half, width), BF),
        in_specs=[smem_spec(), smem_spec()] + [vmem_spec()] * 3,
        out_specs=vmem_spec(),
        compiler_params=pltpu.CompilerParams(vmem_limit_bytes=44 * MIB),
        cost_estimate=cost(4 * groups * lay.length * width * width, 2 * 2 * n * lay.g_half * width),
        name="grow_weight",
    )(where, places, mixed, pre_own, pre_other)


def shrink_backward(lay, where, places, si, back_own, back_other, shrunk, iso, season_low, age, gain):
    n, width = lay.n, lay.width
    most = shrunk.shape[0]
    groups = season_low.shape[0]
    count = len(si.arrays)

    def kernel(where, places_ref, age_ref, gain_ref, b0, b1, shrunk_ref, iso_ref, season_ref, *refs):
        pieces, (pre_ref, grad_ref, gain_grad_ref, whole, sems) = refs[:count], refs[count:]

        def body(b):
            load_si(lay, b, where, si.meta, pieces, whole, sems)
            npos, taps = lay.npos[b], lay.taps[b]
            m = groups * npos
            mixed_back = jnp.concatenate([b0[: m // 2], b1[: m // 2]], axis=0)
            shrunk, iso = shrunk_ref[:m], iso_ref[:m]
            hat, inverse = normal(iso + shrunk)
            gain_grad_ref[...] = jnp.sum(mixed_back * hat, axis=0, keepdims=True)
            joint = normal_back(mixed_back, hat, inverse, gain_ref[...])
            iso_pre = (joint * (1.0 - iso * iso)).astype(BF)
            low = shrunk.astype(BF).astype(F32)
            age = age_ref[:m]

            def store(part, row, d):
                first, half, _, shard = part
                lo = row
                while lo < row + width:
                    dp, h, r = lo // shard, (lo % shard) // half, lo % half
                    rows = min(half - r, row + width - lo)
                    side = jnp.where(where[1] == h, 0, 1)
                    grad_ref[side, places_ref[dp], first + r : first + r + rows, :] = d[
                        lo - row : lo - row + rows
                    ].astype(BF)
                    lo += rows

            part_s, part_i = lay.si_parts(b)
            base = lay.shrink[b]
            wait_rows(whole, 0, base, sems.at[0])
            wait_rows(whole, base, lay.iso[b], sems.at[1])
            total = joint
            for k in range(taps):
                tap = taps - 1 - k
                back = dot_t(iso_pre, whole[base + tap * width : base + (tap + 1) * width])
                if k:
                    back = pltpu.roll(jnp.where(age >= k, back, 0.0), m - k, 0)
                total += back
                store(part_i, tap * width, dot_w(tap_rows(low, age, k).astype(BF), iso_pre))
            pre = (total * (1.0 - shrunk * shrunk)).astype(BF)
            pre_ref[:m] = pre
            for s in range(STRIDES[b]):
                x = season_ref[:, s * npos : (s + 1) * npos, :].reshape(m, width)
                store(part_s, s * width, dot_w(x, pre))

        by_branch(where, body)

    total = lay.shrink[0] + lay.iso[0]
    return pl.pallas_call(
        kernel,
        out_shape=[
            jax.ShapeDtypeStruct((most, width), BF),
            jax.ShapeDtypeStruct((2, n, lay.si_half, width), BF),
            jax.ShapeDtypeStruct((1, width), F32),
        ],
        in_specs=[smem_spec(), smem_spec()] + [vmem_spec()] * 7 + [any_spec()] * count,
        out_specs=[vmem_spec()] * 3,
        scratch_shapes=[pltpu.VMEM((total, width), BF), pltpu.SemaphoreType.DMA((2,))],
        compiler_params=pltpu.CompilerParams(vmem_limit_bytes=58 * MIB),
        cost_estimate=cost(6 * most * width * total // 2, 4 * total * width),
        name="shrink_backward",
    )(where, places, age, gain, back_own, back_other, shrunk, iso, season_low, *si.arrays)


def season_backward(lay, where, si, pre, sum_own, sum_other, order):
    width, length = lay.width, lay.length
    groups = sum_own.shape[0]
    count = len(si.arrays)

    def kernel(where, order_ref, pre_ref, own_ref, other_ref, *refs):
        pieces, (own_out, other_out, whole, rows_ref, sems) = refs[:count], refs[count:]

        def body(b):
            core = where[1]
            npos = lay.npos[b]
            m = groups * npos
            parts = lay.si_parts(b)[:1]
            for (source, other, first, rows), ref in zip(si.meta, pieces):
                src = where[2 + source]
                h = 1 - core if other else core
                for row, rows_in, inside, part in over(parts, first, rows):
                    at = src * part[3] + h * part[1] + inside
                    start_copy(ref, row, rows_in, whole, at, sems)
            wait_rows(whole, 0, lay.shrink[b], sems)
            for s in range(STRIDES[b]):
                cut = slice(s * npos, (s + 1) * npos)
                d = dot_t(pre_ref[: 2 * m], whole[s * width : (s + 1) * width])
                rows_ref[:groups, cut, :] = (
                    d[:m].reshape(groups, npos, width) + own_ref[:, cut, :]
                ).astype(BF)
                rows_ref[groups:, cut, :] = (
                    d[m:].reshape(groups, npos, width) + other_ref[:, cut, :]
                ).astype(BF)

        by_branch(where, body)
        for g in range(groups):
            own_out[g] = dot_w(order_ref[...], rows_ref[g]).astype(BF)
            other_out[g] = dot_w(order_ref[...], rows_ref[groups + g]).astype(BF)

    most = max(lay.shrink)
    return pl.pallas_call(
        kernel,
        out_shape=[jax.ShapeDtypeStruct((groups, length, width), BF)] * 2,
        in_specs=[smem_spec()] + [vmem_spec()] * 4 + [any_spec()] * count,
        out_specs=[vmem_spec()] * 2,
        scratch_shapes=[
            pltpu.VMEM((most, width), BF),
            pltpu.VMEM((2 * groups, length, width), BF),
            pltpu.SemaphoreType.DMA,
        ],
        compiler_params=pltpu.CompilerParams(vmem_limit_bytes=52 * MIB),
        cost_estimate=cost(
            4 * groups * length * width * (width + length), 2 * most * width + 24 * groups * length * width
        ),
        name="season_backward",
    )(where, order, pre, sum_own, sum_other, *si.arrays)


def dense(lay, where, gf, tile, mine, received, trend_low, out_grad, gain_middle, gain_output):
    width, length, chunks = lay.width, lay.length, lay.chunks
    count = len(gf.arrays)
    part = length // 2
    ff = width * chunks

    def kernel(where, gm_ref, go_ref, mine_ref, got_ref, trend_ref, grad_ref, *refs):
        pieces, rest = refs[:count], refs[count:]
        (out_ref, jm_ref, js_ref, tb_ref, ml_ref, hid_ref, hg_ref, ll_ref, mg_ref) = rest[:9]
        (gains_ref, merge, contract, trend, expand, slope_ref, sems) = rest[9:]
        for c in range(2):
            pl.when(where[1] == c)(
                functools.partial(
                    load_f, lay, c, where, gf.meta, pieces, (merge, contract, trend, expand), sems
                )
            )
        b = where[0]
        for t, (w, rows) in enumerate(
            ((merge, 2 * width), (contract, ff), (trend, width), (expand, ff))
        ):
            wait_rows(w, 0, rows, sems.at[t])
        gm, go = gm_ref[...], go_ref[...]
        at_mine = pl.multiple_of(b * width, width)
        at_other = pl.multiple_of((1 - b) * width, width)

        def block(i, gains):
            rows = pl.ds(pl.multiple_of(i * part, part), part)
            merged = dot(mine_ref[0, rows, :], merge[pl.ds(at_mine, width)])
            merged += dot(got_ref[0, rows, :], merge[pl.ds(at_other, width)])
            mhat, minv = normal(merged)
            middle = mhat * gm
            mlow = middle.astype(BF)
            ml_ref[rows, :] = mlow
            lifted = jnp.zeros((part, width), F32)
            for j in range(chunks):
                cols = slice(j * width, (j + 1) * width)
                h = dot(mlow, expand[cols])
                phi, dens = erf_pair(h)
                hid = (h * phi).astype(BF)
                slope_ref[:, cols] = phi + dens
                hid_ref[rows, cols] = hid
                lifted += dot(hid, contract[cols])
            ohat, oinv = normal(middle + lifted)
            g_low = grad_ref[0, rows, :]
            projected = dot(trend_ref[0, rows, :], trend[...])
            out_ref[rows, :] = (ohat * go + projected).astype(BF)
            g = g_low.astype(F32)
            tb_ref[rows, :] = dot_t(g_low, trend[...])
            d = normal_back(g, ohat, oinv, go)
            llow = d.astype(BF)
            ll_ref[rows, :] = llow
            back = d
            for j in range(chunks):
                cols = slice(j * width, (j + 1) * width)
                hg = (dot_t(llow, contract[cols]) * slope_ref[:, cols]).astype(BF)
                hg_ref[rows, cols] = hg
                back += dot_t(hg, expand[cols])
            mg = normal_back(back, mhat, minv, gm).astype(BF)
            mg_ref[rows, :] = mg
            jm_ref[rows, :] = dot_t(mg, merge[pl.ds(at_mine, width)]).astype(BF)
            js_ref[rows, :] = dot_t(mg, merge[pl.ds(at_other, width)]).astype(BF)
            return (
                gains[0] + jnp.sum(back * mhat, axis=0, keepdims=True),
                gains[1] + jnp.sum(g * ohat, axis=0, keepdims=True),
            )

        zero = jnp.zeros((1, width), F32)
        a, c = lax.fori_loop(0, length // part, block, (zero, zero))
        gains_ref[0:1, :] = a
        gains_ref[1:2, :] = c

    block_spec = pl.BlockSpec((1, length, width), lambda g: (tile, 0, 0))
    whole_spec = pl.BlockSpec((1, length, width), lambda g: (0, 0, 0))
    shapes = [(width, BF)] * 3 + [(width, F32), (width, BF), (ff, BF), (ff, BF), (width, BF), (width, BF)]
    return pl.pallas_call(
        kernel,
        grid=(1,),
        out_shape=[jax.ShapeDtypeStruct((length, w), t) for w, t in shapes]
        + [jax.ShapeDtypeStruct((2, width), F32)],
        in_specs=[
            smem_spec(),
            vmem_spec(),
            vmem_spec(),
            block_spec,
            whole_spec,
            block_spec,
            block_spec,
        ]
        + [any_spec()] * count,
        out_specs=[vmem_spec()] * 10,
        scratch_shapes=[
            pltpu.VMEM((2 * width, width), BF),
            pltpu.VMEM((ff, width), BF),
            pltpu.VMEM((width, width), BF),
            pltpu.VMEM((ff, width), BF),
            pltpu.VMEM((part, ff), F32),
            pltpu.SemaphoreType.DMA((4,)),
        ],
        compiler_params=pltpu.CompilerParams(vmem_limit_bytes=56 * MIB),
        cost_estimate=cost(
            2 * length * width * (4 * width + 4 * ff + 2 * width), 12 * MIB + 20 * MIB
        ),
        name="dense_%d" % tile,
    )(where, gain_middle, gain_output, mine, received, trend_low, out_grad, *gf.arrays)


def dense_weights(lay, where, places, mine, received, trend_low, out_grad, saved):
    n, width, chunks, length = lay.n, lay.width, lay.chunks, lay.length
    groups = len(saved)

    def kernel(where, places_ref, mine_ref, trend_ref, grad_ref, *refs):
        got = refs[:groups]
        kept = [refs[groups + 5 * g : groups + 5 * (g + 1)] for g in range(groups)]
        out_ref = refs[-1]
        core = where[1]

        def store(h, first, shard, row, d):
            side = jnp.where(core == h, 0, 1)
            lo = row
            while lo < row + d.shape[0]:
                dp, r = lo // shard, lo % shard
                rows = min(shard - r, row + d.shape[0] - lo)
                out_ref[side, places_ref[dp], first + r : first + r + rows, :] = d[
                    lo - row : lo - row + rows
                ].astype(BF)
                lo += rows

        def total(pairs):
            d = None
            for x, g in pairs:
                v = dot_w(x, g)
                d = v if d is None else d + v
            return d

        base = -lay.g_half
        for h in range(2):
            used = 0
            for first, rows, name, j in lay.f_parts(h):
                first += base
                used = first + rows
                if name == "contract":
                    for q in range(chunks):
                        cols = slice(q * width, (q + 1) * width)
                        d = total([(k[1][:, cols], k[3][...]) for k in kept])
                        store(h, first, rows, q * width, d)
                elif name == "merge":
                    for q in range(2):
                        first_half = where[0] == q

                        def one(arrays, q=q, first=first, rows=rows):
                            store(h, first, rows, q * width, total(list(zip(arrays, [k[4][...] for k in kept]))))

                        pl.when(first_half)(lambda: one([mine_ref[g] for g in range(groups)]))
                        pl.when(jnp.logical_not(first_half))(lambda: one([v[0] for v in got]))
                elif name == "trend":
                    d = total([(trend_ref[g], grad_ref[g]) for g in range(groups)])
                    store(h, first, rows, 0, d)
                else:
                    cols = slice(j * width, (j + 1) * width)
                    d = total([(k[0][...], k[2][:, cols]) for k in kept])
                    store(h, first, rows, 0, d)
            rest = lay.f_half - used
            if rest:
                side = jnp.where(core == h, 0, 1)
                out_ref[side, :, used:, :] = jnp.zeros((n, rest, width), BF)

    flat = [v for s in saved for v in s]
    ff = chunks * width
    return pl.pallas_call(
        kernel,
        out_shape=jax.ShapeDtypeStruct((2, n, lay.f_half, width), BF),
        in_specs=[smem_spec(), smem_spec()] + [vmem_spec()] * (3 + groups + len(flat)),
        out_specs=vmem_spec(),
        compiler_params=pltpu.CompilerParams(vmem_limit_bytes=58 * MIB),
        cost_estimate=cost(
            2 * groups * length * width * (2 * width + 2 * ff + width), 45 * MIB
        ),
        name="dense_weights",
    )(where, places, mine, trend_low, out_grad, *received, *flat)


def series_bounds(kinds):
    follows = kinds == 2
    start = jnp.zeros_like(kinds[:, 0])
    firsts = []
    for b in range(GROUP):
        start = jnp.where(follows[:, b], start, b) if b else start
        firsts.append(start)
    stop = jnp.full_like(start, GROUP - 1)
    lasts = [stop]
    for b in reversed(range(GROUP - 1)):
        stop = jnp.where(follows[:, b + 1], stop, b)
        lasts.append(stop)
    return jnp.stack(firsts, 1), jnp.stack(lasts[::-1], 1)


def pick(table, block):
    found = jnp.zeros((table.shape[0], block.shape[0]), table.dtype)
    for b in range(GROUP):
        found = jnp.where(block[None, :] == b, table[:, b : b + 1], found)
    return found


def window_counts(kinds, block_len, step):
    firsts, lasts = series_bounds(kinds)
    length = GROUP * block_len
    block = step // block_len
    first = pick(firsts, block)[:, :, None] * block_len
    last = pick(lasts, block)[:, :, None] * block_len + (block_len - 1)
    i = step[None, :, None]
    j = jnp.arange(length, dtype=jnp.int32)[None, None, :]
    count = ((jnp.abs(i - j) <= HALF) & (j >= first) & (j <= last)).astype(jnp.int32)
    count += jnp.where(j == first, jnp.maximum(first - i + HALF, 0), 0)
    count += jnp.where(j == last, jnp.maximum(i + HALF - last, 0), 0)
    return count.astype(F32).astype(BF)


def exchange(axis, size, step):
    return lambda v: lax.ppermute(v, axis, [(i, i ^ step) for i in range(size)])


def on_device(
    n,
    series_in,
    block_kinds,
    out_grad,
    fine_shrink,
    coarse_shrink,
    fine_isometric,
    coarse_isometric,
    fine_grow,
    coarse_grow,
    merge_weight,
    expand_weight,
    contract_weight,
    trend_weight,
    branch_gain,
    middle_gain,
    output_gain,
):
    ring = Ring(n)
    member = lax.axis_index("group")
    core, y = member % 2, member // 2
    block_count = block_kinds.shape[0]
    width = series_in.shape[1]
    block_len = series_in.shape[0] // block_count
    groups = block_count // GROUP
    lay = Layout(n, width, block_len, expand_weight.shape[1])
    length = lay.length
    share = branch_gain.shape[0]
    fine = y == 0

    def right(v):
        return lax.ppermute(v, "dp", ring.right)

    def left(v):
        return lax.ppermute(v, "dp", ring.left)

    def cut(v, h, rows):
        return lax.dynamic_slice_in_dim(v, h * rows, rows, axis=0)

    def si_half(h):
        s, i = (STRIDES[0] * width // n) // 2, (lay.taps[0] * width // n) // 2
        s2, i2 = (STRIDES[1] * width // n) // 2, (lay.taps[1] * width // n) // 2
        return jnp.where(
            fine,
            jnp.concatenate([cut(fine_shrink, h, s), cut(fine_isometric, h, i)]),
            jnp.concatenate([cut(coarse_shrink, h, s2), cut(coarse_isometric, h, i2)]),
        )

    def blocks_of(v, first, count):
        v = lax.dynamic_slice_in_dim(v, first * width, count * width, axis=1)
        return jnp.concatenate([v[:, j * width : (j + 1) * width] for j in range(count)])

    def gf_half(h):
        a, b = STRIDES[0] // 2, STRIDES[1] // 2
        fine_part = blocks_of(fine_grow, h * a, a)
        fine_part = jnp.pad(fine_part, ((0, lay.g_half - fine_part.shape[0]), (0, 0)))
        grow = jnp.where(fine, fine_part, blocks_of(coarse_grow, h * b, b))
        first = jnp.concatenate([contract_weight, merge_weight])
        second = jnp.concatenate([trend_weight, blocks_of(expand_weight, 0, lay.chunks)])
        first = jnp.pad(first, ((0, lay.f_half - first.shape[0]), (0, 0)))
        second = jnp.pad(second, ((0, lay.f_half - second.shape[0]), (0, 0)))
        return jnp.concatenate([grow, jnp.where(h == 0, first, second)])

    si_own, gf_own = si_half(core), gf_half(core)
    offsets = [0]
    si, gf = Pieces(), Pieces()
    si.add(0, 0, 0, si_own)
    si.add(0, 1, 0, si_half(1 - core))
    gf.add(0, 0, 0, gf_own)
    gf.add(0, 1, 0, gf_half(1 - core))
    for k in range(1, n // 2):
        offsets += [-k, k]
    offsets.append(n // 2)

    def source(offset):
        return offsets.index(offset if abs(offset) < n // 2 else n // 2)

    where = jnp.stack([y, core] + [ring.index(o) for o in offsets]).astype(jnp.int32)

    gains = jnp.stack([branch_gain, middle_gain, output_gain]).astype(F32)
    gains = lax.dynamic_update_slice(
        jnp.zeros((3, width), F32), gains, (jnp.int32(0), ring.me * share)
    )
    x_own = series_in.reshape(groups, length, width)
    kinds_own = block_kinds.reshape(groups, GROUP)
    x_other = []
    kinds_other = None
    last = n // 2
    ways = {"r": {}, "l": {}}
    got = {}
    si_r = si_l = si_own
    gf_r = gf_l = gf_own
    step_index = 1
    prepared = None
    hat_rows = lay.si_half // 2
    gf_rows = (lay.g_half + lay.f_half) // 2

    def prepare(kinds_other, *xs):
        other = jnp.stack(xs)
        x_all = jnp.concatenate([x_own, other])
        kinds = jnp.concatenate([kinds_own, kinds_other.astype(jnp.int32).reshape(groups, GROUP)])
        r = jnp.arange(length, dtype=jnp.int32)
        npos = jnp.where(fine, lay.npos[0], lay.npos[1])
        stride = jnp.where(fine, STRIDES[0], STRIDES[1])
        taps = jnp.where(fine, lay.taps[0], lay.taps[1])
        step = (r % npos) * stride + r // npos
        order = (step[:, None] == r[None, :]).astype(F32).astype(BF)
        counts = window_counts(kinds, block_len, step)
        mean = jnp.einsum("grj,gjd->grd", counts, x_all, preferred_element_type=F32)
        season = jnp.einsum("rj,gjd->grd", order, x_all, preferred_element_type=F32)
        season = season - mean * (1.0 / WINDOW)
        own_counts = window_counts(kinds_own, block_len, r)
        trend = jnp.einsum("gij,gjd->gid", own_counts, x_own, preferred_element_type=F32)
        trend_low = (trend * (1.0 / WINDOW)).astype(BF)
        q = jnp.arange(2 * groups * max(lay.npos), dtype=jnp.int32)
        group = q // npos
        pos = q % npos
        block = pos // taps
        firsts, _ = series_bounds(kinds)
        first = jnp.zeros_like(q)
        for g in range(2 * groups):
            for b in range(GROUP):
                first = jnp.where((group == g) & (block == b), firsts[g, b], first)
        age = (pos - first * taps)[:, None]
        return season, season.astype(BF), order, own_counts, trend_low, age

    doublings = []
    size = 1
    while size < n:
        doublings.append(size)
        size *= 2
    for t in range(1, last + 3):
        sends = {}
        if t <= last:
            if t < last:
                sends["sr"], sends["sl"] = (si_r, right), (si_l, left)
            else:
                sends["sr"], sends["sl"] = (si_r[:hat_rows], right), (si_l[hat_rows:], left)
        if 1 <= t - 1 <= last:
            if t - 1 < last:
                sends["gr"], sends["gl"] = (gf_r, right), (gf_l, left)
            else:
                sends["gr"], sends["gl"] = (gf_r[:gf_rows], right), (gf_l[gf_rows:], left)
            sends["csr"], sends["csl"] = (si_r, swap_core), (si_l, swap_core)
        if 1 <= t - 2 <= last:
            sends["cgr"], sends["cgl"] = (gf_r, swap_core), (gf_l, swap_core)
        if t <= groups:
            sends["x"] = (x_own[t - 1], swap_y)
        if t == 1:
            sends["k"] = (block_kinds.astype(F32), swap_y)
        if t <= len(doublings):
            sends["gain"] = (gains, exchange("dp", n, doublings[t - 1]))
        work, given = None, ()
        if t == last + 1:
            work, given = prepare, (kinds_other, *x_other)
        arrived, done = slot(sends, work, given)
        if done:
            prepared = done
        if "x" in arrived:
            x_other.append(arrived["x"])
        if "k" in arrived:
            kinds_other = arrived["k"]
        if "gain" in arrived:
            gains = gains + arrived["gain"]

        def keep(pieces, step, other, a, b, half):
            pieces.add(source(-step), other, 0, a)
            pieces.add(source(step), other, half if step == last else 0, b)

        if "csr" in arrived:
            keep(si, t - 1, 1, arrived["csr"], arrived["csl"], hat_rows)
        if "cgr" in arrived:
            keep(gf, t - 2, 1, arrived["cgr"], arrived["cgl"], gf_rows)
        if "sr" in arrived:
            si_r, si_l = arrived["sr"], arrived["sl"]
            keep(si, t, 0, si_r, si_l, hat_rows)
        if "gr" in arrived:
            gf_r, gf_l = arrived["gr"], arrived["gl"]
            keep(gf, t - 1, 0, gf_r, gf_l, gf_rows)
    season, season_low, order, own_counts, trend_low, age = prepared
    gain_b, gain_m, gain_o = gains[0:1], gains[1:2], gains[2:3]

    shrunk, iso, mixed = shrink_forward(lay, where, si, season_low, age, gain_b)
    branch_other, up_other = grow_forward(lay, where, gf, 1, mixed, season, order, gain_b)
    parts = [branch_other[g : g + 1] for g in range(groups)]
    received = [swap_y(p) for p in parts]
    branch_own, up_own = grow_forward(lay, where, gf, 0, mixed, season, order, gain_b)

    grads_in = out_grad.reshape(groups, length, width)
    outs, back_own, back_got, trend_back, saved, dense_gains = [], [], [], [], [], None
    for g in range(groups):
        made = dense(
            lay, where, gf, g, branch_own, received[g], trend_low, grads_in, gain_m, gain_o
        )
        outs.append(made[0])
        back_own.append(made[1])
        back_got.append(swap_y(made[2]))
        trend_back.append(made[3])
        saved.append(made[4:9])
        dense_gains = made[9] if dense_gains is None else dense_gains + made[9]
    series_out = jnp.concatenate(outs)

    ring_order = [n // 2]
    for k in range(n // 2 - 1, 0, -1):
        ring_order += [k, -k]
    ring_order.append(0)
    spot = jnp.zeros((n,), jnp.int32)
    for place, offset in enumerate(ring_order):
        spot = jnp.where(jnp.arange(n) == ring.index(offset), place, spot)
    f_local = dense_weights(lay, where, spot, branch_own, received, trend_low, grads_in, saved)

    pre_own, mixed_back_own, sum_own, gains_own = grow_backward(
        lay, where, gf, 0, jnp.stack(back_own), up_own, season, order, gain_b
    )
    pre_other, mixed_back_other, sum_other, gains_other = grow_backward(
        lay, where, gf, 1, jnp.stack(back_got), up_other, season, order, gain_b
    )
    g_local = grow_weight(lay, where, spot, mixed, pre_own, pre_other)
    shrink_pre, si_local, gains_si = shrink_backward(
        lay, where, spot, si, mixed_back_own, mixed_back_other, shrunk, iso, season_low, age, gain_b
    )

    class Chain:
        def __init__(self, local):
            self.local = local
            self.keep = local[0]
            self.got = None
            self.step = last
            self.r = self.l = None
            self.half = local.shape[2] // 2

        def give(self):
            return self.local[1]

        def here(self, place):
            return self.keep[place].astype(F32) + self.got[place].astype(F32)

        def sends(self):
            k = self.step
            if k == last:
                part = self.here(0)
                return part[: self.half].astype(BF), part[self.half :].astype(BF)
            place = 1 + 2 * (last - 1 - k)
            a, b = self.here(place), self.here(place + 1)
            if k == last - 1:
                h = self.half
                a = jnp.concatenate([a[:h] + self.r.astype(F32), a[h:]])
                b = jnp.concatenate([b[:h], b[h:] + self.l.astype(F32)])
            else:
                a, b = a + self.r.astype(F32), b + self.l.astype(F32)
            return a.astype(BF), b.astype(BF)

        def receive(self, r, l):
            self.r, self.l = r, l
            self.step -= 1

        def total(self):
            return (self.here(n - 1) + self.r.astype(F32) + self.l.astype(F32)).astype(BF)

    f, g, s = Chain(f_local), Chain(g_local), Chain(si_local)
    f.got = swap_core(f.give())

    def move(chains, extra=None, work=None, given=()):
        sends = dict(extra or {})
        for name, chain in chains.items():
            a, b = chain.sends()
            sends[name + "r"], sends[name + "l"] = (a, right), (b, left)
        arrived, done = slot(sends, work, given)
        for name, chain in chains.items():
            chain.receive(arrived[name + "r"], arrived[name + "l"])
        return arrived, done

    def season_work(pre, sum_own, sum_other):
        return season_backward(lay, where, si, pre, sum_own, sum_other, order)

    for _ in range(last - 2):
        move({"f": f})
    arrived, _ = move({"f": f}, {"g": (g.give(), swap_core)})
    g.got = arrived["g"]
    arrived, _ = move({"f": f, "g": g}, {"s": (s.give(), swap_core)})
    s.got = arrived["s"]
    f_mine = f.total()
    arrived, (season_own, season_send) = move(
        {"g": g, "s": s}, {"f": (f_mine, swap_y)}, season_work, (shrink_pre, sum_own, sum_other)
    )
    f_half = (f_mine.astype(F32) + arrived["f"].astype(F32)).astype(BF)
    tail_sends = [season_send[i] for i in range(groups)]
    tail = []
    extra = {"f": (f_half, swap_core)}
    f_other = g_y = g_core = None
    while s.step > 0:
        chains = {"s": s}
        if g.step > 0:
            chains["g"] = g
        elif g_y is None:
            g_mine = g.total()
            extra["g"] = (g_mine, swap_y)
        elif g_core is None:
            extra["gc"], extra["gd"] = (g_mine, swap_core), (g_y, swap_core)
        if tail_sends:
            extra["x"] = (tail_sends.pop(0), swap_y)
        arrived, _ = move(chains, extra)
        extra = {}
        if "f" in arrived:
            f_other = arrived["f"]
        if "g" in arrived:
            g_y = arrived["g"]
        if "gc" in arrived:
            g_core = (arrived["gc"], arrived["gd"])
        if "x" in arrived:
            tail.append(arrived["x"])
    s_mine = s.total()
    extra = {"s": (s_mine, swap_y)}
    if g_y is None:
        g_mine = g.total()
        g_y = swap_y(g_mine)
    if g_core is None:
        extra["gc"], extra["gd"] = (g_mine, swap_core), (g_y, swap_core)
    while tail_sends:
        tail.append(swap_y(tail_sends.pop(0)))

    def finish(*tail):
        total = season_own.astype(F32) + jnp.stack(tail).astype(F32)
        rest = jnp.stack(trend_back) - total
        spread = (rest * (1.0 / WINDOW)).astype(BF)
        averaged = jnp.einsum("gij,gid->gjd", own_counts, spread, preferred_element_type=F32)
        return ((total + averaged).astype(BF),)

    arrived, (series_grad,) = slot(extra, finish, tail)
    if "gc" in arrived:
        g_core = (arrived["gc"], arrived["gd"])
    s_y = arrived["s"]
    s_core = (swap_core(s_mine), swap_core(s_y))

    def both(mine, other):
        return jnp.where(core == 0, mine, other), jnp.where(core == 0, other, mine)

    def branches(mine, over_y):
        return jnp.where(fine, mine, over_y), jnp.where(fine, over_y, mine)

    s_fine, s_coarse = branches(s_mine, s_y)
    t_fine, t_coarse = branches(*s_core)
    g_fine, g_coarse = branches(g_mine, g_y)
    h_fine, h_coarse = branches(*g_core)

    def si_out(b, mine, other):
        lo, hi = both(mine, other)
        (f0, r0, _, _), (f1, r1, _, _) = lay.si_parts(b)
        shrink = jnp.concatenate([lo[f0 : f0 + r0], hi[f0 : f0 + r0]])
        return shrink.astype(F32), jnp.concatenate([lo[f1 : f1 + r1], hi[f1 : f1 + r1]]).astype(F32)

    def g_out(b, mine, other):
        lo, hi = both(mine, other)
        cols = [v[r : r + k] for v in (lo, hi) for r, k, _ in lay.g_parts(b)]
        return jnp.concatenate(cols, axis=1).astype(F32)

    fine_shrink_grad, fine_iso_grad = si_out(0, s_fine, t_fine)
    coarse_shrink_grad, coarse_iso_grad = si_out(1, s_coarse, t_coarse)
    fine_grow_grad, coarse_grow_grad = g_out(0, g_fine, h_fine), g_out(1, g_coarse, h_coarse)
    lo, hi = both(f_half, f_other)
    (a0, a1, _, _), (b0, b1, _, _) = lay.f_parts(0)
    z = lay.g_half
    contract_grad = lo[a0 - z : a0 - z + a1].astype(F32)
    merge_grad = lo[b0 - z : b0 - z + b1].astype(F32)
    rest = [hi[a - z : a - z + rows].astype(F32) for a, rows, _, _ in lay.f_parts(1)]
    trend_grad, expand_grad = rest[0], jnp.concatenate(rest[1:], axis=1)

    gain_grads = jnp.concatenate([gains_own + gains_other + gains_si, dense_gains])
    for size in doublings:
        gain_grads = gain_grads + exchange("dp", n, size)(gain_grads)
    for size in (1, 2):
        gain_grads = gain_grads + exchange("group", 4, size)(gain_grads)
    gain_grads = lax.dynamic_slice(gain_grads, (jnp.int32(0), ring.me * share), (3, share))
    return (
        series_out,
        series_grad.reshape(series_in.shape),
        fine_shrink_grad,
        coarse_shrink_grad,
        fine_iso_grad,
        coarse_iso_grad,
        fine_grow_grad,
        coarse_grow_grad,
        merge_grad,
        expand_grad,
        contract_grad,
        trend_grad,
        gain_grads[0],
        gain_grads[1],
        gain_grads[2],
    )


def solution(mesh):
    n = mesh.shape["dp"]
    rows = P(("dp", "group"), None)
    weight = P("dp", None)
    return jax.shard_map(
        lambda *args: on_device(n, *args),
        mesh=mesh,
        in_specs=(rows, P(("dp", "group")), rows) + (weight,) * 10 + (P("dp"),) * 3,
        out_specs=(rows, rows) + (weight,) * 10 + (P("dp"),) * 3,
        check_vma=False,
    )
```

```python
import functools
import math

import jax
import jax.numpy as jnp
from jax import lax
from jax.experimental import pallas as pl
from jax.experimental.pallas import tpu as pltpu
from jax.sharding import PartitionSpec as P

STRIDES = (12, 16)
WINDOW = 25
HALF = WINDOW // 2
GROUP = 4
BF = jnp.bfloat16
F32 = jnp.float32
MIB = 1024 * 1024
CORE_SWAP = ((0, 1), (1, 0), (2, 3), (3, 2))
Y_SWAP = ((0, 2), (2, 0), (1, 3), (3, 1))


class Layout:
    def __init__(self, n, width, block_len, ff):
        self.n, self.width, self.block_len = n, width, block_len
        self.length = GROUP * block_len
        self.taps = tuple(block_len // s for s in STRIDES)
        self.shrink = tuple(s * width for s in STRIDES)
        self.iso = tuple(p * width for p in self.taps)
        self.si_half = (self.shrink[0] + self.iso[0]) // (2 * n)
        self.k = width // n
        self.g_half = max(STRIDES) // 2 * self.k
        self.chunks = ff // width
        self.merge, self.contract = 2 * width // n, ff // n
        self.f_half = max(self.contract + self.merge, self.k * (1 + self.chunks))
        self.npos = tuple(GROUP * p for p in self.taps)

    def si_parts(self, b):
        s, i = self.shrink[b] // self.n, self.iso[b] // self.n
        return [(0, s // 2, 0, s), (s // 2, i // 2, self.shrink[b], i)]

    def g_parts(self, b):
        return [(j * self.k, self.k, j) for j in range(STRIDES[b] // 2)]

    def f_parts(self, h):
        base = self.g_half
        if h == 0:
            return [
                (base, self.contract, "contract", 0),
                (base + self.contract, self.merge, "merge", 0),
            ]
        found = [(base, self.k, "trend", 0)]
        for j in range(self.chunks):
            found.append((base + (1 + j) * self.k, self.k, "expand", j))
        return found


def held(*values):
    return lax.optimization_barrier(values)


class Ring:
    def __init__(self, n):
        self.n = n
        order = list(range(0, n, 2)) + list(range(n - 1, 0, -2))
        self.right = [(order[k], order[(k + 1) % n]) for k in range(n)]
        self.left = [(b, a) for a, b in self.right]
        d = lax.axis_index("dp")
        self.me = d
        self.pos = jnp.where(d % 2 == 0, d // 2, n - 1 - d // 2)

    def index(self, offset):
        if offset == 0:
            return self.me
        r = (self.pos + offset) % self.n
        return jnp.where(r < self.n // 2, 2 * r, 2 * (self.n - 1 - r) + 1)


def slot(sends, work=None, given=()):
    names = list(sends)
    tied = held(*[sends[k][0] for k in names], *given)
    moved = [sends[k][1](v) for k, v in zip(names, tied)]
    done = tuple(work(*tied[len(names) :])) if work is not None else ()
    out = held(*moved, *done)
    return dict(zip(names, out[: len(names)])), out[len(names) :]


def swap_core(v):
    return lax.ppermute(v, "group", CORE_SWAP)


def swap_y(v):
    return lax.ppermute(v, "group", Y_SWAP)


def dot(a, b):
    return jnp.dot(a, b, preferred_element_type=F32)


def dot_t(a, b):
    return lax.dot_general(a, b, (((1,), (1,)), ((), ())), preferred_element_type=F32)


def dot_w(a, b):
    return lax.dot_general(a, b, (((0,), (0,)), ((), ())), preferred_element_type=F32)


def normal(v):
    center = jnp.mean(v, axis=-1, keepdims=True)
    centered = v - center
    inverse = lax.rsqrt(jnp.mean(centered * centered, axis=-1, keepdims=True) + 1e-05)
    return centered * inverse, inverse


def normal_back(grad, hat, inverse, gain):
    g = grad * gain
    a = jnp.mean(g, axis=-1, keepdims=True)
    b = jnp.mean(g * hat, axis=-1, keepdims=True)
    return inverse * (g - a - hat * b)


def erf_pair(h):
    x = jnp.abs(h) * (1.0 / math.sqrt(2.0))
    d = 1.0 + 0.3275911 * x
    t = pl.reciprocal(d, approx=True)
    t = t * (2.0 - d * t)
    e = jnp.exp(-0.5 * h * h)
    p = t * (
        0.254829592
        + t * (-0.284496736 + t * (1.421413741 + t * (-1.453152027 + t * 1.061405429)))
    )
    q = 0.5 * p * e
    return jnp.where(h >= 0, 1.0 - q, q), h * e * (1.0 / math.sqrt(2.0 * math.pi))


def over(parts, first, rows):
    for part in parts:
        lo, hi = max(first, part[0]), min(first + rows, part[0] + part[1])
        if lo < hi:
            yield lo - first, hi - lo, lo - part[0], part


def start_copy(piece, row, rows, whole, at, sem):
    at = at if isinstance(at, int) else pl.multiple_of(at, 16)
    pltpu.make_async_copy(
        piece.at[pl.ds(row, rows)], whole.at[pl.ds(at, rows)], sem
    ).start()


def wait_rows(whole, first, rows, sem):
    view = whole.at[pl.ds(first, rows)]
    pltpu.make_async_copy(view, view, sem).wait()


class Pieces:
    def __init__(self):
        self.meta, self.arrays = [], []

    def add(self, source, other, first, array):
        self.meta.append((source, other, first, array.shape[0]))
        self.arrays.append(array)


def load_si(lay, b, where, meta, refs, whole, sems):
    core = where[1]
    for (source, other, first, rows), ref in zip(meta, refs):
        src = where[2 + source]
        h = 1 - core if other else core
        for row, count, inside, part in over(lay.si_parts(b), first, rows):
            _, half, base, shard = part
            at = base + src * shard + h * half + inside
            start_copy(ref, row, count, whole, at, sems.at[0 if base == 0 else 1])


def load_g(lay, b, where, meta, refs, whole, sem):
    core = where[1]
    for (source, other, first, rows), ref in zip(meta, refs):
        src = where[2 + source]
        h = 1 - core if other else core
        for row, count, inside, part in over(lay.g_parts(b), first - lay.si_half, rows):
            at = (h * (STRIDES[b] // 2) + part[2]) * lay.width + src * lay.k + inside
            start_copy(ref, row, count, whole, at, sem)


def load_f(lay, c, where, meta, refs, wholes, sems):
    names = ("merge", "contract", "trend", "expand")
    for (source, other, first, rows), ref in zip(meta, refs):
        src = where[2 + source]
        h = 1 - c if other else c
        for row, count, inside, part in over(lay.f_parts(h), first - lay.si_half, rows):
            t = names.index(part[2])
            at = part[3] * lay.width + src * part[1] + inside
            start_copy(ref, row, count, wholes[t], at, sems.at[t])


def any_spec():
    return pl.BlockSpec(memory_space=pl.ANY)


def vmem_spec():
    return pl.BlockSpec(memory_space=pltpu.VMEM)


def smem_spec():
    return pl.BlockSpec(memory_space=pltpu.SMEM)


def cost(flops, moved):
    return pl.CostEstimate(flops=int(flops), bytes_accessed=int(moved), transcendentals=0)


def by_branch(where, body):
    for b in range(2):
        pl.when(where[0] == b)(functools.partial(body, b))


def half_of(lay, where, sibling, fs, cs, fi, ci, fg, cg, weights):
    width, k = lay.width, lay.k
    base = lay.si_half
    rows = base + lay.g_half + lay.f_half

    def kernel(where, fs, cs, fi, ci, fg, cg, contract, merge, trend, expand, out, sems):
        def moves(b, h):
            found = []
            for i, (first, half, _, _) in enumerate(lay.si_parts(b)):
                source = ((fs, fi), (cs, ci))[b][i]
                found.append((source.at[pl.ds(h * half, half)], out.at[pl.ds(first, half)]))
            for first, count, j in lay.g_parts(b):
                col = (h * (STRIDES[b] // 2) + j) * width
                source = (fg, cg)[b].at[:, pl.ds(col, width)]
                found.append((source, out.at[pl.ds(base + first, count)]))
            named = {"contract": contract, "merge": merge, "trend": trend}
            for first, count, name, j in lay.f_parts(h):
                source = expand.at[:, pl.ds(j * width, width)] if name == "expand" else named[name]
                found.append((source, out.at[pl.ds(base + first, count)]))
            return [(x, y, sems.at[i]) for i, (x, y) in enumerate(found)]

        for b in range(2):
            for h in range(2):

                @pl.when((where[0] == b) & (where[1] == (1 - h if sibling else h)))
                def _(b=b, h=h):
                    used = lay.g_parts(b)[-1][0] + k
                    if used < lay.g_half:
                        out[base + used : base + lay.g_half, :] = jnp.zeros(
                            (lay.g_half - used, width), BF
                        )
                    used = lay.f_parts(h)[-1][0] + lay.f_parts(h)[-1][1]
                    if used < lay.g_half + lay.f_half:
                        out[base + used :, :] = jnp.zeros((rows - base - used, width), BF)
                    for x, y, sem in moves(b, h):
                        pltpu.make_async_copy(x, y, sem).start()
                    for x, y, sem in moves(b, h):
                        pltpu.make_async_copy(x, y, sem).wait()

    return pl.pallas_call(
        kernel,
        out_shape=jax.ShapeDtypeStruct((rows, width), BF),
        in_specs=[smem_spec()] + [any_spec()] * 10,
        out_specs=vmem_spec(),
        scratch_shapes=[pltpu.SemaphoreType.DMA((8 + max(STRIDES),))],
        compiler_params=pltpu.CompilerParams(vmem_limit_bytes=60 * MIB),
        cost_estimate=cost(0, 4 * rows * width),
        name="sibling_half" if sibling else "own_half",
    )(where, fs, cs, fi, ci, fg, cg, *weights)


def bounds_of(kinds, base):
    firsts, lasts = [jnp.int32(0)], [jnp.int32(GROUP - 1)]
    for b in range(1, GROUP):
        firsts.append(jnp.where(kinds[base + b] == 2, firsts[-1], b))
    for b in reversed(range(GROUP - 1)):
        lasts.insert(0, jnp.where(kinds[base + b + 1] == 2, lasts[0], b))
    return firsts, lasts


def counts_of(lay, kinds, base, step):
    firsts, lasts = bounds_of(kinds, base)
    length = lay.length
    first = jnp.zeros_like(step)
    last = jnp.full_like(step, length - 1)
    for b in range(GROUP):
        inside = (step >= b * lay.block_len) & (step < (b + 1) * lay.block_len)
        first = jnp.where(inside, firsts[b] * lay.block_len, first)
        last = jnp.where(inside, lasts[b] * lay.block_len + (lay.block_len - 1), last)
    j = lax.broadcasted_iota(jnp.int32, (length, length), 1)
    low = jnp.maximum(step - HALF, first)
    high = jnp.minimum(step + HALF, last)
    count = jnp.where((j >= low) & (j <= high), 1.0, 0.0)
    before = jnp.maximum(first - step + HALF, 0).astype(F32)
    after = jnp.maximum(step + HALF - last, 0).astype(F32)
    count += jnp.where(j == first, before, 0.0)
    count += jnp.where(j == last, after, 0.0)
    return count.astype(BF)


def season_kernel(lay, kinds, step, x, with_trend):
    width, length = lay.width, lay.length
    groups = x.shape[0]

    def kernel(kinds_ref, step_ref, x_ref, season_ref, low_ref, *refs):
        base = pl.program_id(0) * GROUP
        step = step_ref[...]
        x = x_ref[0]
        j = lax.broadcasted_iota(jnp.int32, (length, length), 1)
        order = jnp.where(j == step, 1.0, 0.0).astype(BF)
        season = dot(order, x) - dot(counts_of(lay, kinds_ref, base, step), x) * (1.0 / WINDOW)
        season_ref[0] = season
        low_ref[0] = season.astype(BF)
        if with_trend:
            counts_ref, trend_ref, order_ref = refs
            order_ref[...] = order
            plain = lax.broadcasted_iota(jnp.int32, (length, 1), 0)
            counts = counts_of(lay, kinds_ref, base, plain)
            counts_ref[0] = counts
            trend_ref[0] = (dot(counts, x) * (1.0 / WINDOW)).astype(BF)

    group = pl.BlockSpec((1, length, width), lambda g: (g, 0, 0))
    square = pl.BlockSpec((1, length, length), lambda g: (g, 0, 0))
    shapes = [
        jax.ShapeDtypeStruct((groups, length, width), F32),
        jax.ShapeDtypeStruct((groups, length, width), BF),
    ]
    specs = [group, group]
    if with_trend:
        shapes += [
            jax.ShapeDtypeStruct((groups, length, length), BF),
            jax.ShapeDtypeStruct((groups, length, width), BF),
            jax.ShapeDtypeStruct((length, length), BF),
        ]
        specs += [square, group, pl.BlockSpec((length, length), lambda g: (0, 0))]
    return pl.pallas_call(
        kernel,
        grid=(groups,),
        out_shape=shapes,
        in_specs=[smem_spec(), pl.BlockSpec((length, 1), lambda g: (0, 0)), group],
        out_specs=specs,
        compiler_params=pltpu.CompilerParams(vmem_limit_bytes=60 * MIB),
        cost_estimate=cost(6 * groups * length * length * width, 12 * groups * length * width),
        name="season_trend" if with_trend else "season",
    )(kinds, step, x)


def tap_rows(x, age, k):
    if k == 0:
        return x
    return jnp.where(age >= k, pltpu.roll(x, k, 0), 0.0)


def step_rows(own, other, s, npos):
    cut = slice(s * npos, (s + 1) * npos)
    x = jnp.concatenate([own[:, cut, :], other[:, cut, :]], axis=0)
    return x.reshape(x.shape[0] * npos, x.shape[2])


def shrink_forward(lay, where, si, low_own, low_other, kinds_own, kinds_other, gain):
    n, width = lay.n, lay.width
    groups = 2 * low_own.shape[0]
    most = groups * max(lay.npos)
    count = len(si.arrays)
    total = lay.shrink[0] + lay.iso[0]

    def kernel(where, kinds_own, kinds_other, gain_ref, own_ref, other_ref, *refs):
        pieces, rest = refs[:count], refs[count:]
        shrunk_ref, iso_ref, mixed_ref, age_ref, whole_out, whole, sems = rest

        def body(b):
            load_si(lay, b, where, si.meta, pieces, whole, sems)
            npos = lay.npos[b]
            m = groups * npos
            wait_rows(whole, 0, lay.shrink[b], sems.at[0])
            z = jnp.zeros((m, width), F32)
            for s in range(STRIDES[b]):
                z += dot(step_rows(own_ref, other_ref, s, npos), whole[s * width : (s + 1) * width])
            shrunk = jnp.tanh(z)
            shrunk_ref[:m] = shrunk
            low = shrunk.astype(BF).astype(F32)
            wait_rows(whole, lay.shrink[b], lay.iso[b], sems.at[1])
            pltpu.make_async_copy(whole, whole_out, sems.at[2]).start()
            taps = lay.taps[b]
            base = lay.shrink[b]
            row = lax.broadcasted_iota(jnp.int32, (m, 1), 0)
            age = jnp.zeros_like(row)
            for g in range(groups):
                own = g < groups // 2
                kinds = kinds_own if own else kinds_other
                firsts, _ = bounds_of(kinds, (g if own else g - groups // 2) * GROUP)
                for i in range(GROUP):
                    lo = g * npos + i * taps
                    inside = (row >= lo) & (row < lo + taps)
                    age = jnp.where(inside, row - lo + (i - firsts[i]) * taps, age)
            age_ref[:m] = age
            e = jnp.zeros((m, width), F32)
            for k in range(taps):
                at = base + (taps - 1 - k) * width
                e += dot(tap_rows(low, age, k).astype(BF), whole[at : at + width])
            iso = jnp.tanh(e)
            iso_ref[:m] = iso
            hat, _ = normal(iso + shrunk)
            mixed_ref[:m] = (hat * gain_ref[...]).astype(BF)
            pltpu.make_async_copy(whole, whole_out, sems.at[2]).wait()

        by_branch(where, body)

    return pl.pallas_call(
        kernel,
        out_shape=[
            jax.ShapeDtypeStruct((most, width), F32),
            jax.ShapeDtypeStruct((most, width), F32),
            jax.ShapeDtypeStruct((most, width), BF),
            jax.ShapeDtypeStruct((most, 1), jnp.int32),
            jax.ShapeDtypeStruct((total, width), BF),
        ],
        in_specs=[smem_spec()] * 3 + [vmem_spec()] * 3 + [any_spec()] * count,
        out_specs=[vmem_spec()] * 4 + [any_spec()],
        scratch_shapes=[pltpu.VMEM((total, width), BF), pltpu.SemaphoreType.DMA((3,))],
        compiler_params=pltpu.CompilerParams(vmem_limit_bytes=60 * MIB),
        cost_estimate=cost(2 * most * width * total, 4 * total * width),
        name="shrink_forward",
    )(where, kinds_own, kinds_other, gain, low_own, low_other, *si.arrays)


def stage(lay, b, copies):
    def view(ref, first, rows, middle):
        return ref.at[:, pl.ds(first, rows), :] if middle else ref.at[pl.ds(first, rows)]

    def run(i):
        for source, target, rows, sems, middle in copies:
            yield pltpu.make_async_copy(
                view(source, i * 4 * rows, 4 * rows, middle),
                view(target, i * 4 * rows, 4 * rows, middle),
                sems.at[i],
            )

    def start(i):
        for c in run(i):
            c.start()

    def wait(i):
        for c in run(i):
            c.wait()

    return start, wait


def grow_forward(lay, where, gf, part, mixed, season, order, gain):
    width = lay.width
    groups = season.shape[0]
    length = lay.length
    pieces_in = isinstance(gf, Pieces)
    arrays = gf.arrays if pieces_in else [gf]
    count = len(arrays)
    most = max(STRIDES) * width
    runs = max(STRIDES) // 4

    def kernel(where, gain_ref, order_ref, mixed_ref, season_in, *refs):
        pieces, rest = refs[:count], refs[count:]
        outs, up_out = rest[:groups], rest[groups]
        scratch = rest[groups + 1 + pieces_in :]
        rows_ref, whole, season_ref, up_ref, in_sems, w_sems, up_sems, sems = scratch

        def body(b):
            npos = lay.npos[b]
            m = groups * npos
            copies = [(season_in, season_ref, npos, in_sems, True)]
            if not pieces_in:
                copies.append((pieces[0], whole, width, w_sems, False))
            start, wait = stage(lay, b, copies)
            up_start, up_wait = stage(lay, b, [(up_ref, up_out, npos, up_sems, True)])
            if pieces_in:
                load_g(lay, b, where, gf.meta, pieces, whole, sems.at[0])
            for i in range(STRIDES[b] // 4):
                start(i)
            if pieces_in:
                wait_rows(whole, 0, STRIDES[b] * width, sems.at[0])
                pltpu.make_async_copy(whole, rest[groups + 1], sems.at[1]).start()
            x = mixed_ref[part * m : (part + 1) * m]
            gain = gain_ref[...]
            for s in range(STRIDES[b]):
                if s % 4 == 0:
                    wait(s // 4)
                cut = slice(s * npos, (s + 1) * npos)
                up = jnp.tanh(dot(x, whole[s * width : (s + 1) * width]))
                up_ref[:, cut, :] = up.reshape(groups, npos, width)
                hat, _ = normal(up + season_ref[:, cut, :].reshape(m, width))
                rows_ref[:, cut, :] = (hat * gain).astype(BF).reshape(groups, npos, width)
                if s % 4 == 3:
                    up_start(s // 4)
            for g in range(groups):
                outs[g][0] = dot_w(order_ref[...], rows_ref[g]).astype(BF)
            for i in range(STRIDES[b] // 4):
                up_wait(i)
            if pieces_in:
                pltpu.make_async_copy(whole, rest[groups + 1], sems.at[1]).wait()

        by_branch(where, body)

    shapes = [jax.ShapeDtypeStruct((1, length, width), BF)] * groups
    shapes.append(jax.ShapeDtypeStruct((groups, length, width), F32))
    if pieces_in:
        shapes.append(jax.ShapeDtypeStruct((most, width), BF))
    return pl.pallas_call(
        kernel,
        out_shape=shapes,
        in_specs=[smem_spec()] + [vmem_spec()] * 3 + [any_spec()] * (1 + count),
        out_specs=[vmem_spec()] * groups + [any_spec()] * (1 + pieces_in),
        scratch_shapes=[
            pltpu.VMEM((groups, length, width), BF),
            pltpu.VMEM((most, width), BF),
            pltpu.VMEM((groups, length, width), F32),
            pltpu.VMEM((groups, length, width), F32),
        ]
        + [pltpu.SemaphoreType.DMA((runs,))] * 3
        + [pltpu.SemaphoreType.DMA((2,))],
        compiler_params=pltpu.CompilerParams(vmem_limit_bytes=60 * MIB),
        cost_estimate=cost(
            2 * groups * length * width * (width + length),
            2 * most * width + 14 * groups * length * width,
        ),
        name="grow_forward",
    )(where, gain, order, mixed, season, *arrays)


def grow_backward(lay, where, whole, grads, up, season, order, gain):
    width = lay.width
    groups = season.shape[0]
    length = lay.length
    most = groups * max(lay.npos)
    runs = max(STRIDES) // 4

    def kernel(where, gain_ref, order_ref, up_in, season_in, whole_in, *refs):
        grad_refs, rest = refs[:groups], refs[groups:]
        pre_ref, back_ref, sum_out, gain_grad_ref = rest[:4]
        rows_ref, whole, up_ref, season_ref, sum_ref = rest[4:9]
        sems, sum_sems = rest[9:12], rest[12]

        def body(b):
            npos = lay.npos[b]
            m = groups * npos
            start, wait = stage(
                lay,
                b,
                [
                    (up_in, up_ref, npos, sems[0], True),
                    (season_in, season_ref, npos, sems[1], True),
                    (whole_in, whole, width, sems[2], False),
                ],
            )
            sum_start, sum_wait = stage(lay, b, [(sum_ref, sum_out, npos, sum_sems, True)])
            for i in range(STRIDES[b] // 4):
                start(i)
            for g in range(groups):
                rows_ref[g] = dot(order_ref[...], grad_refs[g][...]).astype(BF)
            total = jnp.zeros((m, width), F32)
            gains = jnp.zeros((1, width), F32)
            for s in range(STRIDES[b]):
                if s % 4 == 0:
                    wait(s // 4)
                cut = slice(s * npos, (s + 1) * npos)
                up = up_ref[:, cut, :].reshape(m, width)
                hat, inverse = normal(up + season_ref[:, cut, :].reshape(m, width))
                g = rows_ref[:, cut, :].reshape(m, width).astype(F32)
                gains += jnp.sum(g * hat, axis=0, keepdims=True)
                d = normal_back(g, hat, inverse, gain_ref[...])
                sum_ref[:, cut, :] = d.reshape(groups, npos, width)
                pre = (d * (1.0 - up * up)).astype(BF)
                pre_ref[:, cut, :] = pre.reshape(groups, npos, width)
                total += dot_t(pre, whole[s * width : (s + 1) * width])
                if s % 4 == 3:
                    sum_start(s // 4)
            back_ref[:m] = total
            gain_grad_ref[...] = gains
            for i in range(STRIDES[b] // 4):
                sum_wait(i)

        by_branch(where, body)

    return pl.pallas_call(
        kernel,
        out_shape=[
            jax.ShapeDtypeStruct((groups, length, width), BF),
            jax.ShapeDtypeStruct((most, width), F32),
            jax.ShapeDtypeStruct((groups, length, width), F32),
            jax.ShapeDtypeStruct((1, width), F32),
        ],
        in_specs=[smem_spec()] + [vmem_spec()] * 2 + [any_spec()] * 3 + [vmem_spec()] * groups,
        out_specs=[vmem_spec(), vmem_spec(), any_spec(), vmem_spec()],
        scratch_shapes=[
            pltpu.VMEM((groups, length, width), BF),
            pltpu.VMEM((whole.shape[0], width), BF),
            pltpu.VMEM((groups, length, width), F32),
            pltpu.VMEM((groups, length, width), F32),
            pltpu.VMEM((groups, length, width), F32),
        ]
        + [pltpu.SemaphoreType.DMA((runs,))] * 4,
        compiler_params=pltpu.CompilerParams(vmem_limit_bytes=60 * MIB),
        cost_estimate=cost(
            2 * groups * length * width * (width + length),
            2 * whole.shape[0] * width + 18 * groups * length * width,
        ),
        name="grow_backward",
    )(where, gain, order, up, season, whole, *grads)


class Outlet:
    def __init__(self, n, rows, width, cuts):
        self.n, self.rows, self.width = n, rows, width
        self.bounds = [(0, n)] if cuts is None else cuts

    def shapes(self):
        sizes = [self.n] + [hi - lo for lo, hi in self.bounds]
        return [jax.ShapeDtypeStruct((c, self.rows, self.width), BF) for c in sizes]

    def scratch(self):
        return [
            pltpu.VMEM((2, self.n, self.rows, self.width), BF),
            pltpu.SemaphoreType.DMA((1 + len(self.bounds),)),
        ]

    def copies(self, held_ref, outs, sems):
        found = [pltpu.make_async_copy(held_ref.at[0], outs[0], sems.at[0])]
        for i, (lo, hi) in enumerate(self.bounds):
            source = held_ref.at[1, pl.ds(lo, hi - lo)]
            found.append(pltpu.make_async_copy(source, outs[1 + i], sems.at[1 + i]))
        return found

    def flush(self, held_ref, outs, sems):
        for c in self.copies(held_ref, outs, sems):
            c.start()
        for c in self.copies(held_ref, outs, sems):
            c.wait()


def grow_weight(lay, where, places, mixed, pre_own, pre_other, outlet):
    n, width, k = lay.n, lay.width, lay.k
    groups = pre_own.shape[0]
    made = len(outlet.shapes())

    def kernel(where, places_ref, mixed_ref, own_ref, other_ref, *refs):
        outs, (out_ref, sems) = refs[:made], refs[made:]

        def body(b):
            npos = lay.npos[b]
            x = mixed_ref[: 2 * groups * npos]
            steps = STRIDES[b] // 2
            for s in range(STRIDES[b]):
                d = dot_w(x, step_rows(own_ref, other_ref, s, npos)).astype(BF)
                side = jnp.where(where[1] == s // steps, 0, 1)
                at = (s % steps) * k
                for shard in range(n):
                    out_ref[side, places_ref[shard], at : at + k, :] = d[shard * k : (shard + 1) * k]
            rest = lay.g_half - steps * k
            if rest:
                out_ref[:, :, steps * k :, :] = jnp.zeros((2, n, rest, width), BF)

        by_branch(where, body)
        outlet.flush(out_ref, outs, sems)

    return pl.pallas_call(
        kernel,
        out_shape=outlet.shapes(),
        in_specs=[smem_spec(), smem_spec()] + [vmem_spec()] * 3,
        out_specs=[any_spec()] * made,
        scratch_shapes=outlet.scratch(),
        compiler_params=pltpu.CompilerParams(vmem_limit_bytes=60 * MIB),
        cost_estimate=cost(4 * groups * lay.length * width * width, 2 * 2 * n * lay.g_half * width),
        name="grow_weight",
    )(where, places, mixed, pre_own, pre_other)


def shrink_backward(lay, where, whole, back_own, back_other, shrunk, iso, age, gain):
    width = lay.width
    most = shrunk.shape[0]

    def kernel(where, age_ref, gain_ref, b0, b1, shrunk_ref, iso_ref, whole_in, *refs):
        pre_ref, iso_pre_ref, gain_grad_ref, whole, sem = refs

        def body(b):
            npos, taps = lay.npos[b], lay.taps[b]
            base = lay.shrink[b]
            source = whole_in.at[pl.ds(base, lay.iso[b])]
            fetch = pltpu.make_async_copy(source, whole.at[pl.ds(0, lay.iso[b])], sem)
            fetch.start()
            m = (most // max(lay.npos)) * npos
            mixed_back = jnp.concatenate([b0[: m // 2], b1[: m // 2]], axis=0)
            shrunk, iso = shrunk_ref[:m], iso_ref[:m]
            hat, inverse = normal(iso + shrunk)
            gain_grad_ref[...] = jnp.sum(mixed_back * hat, axis=0, keepdims=True)
            joint = normal_back(mixed_back, hat, inverse, gain_ref[...])
            iso_pre = (joint * (1.0 - iso * iso)).astype(BF)
            iso_pre_ref[:m] = iso_pre
            age = age_ref[:m]
            total = joint
            fetch.wait()
            for k in range(taps):
                tap = taps - 1 - k
                back = dot_t(iso_pre, whole[tap * width : (tap + 1) * width])
                if k:
                    back = pltpu.roll(jnp.where(age >= k, back, 0.0), m - k, 0)
                total += back
            pre_ref[:m] = (total * (1.0 - shrunk * shrunk)).astype(BF)

        by_branch(where, body)

    return pl.pallas_call(
        kernel,
        out_shape=[
            jax.ShapeDtypeStruct((most, width), BF),
            jax.ShapeDtypeStruct((most, width), BF),
            jax.ShapeDtypeStruct((1, width), F32),
        ],
        in_specs=[smem_spec()] + [vmem_spec()] * 6 + [any_spec()],
        out_specs=[vmem_spec()] * 3,
        scratch_shapes=[pltpu.VMEM((max(lay.iso), width), BF), pltpu.SemaphoreType.DMA],
        compiler_params=pltpu.CompilerParams(vmem_limit_bytes=60 * MIB),
        cost_estimate=cost(2 * most * width * lay.iso[0], 2 * lay.iso[0] * width),
        name="shrink_backward",
    )(where, age, gain, back_own, back_other, shrunk, iso, whole)


def shrink_weight(lay, where, places, iso_pre, pre, shrunk, low_own, low_other, gains, age, outlet):
    width = lay.width
    most = shrunk.shape[0]
    made = len(outlet.shapes())

    def kernel(where, places_ref, age_ref, gains_ref, iso_pre_ref, pre_ref, shrunk_ref, *refs):
        own_ref, other_ref = refs[:2]
        outs, (grad_ref, sems) = refs[2 : 2 + made], refs[2 + made :]
        extra = gains_ref[...].astype(BF)
        for side in range(2):
            for place in range(lay.n):
                grad_ref[side, place, lay.si_half :, :] = extra

        def body(b):
            npos, taps = lay.npos[b], lay.taps[b]
            m = (most // max(lay.npos)) * npos

            def store(part, row, d):
                first, half, _, shard = part
                d = d.astype(BF)
                lo = row
                while lo < row + width:
                    dp, h, r = lo // shard, (lo % shard) // half, lo % half
                    rows = min(half - r, row + width - lo)
                    side = jnp.where(where[1] == h, 0, 1)
                    grad_ref[side, places_ref[dp], first + r : first + r + rows, :] = d[
                        lo - row : lo - row + rows
                    ]
                    lo += rows

            part_s, part_i = lay.si_parts(b)
            low = shrunk_ref[:m].astype(BF).astype(F32)
            age = age_ref[:m]
            iso_pre, pre = iso_pre_ref[:m], pre_ref[:m]
            for k in range(taps):
                tap = taps - 1 - k
                store(part_i, tap * width, dot_w(tap_rows(low, age, k).astype(BF), iso_pre))
            for s in range(STRIDES[b]):
                store(part_s, s * width, dot_w(step_rows(own_ref, other_ref, s, npos), pre))

        by_branch(where, body)
        outlet.flush(grad_ref, outs, sems)

    return pl.pallas_call(
        kernel,
        out_shape=outlet.shapes(),
        in_specs=[smem_spec(), smem_spec()] + [vmem_spec()] * 7,
        out_specs=[any_spec()] * made,
        scratch_shapes=outlet.scratch(),
        compiler_params=pltpu.CompilerParams(vmem_limit_bytes=60 * MIB),
        cost_estimate=cost(2 * most * width * (lay.iso[0] + lay.shrink[0]), 30 * MIB),
        name="shrink_weight",
    )(where, places, age, gains, iso_pre, pre, shrunk, low_own, low_other)


def season_backward(lay, where, whole, pre, sum_own, sum_other, order):
    width, length = lay.width, lay.length
    groups = sum_own.shape[0]
    most = max(lay.shrink)

    def kernel(where, order_ref, pre_ref, own_ref, other_ref, whole_in, *refs):
        outs, (whole, rows_ref, sem) = refs[: groups + 1], refs[groups + 1 :]

        def body(b):
            fetch = pltpu.make_async_copy(
                whole_in.at[pl.ds(0, lay.shrink[b])], whole.at[pl.ds(0, lay.shrink[b])], sem
            )
            fetch.start()
            npos = lay.npos[b]
            m = groups * npos
            fetch.wait()
            for s in range(STRIDES[b]):
                cut = slice(s * npos, (s + 1) * npos)
                d = dot_t(pre_ref[: 2 * m], whole[s * width : (s + 1) * width])
                rows_ref[:groups, cut, :] = (
                    d[:m].reshape(groups, npos, width) + own_ref[:, cut, :]
                ).astype(BF)
                rows_ref[groups:, cut, :] = (
                    d[m:].reshape(groups, npos, width) + other_ref[:, cut, :]
                ).astype(BF)

        by_branch(where, body)
        for g in range(groups):
            outs[0][g] = dot_w(order_ref[...], rows_ref[g]).astype(BF)
            outs[1 + g][...] = dot_w(order_ref[...], rows_ref[groups + g]).astype(BF)

    return pl.pallas_call(
        kernel,
        out_shape=[jax.ShapeDtypeStruct((groups, length, width), BF)]
        + [jax.ShapeDtypeStruct((length, width), BF)] * groups,
        in_specs=[smem_spec()] + [vmem_spec()] * 4 + [any_spec()],
        out_specs=[vmem_spec()] * (1 + groups),
        scratch_shapes=[
            pltpu.VMEM((most, width), BF),
            pltpu.VMEM((2 * groups, length, width), BF),
            pltpu.SemaphoreType.DMA,
        ],
        compiler_params=pltpu.CompilerParams(vmem_limit_bytes=60 * MIB),
        cost_estimate=cost(
            4 * groups * length * width * (width + length),
            2 * most * width + 24 * groups * length * width,
        ),
        name="season_backward",
    )(where, order, pre, sum_own, sum_other, whole)


def dense_whole(lay, where, gf):
    width, ff = lay.width, lay.width * lay.chunks
    count = len(gf.arrays)
    sizes = (2 * width, ff, width, ff)

    def kernel(where, *refs):
        pieces, wholes, sems = refs[:count], refs[count:-1], refs[-1]
        for c in range(2):
            pl.when(where[1] == c)(
                functools.partial(load_f, lay, c, where, gf.meta, pieces, wholes, sems)
            )
        for t in range(4):
            wait_rows(wholes[t], 0, sizes[t], sems.at[t])

    return pl.pallas_call(
        kernel,
        out_shape=[jax.ShapeDtypeStruct((r, width), BF) for r in sizes],
        in_specs=[smem_spec()] + [any_spec()] * count,
        out_specs=[vmem_spec()] * 4,
        scratch_shapes=[pltpu.SemaphoreType.DMA((4,))],
        compiler_params=pltpu.CompilerParams(vmem_limit_bytes=60 * MIB),
        cost_estimate=cost(0, 4 * sum(sizes) * width),
        name="dense_whole",
    )(where, *gf.arrays)


def dense(lay, where, tile, wholes, mine, received, trend_low, out_grad, gain_middle, gain_output):
    width, length, chunks = lay.width, lay.length, lay.chunks
    cuts = 2
    part = length // cuts
    ff = width * chunks

    def kernel(where, tile_ref, gm_ref, go_ref, merge, contract, trend, expand, *refs):
        mine_ref, got_ref, trend_ref, grad_ref = refs[:4]
        (out_ref, jm_ref, js_ref, tb_ref, ml_ref, hid_ref, hg_ref, ll_ref, mg_ref) = refs[4:13]
        gains_ref, slope_ref = refs[13:]
        b = where[0]
        gm, go = gm_ref[...], go_ref[...]
        at_mine = pl.multiple_of(b * width, width)
        at_other = pl.multiple_of((1 - b) * width, width)

        merged = dot(mine_ref[...], merge[pl.ds(at_mine, width)])
        merged += dot(got_ref[...], merge[pl.ds(at_other, width)])
        mhat, minv = normal(merged)
        middle = mhat * gm
        mlow = middle.astype(BF)
        ml_ref[...] = mlow
        lifted = jnp.zeros((part, width), F32)
        for j in range(chunks):
            cols = slice(j * width, (j + 1) * width)
            h = dot(mlow, expand[cols])
            phi, dens = erf_pair(h)
            hid = (h * phi).astype(BF)
            slope_ref[:, cols] = phi + dens
            hid_ref[:, cols] = hid
            lifted += dot(hid, contract[cols])
        ohat, oinv = normal(middle + lifted)
        g_low = grad_ref[0]
        projected = dot(trend_ref[0], trend[...])
        out_ref[...] = (ohat * go + projected).astype(BF)
        g = g_low.astype(F32)
        tb_ref[...] = dot_t(g_low, trend[...])
        d = normal_back(g, ohat, oinv, go)
        llow = d.astype(BF)
        ll_ref[...] = llow
        back = d
        for j in range(chunks):
            cols = slice(j * width, (j + 1) * width)
            hg = (dot_t(llow, contract[cols]) * slope_ref[:, cols]).astype(BF)
            hg_ref[:, cols] = hg
            back += dot_t(hg, expand[cols])
        mg = normal_back(back, mhat, minv, gm).astype(BF)
        mg_ref[...] = mg
        jm_ref[...] = dot_t(mg, merge[pl.ds(at_mine, width)]).astype(BF)
        js_ref[...] = dot_t(mg, merge[pl.ds(at_other, width)]).astype(BF)

        @pl.when(pl.program_id(0) == 0)
        def _():
            gains_ref[...] = jnp.zeros_like(gains_ref)

        gains_ref[0:1, :] += jnp.sum(back * mhat, axis=0, keepdims=True)
        gains_ref[1:2, :] += jnp.sum(g * ohat, axis=0, keepdims=True)

    of_tile = pl.BlockSpec((1, part, width), lambda i, w, t: (t[0], i, 0))
    alone = pl.BlockSpec((part, width), lambda i, w, t: (i, 0))
    shapes = [(width, BF)] * 3 + [(width, F32), (width, BF), (ff, BF), (ff, BF), (width, BF), (width, BF)]
    return pl.pallas_call(
        kernel,
        grid_spec=pltpu.PrefetchScalarGridSpec(
            num_scalar_prefetch=2,
            grid=(cuts,),
            in_specs=[vmem_spec()] * 6 + [alone, alone, of_tile, of_tile],
            out_specs=[pl.BlockSpec((part, w), lambda i, w, t: (i, 0)) for w, _ in shapes]
            + [pl.BlockSpec((2, width), lambda i, w, t: (0, 0))],
            scratch_shapes=[pltpu.VMEM((part, ff), F32)],
        ),
        out_shape=[jax.ShapeDtypeStruct((length, w), t) for w, t in shapes]
        + [jax.ShapeDtypeStruct((2, width), F32)],
        compiler_params=pltpu.CompilerParams(vmem_limit_bytes=60 * MIB),
        cost_estimate=cost(
            2 * length * width * (4 * width + 4 * ff + 2 * width), 12 * MIB + 20 * MIB
        ),
        name="dense",
    )(where, tile, gain_middle, gain_output, *wholes, mine, received, trend_low, out_grad)


def dense_weights(lay, where, places, mine, received, trend_low, out_grad, saved, outlet):
    n, width, chunks, length = lay.n, lay.width, lay.chunks, lay.length
    groups = len(saved)
    made = len(outlet.shapes())
    base = lay.g_half
    (_, contract, _, _), (merge_at, merge, _, _) = lay.f_parts(0)
    merge_at -= base

    def kernel(where, places_ref, *refs):
        refs = list(refs)

        def take(count):
            out = refs[:count]
            del refs[:count]
            return out

        middle, lifted = take(groups), take(groups)
        hidden, slopes = take(groups), take(groups)
        late = take(3 * groups) + take(2)
        outs = take(made)
        out_ref, sems, mine_ref, got_ref, grad_ref, trend_ref, up_ref, late_sems = refs
        core, q = where[1], pl.program_id(0)

        def fetches():
            targets = [r.at[g] for r in (mine_ref, got_ref, grad_ref) for g in range(groups)]
            targets += [trend_ref, up_ref]
            return [
                pltpu.make_async_copy(x, y, late_sems.at[i])
                for i, (x, y) in enumerate(zip(late, targets))
            ]

        def side(h):
            return jnp.where(core == h, 0, 1)

        def total(xs, gs):
            d = None
            for x, g in zip(xs, gs):
                v = dot_w(x, g)
                d = v if d is None else d + v
            return d.astype(BF)

        @pl.when(q == 0)
        def _():
            for f in fetches():
                f.start()
            if merge_at + merge < lay.f_half:
                out_ref[side(0), :, merge_at + merge :, :] = jnp.zeros(
                    (n, lay.f_half - merge_at - merge, width), BF
                )

        d = total([r[...] for r in hidden], [r[...] for r in lifted])
        each = width // contract
        for i in range(each):
            out_ref[side(0), places_ref[q * each + i], 0:contract, :] = d[
                i * contract : (i + 1) * contract
            ]
        d = total([r[...] for r in middle], [r[...] for r in slopes])
        at = pl.ds(pl.multiple_of((1 + q) * lay.k, 16), lay.k)
        for dp in range(n):
            out_ref[side(1), places_ref[dp], at, :] = d[dp * lay.k : (dp + 1) * lay.k]

        @pl.when(q == chunks - 1)
        def _():
            for f in fetches():
                f.wait()
            d = total([trend_ref[g] for g in range(groups)], [up_ref[g] for g in range(groups)])
            for dp in range(n):
                out_ref[side(1), places_ref[dp], 0 : lay.k, :] = d[dp * lay.k : (dp + 1) * lay.k]
            each = width // merge
            for ref, first in ((mine_ref, where[0]), (got_ref, 1 - where[0])):
                d = total([ref[g] for g in range(groups)], [grad_ref[g] for g in range(groups)])
                for i in range(each):
                    out_ref[side(0), places_ref[first * each + i], merge_at : merge_at + merge, :] = d[
                        i * merge : (i + 1) * merge
                    ]
            used = (1 + chunks) * lay.k
            if used < lay.f_half:
                out_ref[side(1), :, used:, :] = jnp.zeros((n, lay.f_half - used, width), BF)
            outlet.flush(out_ref, outs, sems)

    whole = pl.BlockSpec((length, width), lambda q: (0, 0))
    column = pl.BlockSpec((length, width), lambda q: (0, q))
    arrays = [k[0] for k in saved] + [k[3] for k in saved]
    arrays += [k[1] for k in saved] + [k[2] for k in saved]
    arrays += [v.reshape(length, width) for v in mine] + list(received) + [k[4] for k in saved]
    arrays += [trend_low, out_grad]
    ff = chunks * width
    square = pltpu.VMEM((groups, length, width), BF)
    return pl.pallas_call(
        kernel,
        grid=(chunks,),
        out_shape=outlet.shapes(),
        in_specs=[smem_spec(), smem_spec()]
        + [whole] * (2 * groups)
        + [column] * (2 * groups)
        + [any_spec()] * (3 * groups + 2),
        out_specs=[any_spec()] * made,
        scratch_shapes=outlet.scratch()
        + [square] * 5
        + [pltpu.SemaphoreType.DMA((3 * groups + 2,))],
        compiler_params=pltpu.CompilerParams(vmem_limit_bytes=60 * MIB),
        cost_estimate=cost(
            2 * groups * length * width * (2 * width + 2 * ff + width), 45 * MIB
        ),
        name="dense_weights",
    )(where, places, *arrays)


def exchange(axis, size, step):
    return lambda v: lax.ppermute(v, axis, [(i, i ^ step) for i in range(size)])


def on_device(
    n,
    series_in,
    block_kinds,
    out_grad,
    fine_shrink,
    coarse_shrink,
    fine_isometric,
    coarse_isometric,
    fine_grow,
    coarse_grow,
    merge_weight,
    expand_weight,
    contract_weight,
    trend_weight,
    branch_gain,
    middle_gain,
    output_gain,
):
    ring = Ring(n)
    member = lax.axis_index("group")
    core, y = member % 2, member // 2
    block_count = block_kinds.shape[0]
    width = series_in.shape[1]
    block_len = series_in.shape[0] // block_count
    groups = block_count // GROUP
    lay = Layout(n, width, block_len, expand_weight.shape[1])
    length = lay.length
    share = branch_gain.shape[0]
    fine = y == 0

    def right(v):
        return lax.ppermute(v, "dp", ring.right)

    def left(v):
        return lax.ppermute(v, "dp", ring.left)

    shards = (fine_shrink, coarse_shrink, fine_isometric, coarse_isometric)
    shards += (fine_grow, coarse_grow)
    dense_shards = (contract_weight, merge_weight, trend_weight, expand_weight)
    member_ids = jnp.stack([y, core]).astype(jnp.int32)
    own = half_of(lay, member_ids, False, *shards, dense_shards)
    offsets = [0]
    pieces = Pieces()
    for k in range(1, n // 2):
        offsets += [-k, k]
    offsets.append(n // 2)

    def source(offset):
        return offsets.index(offset if abs(offset) < n // 2 else n // 2)

    where = jnp.stack([y, core] + [ring.index(o) for o in offsets]).astype(jnp.int32)

    x_own = series_in.reshape(groups, length, width)
    x_other = []
    last = n // 2

    def prepare_own(kinds, x):
        rows = jnp.arange(length, dtype=jnp.int32)
        npos = jnp.where(fine, lay.npos[0], lay.npos[1])
        stride = jnp.where(fine, STRIDES[0], STRIDES[1])
        step = ((rows % npos) * stride + rows // npos)[:, None]
        return (step, *season_kernel(lay, kinds, step, x, True))

    def prepare_other(step, kinds, *xs):
        kinds = kinds.astype(jnp.int32)
        return (kinds, *season_kernel(lay, kinds, step, jnp.stack(xs), False))

    def spread_gains(*parts):
        parts = jnp.stack(parts).astype(F32)
        return lax.dynamic_update_slice(
            jnp.zeros((3, width), F32), parts, (jnp.int32(0), ring.me * share)
        )

    doublings = []
    size = 1
    while size < n:
        doublings.append(size)
        size *= 2
    gains = spread_gains(branch_gain, middle_gain, output_gain)
    hops = [exchange("dp", n, d) for d in doublings]

    def hop(sends):
        if hops:
            sends["gain"] = (gains, hops.pop(0))

    whole_r = whole_l = own
    half_rows = (lay.g_half + lay.f_half) // 2
    si_rows = lay.si_half // 2
    for t in range(1, last):
        sends = {"r": (whole_r, right), "l": (whole_l, left)}
        if t > 1:
            sends["cr"], sends["cl"] = (whole_r, swap_core), (whole_l, swap_core)
        if t <= groups:
            sends["x"] = (x_own[t - 1], swap_y)
        work, given = None, ()
        if t == 1:
            sends["k"] = (block_kinds.astype(F32), swap_y)
            hop(sends)
            work = lambda *v: (half_of(lay, member_ids, True, *v[:6], v[6:]),)
            given = (*shards, *dense_shards)
        elif t == 2:
            work, given = prepare_own, (block_kinds, x_own)
        arrived, done = slot(sends, work, given)
        if t == 1:
            kinds_other = arrived["k"]
            pieces.add(0, 0, 0, own)
            pieces.add(0, 1, 0, done[0])
        elif t == 2:
            step, season_own, low_own, own_counts, trend_low, order = done
        if "x" in arrived:
            x_other.append(arrived["x"])
        if "gain" in arrived:
            gains = gains + arrived["gain"]
        if t > 1:
            pieces.add(source(1 - t), 1, 0, arrived["cr"])
            pieces.add(source(t - 1), 1, 0, arrived["cl"])
        whole_r, whole_l = arrived["r"], arrived["l"]
        pieces.add(source(-t), 0, 0, whole_r)
        pieces.add(source(t), 0, 0, whole_l)
    middle = lay.si_half
    sends = {"r": (whole_r[:si_rows], right), "l": (whole_l[si_rows:middle], left)}
    sends["cr"], sends["cl"] = (whole_r, swap_core), (whole_l, swap_core)
    hop(sends)
    arrived, done = slot(sends, prepare_other, (step, kinds_other, *x_other))
    kinds_other, season_other, low_other = done
    if "gain" in arrived:
        gains = gains + arrived["gain"]
    pieces.add(source(1 - last), 1, 0, arrived["cr"])
    pieces.add(source(last - 1), 1, 0, arrived["cl"])
    si_r, si_l = arrived["r"], arrived["l"]
    pieces.add(source(last), 0, 0, si_r)
    pieces.add(source(last), 0, si_rows, si_l)
    sends = {"cr": (si_r, swap_core), "cl": (si_l, swap_core)}
    hop(sends)
    arrived, _ = slot(sends)
    if "gain" in arrived:
        gains = gains + arrived["gain"]
    pieces.add(source(last), 1, 0, arrived["cr"])
    pieces.add(source(last), 1, si_rows, arrived["cl"])
    for move_gains in hops:
        gains = gains + move_gains(gains)
    gain_b, gain_m, gain_o = gains[0:1], gains[1:2], gains[2:3]

    def run_shrink(low_own, low_other, *arrays):
        pieces.arrays = list(arrays)
        return shrink_forward(
            lay, where, pieces, low_own, low_other, block_kinds, kinds_other, gain_b
        )

    cut_at = middle + half_rows
    sends = {"r": (whole_r[middle:cut_at], right), "l": (whole_l[cut_at:], left)}
    arrived, done = slot(sends, run_shrink, (low_own, low_other, *pieces.arrays))
    shrunk, iso, mixed, age, si_whole = done
    gf_r, gf_l = arrived["r"], arrived["l"]
    pieces.add(source(last), 0, middle, gf_r)
    pieces.add(source(last), 0, cut_at, gf_l)
    arrived, _ = slot({"cr": (gf_r, swap_core), "cl": (gf_l, swap_core)})
    pieces.add(source(last), 1, middle, arrived["cr"])
    pieces.add(source(last), 1, cut_at, arrived["cl"])
    gf = pieces

    *branch_other, up_other, g_whole = grow_forward(
        lay, where, gf, 1, mixed, season_other, order, gain_b
    )
    branch_other = [v.reshape(length, width) for v in branch_other]
    grads_in = out_grad.reshape(groups, length, width)

    def grow_own(mixed, g_whole, season_own, *arrays):
        gf.arrays = list(arrays)
        made = grow_forward(lay, where, g_whole, 0, mixed, season_own, order, gain_b)
        return (*made, *dense_whole(lay, where, gf))

    arrived, done = slot(
        {"b": (branch_other[0], swap_y)}, grow_own, (mixed, g_whole, season_own, *gf.arrays)
    )
    branch_own = [v.reshape(length, width) for v in done[:groups]]
    up_own, wholes = done[groups], done[groups + 1 :]
    received = [arrived["b"]]
    outs, back_own, back_got, waiting, trend_back, saved, dense_gains = [], [], [], [], [], [], None
    for g in range(groups):
        sends = {}
        if g + 1 < groups:
            sends["b"] = (branch_other[g + 1], swap_y)
        elif waiting:
            sends["j"] = (waiting.pop(0), swap_y)

        def run_dense(mine, got, *wholes, g=g):
            tile = jnp.full((1,), g, jnp.int32)
            return dense(
                lay, where, tile, wholes, mine, got, trend_low, grads_in, gain_m, gain_o
            )

        arrived, made = slot(sends, run_dense, (branch_own[g], received[g], *wholes))
        if "b" in arrived:
            received.append(arrived["b"])
        if "j" in arrived:
            back_got.append(arrived["j"])
        outs.append(made[0])
        back_own.append(made[1])
        waiting.append(made[2])
        trend_back.append(made[3])
        saved.append(made[4:9])
        dense_gains = made[9] if dense_gains is None else dense_gains + made[9]
    series_out = jnp.concatenate(outs)

    ring_order = [n // 2]
    for k in range(n // 2 - 1, 0, -1):
        ring_order += [k, -k]
    ring_order.append(0)
    spot = jnp.zeros((n,), jnp.int32)
    for place, offset in enumerate(ring_order):
        spot = jnp.where(jnp.arange(n) == ring.index(offset), place, spot)

    f_outlet = Outlet(n, lay.f_half, width, None)
    g_outlet = Outlet(n, lay.g_half, width, None)
    s_outlet = Outlet(n, lay.si_half + 16, width, None)

    def run_dense_weights(*arrays):
        mine, got, flat = arrays[:groups], arrays[groups : 2 * groups], arrays[2 * groups :]
        kept = [flat[5 * g : 5 * g + 5] for g in range(groups)]
        return dense_weights(
            lay, where, spot, mine, list(got), trend_low, grads_in, kept, f_outlet
        )

    arrived, (f_keep, f_give) = slot(
        {"j": (waiting.pop(0), swap_y)},
        run_dense_weights,
        (*branch_own, *received, *[v for k in saved for v in k]),
    )
    back_got.append(arrived["j"])

    class Chain:
        def __init__(self, keep):
            self.keep = keep
            self.got = []
            self.step = last
            self.r = self.l = None
            self.half = keep.shape[1] // 2

        def here(self, place):
            first = 0
            for v in self.got:
                if place < first + v.shape[0]:
                    got = v[place - first]
                    break
                first += v.shape[0]
            return self.keep[place].astype(F32) + got.astype(F32)

        def sends(self):
            k = self.step
            if k == last:
                part = self.here(0)
                return part[: self.half].astype(BF), part[self.half :].astype(BF)
            place = 1 + 2 * (last - 1 - k)
            a, b = self.here(place), self.here(place + 1)
            if k == last - 1:
                h = self.half
                a = jnp.concatenate([a[:h] + self.r.astype(F32), a[h:]])
                b = jnp.concatenate([b[:h], b[h:] + self.l.astype(F32)])
            else:
                a, b = a + self.r.astype(F32), b + self.l.astype(F32)
            return a.astype(BF), b.astype(BF)

        def total(self):
            return (self.here(n - 1) + self.r.astype(F32) + self.l.astype(F32)).astype(BF)

    def back_of(grads, g_whole, up, season):
        return grow_backward(lay, where, g_whole, grads, up, season, order, gain_b)

    arrived, done = slot(
        {"j": (waiting.pop(0), swap_y), "f": (f_give, swap_core)},
        lambda g_whole, up, season, *grads: back_of(grads, g_whole, up, season),
        (g_whole, up_own, season_own, *back_own),
    )
    back_got.append(arrived["j"])
    pre_own, mixed_back_own, sum_own, gains_own = done
    f = Chain(f_keep)
    f.got = [arrived["f"]]
    chains = {"f": f}
    starts = {"g": 3, "s": 5}
    kept = {}
    finals = {}
    t = 0
    while True:
        active = {k: c for k, c in chains.items() if c.step > 0}
        finishing = [k for k, c in chains.items() if c.step == 0 and k + "mine" not in finals]
        if not active and not finishing and "smine" in finals:
            break
        sends, work, given = {}, None, ()
        for name, chain in active.items():
            a, b = chain.sends()
            sends[name + "r"], sends[name + "l"] = (a, right), (b, left)
        for name in finishing:
            mine = chains[name].total()
            finals[name + "mine"] = mine
            sends[name + "y"] = (mine, swap_y)
            if name != "f":
                sends[name + "c"] = (mine, swap_core)
        for name in ("f", "g"):
            ready = name + "late" in finals and (t > 6 or name == "g")
            if ready and name + "sent" not in finals:
                sends[name + "d"] = (finals[name + "late"], swap_core)
                finals[name + "sent"] = True
        if t == 0:
            work = lambda g_whole, up, season, *grads: back_of(grads, g_whole, up, season)
            given = (g_whole, up_other, season_other, *back_got)
        elif t == 1:
            work = lambda *v: grow_weight(lay, where, spot, *v, g_outlet)
            given = (mixed, pre_own, pre_other)
        elif t == 2:
            work = lambda *v: shrink_backward(lay, where, *v, age, gain_b)
            given = (si_whole, mixed_back_own, mixed_back_other, shrunk, iso)
            sends["g"] = (g_give, swap_core)
        elif t == 3:
            work = lambda *v: shrink_weight(lay, where, spot, *v, age, s_outlet)
            given = (iso_pre, shrink_pre, shrunk, low_own, low_other, grad_gains)
        elif t == 4:
            work = lambda *v: season_backward(lay, where, *v, order)
            given = (si_whole, shrink_pre, sum_own, sum_other)
            sends["s0"] = (s_give, swap_core)
        if t in (5, 6, 8) and tail_sends:
            for i in range(len(tail_sends) if t == 8 else 1):
                sends["x%d" % i] = (tail_sends.pop(0), swap_y)
        if "s" in finishing:
            work, given = finish, (season_mine, own_counts, *trend_back, *tail)
        arrived, done = slot(sends, work, given)
        if t == 0:
            pre_other, mixed_back_other, sum_other, gains_other = done
        elif t == 1:
            g_keep, g_give = done
            chains["g"] = None
        elif t == 2:
            shrink_pre, iso_pre, gains_si = done
            chains["g"] = Chain(g_keep)
            chains["g"].got = [arrived["g"]]
            grad_gains = jnp.concatenate(
                [gains_own + gains_other + gains_si, dense_gains, jnp.zeros((13, width), F32)]
            )
        elif t == 3:
            s_keep, s_give = done
        elif t == 4:
            season_mine, *tail_sends = done
            tail = []
            chains["s"] = Chain(s_keep)
            chains["s"].got = [arrived["s0"]]

            def finish(season_mine, own_counts, *rest):
                backs, tail = rest[:groups], rest[groups:]
                total = season_mine.astype(F32) + jnp.stack(tail).astype(F32)
                rest = jnp.stack(backs) - total
                spread = (rest * (1.0 / WINDOW)).astype(BF)
                averaged = jnp.einsum(
                    "gij,gid->gjd", own_counts, spread, preferred_element_type=F32
                )
                return ((total + averaged).astype(BF),)

        for i in range(groups):
            if "x%d" % i in arrived:
                tail.append(arrived["x%d" % i])
        for name, chain in active.items():
            chain.r, chain.l = arrived[name + "r"], arrived[name + "l"]
            chain.step -= 1
        for name in ("f", "g"):
            if name + "d" in arrived:
                finals[name + "d"] = arrived[name + "d"]
        for name in finishing:
            finals[name + "y"] = arrived[name + "y"]
            if name != "f":
                finals[name + "c"] = arrived[name + "c"]
            if name == "f":
                mine = finals["fmine"].astype(F32) + arrived["fy"].astype(F32)
                finals["flate"] = mine.astype(BF)
            elif name == "g":
                finals["glate"] = arrived["gy"]
            else:
                (series_grad,) = done
        if chains.get("g", 0) is None:
            del chains["g"]
        t += 1
    s_mine, s_y = finals["smine"], finals["sy"]
    s_core = (finals["sc"], swap_core(s_y))
    f_half, f_other = finals["flate"], finals["fd"]
    g_mine, g_y = finals["gmine"], finals["gy"]
    g_core = (finals["gc"], finals["gd"])

    def both(mine, other):
        return jnp.where(core == 0, mine, other), jnp.where(core == 0, other, mine)

    def branches(mine, over_y):
        return jnp.where(fine, mine, over_y), jnp.where(fine, over_y, mine)

    s_fine, s_coarse = branches(s_mine, s_y)
    t_fine, t_coarse = branches(*s_core)
    g_fine, g_coarse = branches(g_mine, g_y)
    h_fine, h_coarse = branches(*g_core)

    def si_out(b, mine, other):
        lo, hi = both(mine, other)
        (f0, r0, _, _), (f1, r1, _, _) = lay.si_parts(b)
        shrink = jnp.concatenate([lo[f0 : f0 + r0], hi[f0 : f0 + r0]])
        return shrink.astype(F32), jnp.concatenate([lo[f1 : f1 + r1], hi[f1 : f1 + r1]]).astype(F32)

    def g_out(b, mine, other):
        lo, hi = both(mine, other)
        cols = [v[r : r + k] for v in (lo, hi) for r, k, _ in lay.g_parts(b)]
        return jnp.concatenate(cols, axis=1).astype(F32)

    fine_shrink_grad, fine_iso_grad = si_out(0, s_fine, t_fine)
    coarse_shrink_grad, coarse_iso_grad = si_out(1, s_coarse, t_coarse)
    fine_grow_grad, coarse_grow_grad = g_out(0, g_fine, h_fine), g_out(1, g_coarse, h_coarse)
    lo, hi = both(f_half, f_other)
    (a0, a1, _, _), (b0, b1, _, _) = lay.f_parts(0)
    z = lay.g_half
    contract_grad = lo[a0 - z : a0 - z + a1].astype(F32)
    merge_grad = lo[b0 - z : b0 - z + b1].astype(F32)
    rest = [hi[a - z : a - z + rows].astype(F32) for a, rows, _, _ in lay.f_parts(1)]
    trend_grad, expand_grad = rest[0], jnp.concatenate(rest[1:], axis=1)

    at = lay.si_half
    gain_grads = s_mine[at : at + 3].astype(F32) + s_y[at : at + 3].astype(F32)
    gain_grads = lax.dynamic_slice(gain_grads, (jnp.int32(0), ring.me * share), (3, share))
    return (
        series_out,
        series_grad.reshape(series_in.shape),
        fine_shrink_grad,
        coarse_shrink_grad,
        fine_iso_grad,
        coarse_iso_grad,
        fine_grow_grad,
        coarse_grow_grad,
        merge_grad,
        expand_grad,
        contract_grad,
        trend_grad,
        gain_grads[0],
        gain_grads[1],
        gain_grads[2],
    )


def solution(mesh):
    n = mesh.shape["dp"]
    rows = P(("dp", "group"), None)
    weight = P("dp", None)
    return jax.shard_map(
        lambda *args: on_device(n, *args),
        mesh=mesh,
        in_specs=(rows, P(("dp", "group")), rows) + (weight,) * 10 + (P("dp"),) * 3,
        out_specs=(rows, rows) + (weight,) * 10 + (P("dp"),) * 3,
        check_vma=False,
    )
```

```python
import functools
import math

import jax
import jax.numpy as jnp
from jax import lax
from jax.experimental import pallas as pl
from jax.experimental.pallas import tpu as pltpu
from jax.sharding import PartitionSpec as P

STRIDES = (12, 16)
WINDOW = 25
HALF = WINDOW // 2
GROUP = 4
BF = jnp.bfloat16
F32 = jnp.float32
MIB = 1024 * 1024
VMEM = 127 * MIB // 2
CORE_SWAP = ((0, 1), (1, 0), (2, 3), (3, 2))
Y_SWAP = ((0, 2), (2, 0), (1, 3), (3, 1))


class Layout:
    def __init__(self, n, width, block_len, ff):
        self.n, self.width, self.block_len = n, width, block_len
        self.length = GROUP * block_len
        self.taps = tuple(block_len // s for s in STRIDES)
        self.shrink = tuple(s * width for s in STRIDES)
        self.iso = tuple(p * width for p in self.taps)
        self.si_half = (self.shrink[0] + self.iso[0]) // (2 * n)
        self.k = width // n
        self.g_half = max(STRIDES) // 2 * self.k
        self.chunks = ff // width
        self.merge, self.contract = 2 * width // n, ff // n
        self.f_half = max(self.contract + self.merge, self.k * (1 + self.chunks))
        self.npos = tuple(GROUP * p for p in self.taps)

    def si_parts(self, b):
        s, i = self.shrink[b] // self.n, self.iso[b] // self.n
        return [(0, s // 2, 0, s), (s // 2, i // 2, self.shrink[b], i)]

    def g_parts(self, b):
        return [(j * self.k, self.k, j) for j in range(STRIDES[b] // 2)]

    def f_parts(self, h):
        base = self.g_half
        if h == 0:
            return [
                (base, self.contract, "contract", 0),
                (base + self.contract, self.merge, "merge", 0),
            ]
        found = [(base, self.k, "trend", 0)]
        for j in range(self.chunks):
            found.append((base + (1 + j) * self.k, self.k, "expand", j))
        return found


def held(*values):
    return lax.optimization_barrier(values)


class Ring:
    def __init__(self, n):
        self.n = n
        order = list(range(0, n, 2)) + list(range(n - 1, 0, -2))
        self.right = [(order[k], order[(k + 1) % n]) for k in range(n)]
        self.left = [(b, a) for a, b in self.right]
        d = lax.axis_index("dp")
        self.me = d
        self.pos = jnp.where(d % 2 == 0, d // 2, n - 1 - d // 2)

    def index(self, offset):
        if offset == 0:
            return self.me
        r = (self.pos + offset) % self.n
        return jnp.where(r < self.n // 2, 2 * r, 2 * (self.n - 1 - r) + 1)


def slot(sends, work=None, given=()):
    names = list(sends)
    tied = held(*[sends[k][0] for k in names], *given)
    moved = [sends[k][1](v) for k, v in zip(names, tied)]
    done = tuple(work(*tied[len(names) :])) if work is not None else ()
    out = held(*moved, *done)
    return dict(zip(names, out[: len(names)])), out[len(names) :]


def swap_core(v):
    return lax.ppermute(v, "group", CORE_SWAP)


def swap_y(v):
    return lax.ppermute(v, "group", Y_SWAP)


def dot(a, b):
    return jnp.dot(a, b, preferred_element_type=F32)


def dot_t(a, b):
    return lax.dot_general(a, b, (((1,), (1,)), ((), ())), preferred_element_type=F32)


def dot_w(a, b):
    return lax.dot_general(a, b, (((0,), (0,)), ((), ())), preferred_element_type=F32)


def normal(v):
    center = jnp.mean(v, axis=-1, keepdims=True)
    centered = v - center
    inverse = lax.rsqrt(jnp.mean(centered * centered, axis=-1, keepdims=True) + 1e-05)
    return centered * inverse, inverse


def normal_back(grad, hat, inverse, gain):
    g = grad * gain
    a = jnp.mean(g, axis=-1, keepdims=True)
    b = jnp.mean(g * hat, axis=-1, keepdims=True)
    return inverse * (g - a - hat * b)


def erf_pair(h):
    d = 1.0 + (0.3275911 / math.sqrt(2.0)) * jnp.abs(h)
    t = pl.reciprocal(d, approx=True)
    t = t * (2.0 - d * t)
    e = jnp.exp(-0.5 * (h * h))
    p = 0.5 * -1.453152027 + t * (0.5 * 1.061405429)
    p = 0.5 * 1.421413741 + t * p
    p = 0.5 * -0.284496736 + t * p
    q = (0.5 * 0.254829592 + t * p) * (t * e)
    return jnp.where(h >= 0, 1.0 - q, q), (h * e) * (1.0 / math.sqrt(2.0 * math.pi))


def over(parts, first, rows):
    for part in parts:
        lo, hi = max(first, part[0]), min(first + rows, part[0] + part[1])
        if lo < hi:
            yield lo - first, hi - lo, lo - part[0], part


def start_copy(piece, row, rows, whole, at, sem):
    at = at if isinstance(at, int) else pl.multiple_of(at, 16)
    pltpu.make_async_copy(
        piece.at[pl.ds(row, rows)], whole.at[pl.ds(at, rows)], sem
    ).start()


def wait_rows(whole, first, rows, sem):
    view = whole.at[pl.ds(first, rows)]
    pltpu.make_async_copy(view, view, sem).wait()


class Pieces:
    def __init__(self):
        self.meta, self.arrays = [], []

    def add(self, source, other, first, array):
        self.meta.append((source, other, first, array.shape[0]))
        self.arrays.append(array)


def load_si(lay, b, where, meta, refs, whole, sems):
    core = where[1]
    for (source, other, first, rows), ref in zip(meta, refs):
        src = where[2 + source]
        h = 1 - core if other else core
        for row, count, inside, part in over(lay.si_parts(b), first, rows):
            _, half, base, shard = part
            at = base + src * shard + h * half + inside
            start_copy(ref, row, count, whole, at, sems.at[0 if base == 0 else 1])


def load_g(lay, b, where, meta, refs, whole, sem):
    core = where[1]
    for (source, other, first, rows), ref in zip(meta, refs):
        src = where[2 + source]
        h = 1 - core if other else core
        for row, count, inside, part in over(lay.g_parts(b), first - lay.si_half, rows):
            at = (h * (STRIDES[b] // 2) + part[2]) * lay.width + src * lay.k + inside
            start_copy(ref, row, count, whole, at, sem)


def load_f(lay, c, where, meta, refs, wholes, sems):
    names = ("merge", "contract", "trend", "expand")
    width = lay.width
    for (source, other, first, rows), ref in zip(meta, refs):
        src = where[2 + source]
        h = 1 - c if other else c
        for row, count, inside, part in over(lay.f_parts(h), first - lay.si_half, rows):
            t = names.index(part[2])
            at = pl.multiple_of(src * part[1] + inside, 16)
            target = wholes[t].at[pl.ds(at, count), pl.ds(part[3] * width, width)]
            pltpu.make_async_copy(ref.at[pl.ds(row, count)], target, sems.at[t]).start()


def any_spec():
    return pl.BlockSpec(memory_space=pl.ANY)


def vmem_spec():
    return pl.BlockSpec(memory_space=pltpu.VMEM)


def smem_spec():
    return pl.BlockSpec(memory_space=pltpu.SMEM)


def cost(flops, moved):
    return pl.CostEstimate(flops=int(flops), bytes_accessed=int(moved), transcendentals=0)


def by_branch(where, body):
    for b in range(2):
        pl.when(where[0] == b)(functools.partial(body, b))


def half_of(lay, where, sibling, fs, cs, fi, ci, fg, cg, weights):
    width, k = lay.width, lay.k
    base = lay.si_half
    rows = base + lay.g_half + lay.f_half

    def kernel(where, fs, cs, fi, ci, fg, cg, contract, merge, trend, expand, out, sems):
        def moves(b, h):
            found = []
            for i, (first, half, _, _) in enumerate(lay.si_parts(b)):
                source = ((fs, fi), (cs, ci))[b][i]
                found.append((source.at[pl.ds(h * half, half)], out.at[pl.ds(first, half)]))
            for first, count, j in lay.g_parts(b):
                col = (h * (STRIDES[b] // 2) + j) * width
                source = (fg, cg)[b].at[:, pl.ds(col, width)]
                found.append((source, out.at[pl.ds(base + first, count)]))
            named = {"contract": contract, "merge": merge, "trend": trend}
            for first, count, name, j in lay.f_parts(h):
                source = expand.at[:, pl.ds(j * width, width)] if name == "expand" else named[name]
                found.append((source, out.at[pl.ds(base + first, count)]))
            return [(x, y, sems.at[i]) for i, (x, y) in enumerate(found)]

        for b in range(2):
            for h in range(2):

                @pl.when((where[0] == b) & (where[1] == (1 - h if sibling else h)))
                def _(b=b, h=h):
                    used = lay.g_parts(b)[-1][0] + k
                    if used < lay.g_half:
                        out[base + used : base + lay.g_half, :] = jnp.zeros(
                            (lay.g_half - used, width), BF
                        )
                    used = lay.f_parts(h)[-1][0] + lay.f_parts(h)[-1][1]
                    if used < lay.g_half + lay.f_half:
                        out[base + used :, :] = jnp.zeros((rows - base - used, width), BF)
                    for x, y, sem in moves(b, h):
                        pltpu.make_async_copy(x, y, sem).start()
                    for x, y, sem in moves(b, h):
                        pltpu.make_async_copy(x, y, sem).wait()

    return pl.pallas_call(
        kernel,
        out_shape=jax.ShapeDtypeStruct((rows, width), BF),
        in_specs=[smem_spec()] + [any_spec()] * 10,
        out_specs=vmem_spec(),
        scratch_shapes=[pltpu.SemaphoreType.DMA((8 + max(STRIDES),))],
        compiler_params=pltpu.CompilerParams(vmem_limit_bytes=VMEM),
        cost_estimate=cost(0, 4 * rows * width),
        name="sibling_half" if sibling else "own_half",
    )(where, fs, cs, fi, ci, fg, cg, *weights)


def bounds_of(kinds, base):
    firsts, lasts = [jnp.int32(0)], [jnp.int32(GROUP - 1)]
    for b in range(1, GROUP):
        firsts.append(jnp.where(kinds[base + b] == 2, firsts[-1], b))
    for b in reversed(range(GROUP - 1)):
        lasts.insert(0, jnp.where(kinds[base + b + 1] == 2, lasts[0], b))
    return firsts, lasts


def counts_of(lay, kinds, base, step):
    firsts, lasts = bounds_of(kinds, base)
    length = lay.length
    first = jnp.zeros_like(step)
    last = jnp.full_like(step, length - 1)
    for b in range(GROUP):
        inside = (step >= b * lay.block_len) & (step < (b + 1) * lay.block_len)
        first = jnp.where(inside, firsts[b] * lay.block_len, first)
        last = jnp.where(inside, lasts[b] * lay.block_len + (lay.block_len - 1), last)
    j = lax.broadcasted_iota(jnp.int32, (length, length), 1)
    low = jnp.maximum(step - HALF, first)
    high = jnp.minimum(step + HALF, last)
    count = jnp.where((j >= low) & (j <= high), 1.0, 0.0)
    before = jnp.maximum(first - step + HALF, 0).astype(F32)
    after = jnp.maximum(step + HALF - last, 0).astype(F32)
    count += jnp.where(j == first, before, 0.0)
    count += jnp.where(j == last, after, 0.0)
    return count.astype(BF)


def season_kernel(lay, kinds, step, x, with_trend):
    width, length = lay.width, lay.length
    groups = x.shape[0]

    def kernel(kinds_ref, step_ref, x_ref, season_ref, low_ref, *refs):
        base = pl.program_id(0) * GROUP
        step = step_ref[...]
        x = x_ref[0]
        j = lax.broadcasted_iota(jnp.int32, (length, length), 1)
        order = jnp.where(j == step, 1.0, 0.0).astype(BF)
        season = dot(order, x) - dot(counts_of(lay, kinds_ref, base, step), x) * (1.0 / WINDOW)
        season_ref[0] = season
        low_ref[0] = season.astype(BF)
        if with_trend:
            counts_ref, trend_ref, order_ref = refs
            order_ref[...] = order
            plain = lax.broadcasted_iota(jnp.int32, (length, 1), 0)
            counts = counts_of(lay, kinds_ref, base, plain)
            counts_ref[0] = counts
            trend_ref[0] = (dot(counts, x) * (1.0 / WINDOW)).astype(BF)

    group = pl.BlockSpec((1, length, width), lambda g: (g, 0, 0))
    square = pl.BlockSpec((1, length, length), lambda g: (g, 0, 0))
    shapes = [
        jax.ShapeDtypeStruct((groups, length, width), F32),
        jax.ShapeDtypeStruct((groups, length, width), BF),
    ]
    specs = [group, group]
    if with_trend:
        shapes += [
            jax.ShapeDtypeStruct((groups, length, length), BF),
            jax.ShapeDtypeStruct((groups, length, width), BF),
            jax.ShapeDtypeStruct((length, length), BF),
        ]
        specs += [square, group, pl.BlockSpec((length, length), lambda g: (0, 0))]
    return pl.pallas_call(
        kernel,
        grid=(groups,),
        out_shape=shapes,
        in_specs=[smem_spec(), pl.BlockSpec((length, 1), lambda g: (0, 0)), group],
        out_specs=specs,
        compiler_params=pltpu.CompilerParams(vmem_limit_bytes=VMEM),
        cost_estimate=cost(6 * groups * length * length * width, 12 * groups * length * width),
        name="season_trend" if with_trend else "season",
    )(kinds, step, x)


def tap_rows(x, age, k):
    if k == 0:
        return x
    return jnp.where(age >= k, pltpu.roll(x, k, 0), 0.0)


def step_rows(own, other, s, npos):
    cut = slice(s * npos, (s + 1) * npos)
    x = jnp.concatenate([own[:, cut, :], other[:, cut, :]], axis=0)
    return x.reshape(x.shape[0] * npos, x.shape[2])


def filled(x, rows):
    if x.shape[0] == rows:
        return x
    return jnp.concatenate([x, jnp.zeros((rows - x.shape[0], x.shape[1]), x.dtype)], axis=0)


def shrink_forward(lay, where, si, low_own, low_other, kinds_own, kinds_other, gain):
    n, width = lay.n, lay.width
    groups = 2 * low_own.shape[0]
    most = groups * max(lay.npos)
    count = len(si.arrays)
    total = lay.shrink[0] + lay.iso[0]

    def kernel(where, kinds_own, kinds_other, gain_ref, own_ref, other_ref, *refs):
        pieces, rest = refs[:count], refs[count:]
        shrunk_ref, iso_ref, mixed_ref, age_ref, taps_out, whole_out, whole, taps_ref, sems = rest

        def body(b):
            load_si(lay, b, where, si.meta, pieces, whole, sems)
            npos = lay.npos[b]
            m = groups * npos
            wait_rows(whole, 0, lay.shrink[b], sems.at[0])
            z = jnp.zeros((m, width), F32)
            for s in range(STRIDES[b]):
                z += dot(step_rows(own_ref, other_ref, s, npos), whole[s * width : (s + 1) * width])
            shrunk = jnp.tanh(z)
            shrunk_ref[:m] = shrunk
            low = shrunk.astype(BF).astype(F32)
            wait_rows(whole, lay.shrink[b], lay.iso[b], sems.at[1])
            pltpu.make_async_copy(whole, whole_out, sems.at[2]).start()
            taps = lay.taps[b]
            base = lay.shrink[b]
            row = lax.broadcasted_iota(jnp.int32, (m, 1), 0)
            age = jnp.zeros_like(row)
            for g in range(groups):
                own = g < groups // 2
                kinds = kinds_own if own else kinds_other
                firsts, _ = bounds_of(kinds, (g if own else g - groups // 2) * GROUP)
                for i in range(GROUP):
                    lo = g * npos + i * taps
                    inside = (row >= lo) & (row < lo + taps)
                    age = jnp.where(inside, row - lo + (i - firsts[i]) * taps, age)
            age_ref[:m] = age
            e = jnp.zeros((m, width), F32)
            for k in range(taps):
                at = base + (taps - 1 - k) * width
                x = tap_rows(low, age, k).astype(BF)
                taps_ref[k, :m, :] = x
                if m < most:
                    taps_ref[k, m:, :] = jnp.zeros((most - m, width), BF)
                e += dot(x, whole[at : at + width])
            keep = pltpu.make_async_copy(taps_ref, taps_out, sems.at[3])
            keep.start()
            iso = jnp.tanh(e)
            iso_ref[:m] = iso
            hat, _ = normal(iso + shrunk)
            mixed_ref[:m] = (hat * gain_ref[...]).astype(BF)
            pltpu.make_async_copy(whole, whole_out, sems.at[2]).wait()
            keep.wait()

        by_branch(where, body)

    return pl.pallas_call(
        kernel,
        out_shape=[
            jax.ShapeDtypeStruct((most, width), F32),
            jax.ShapeDtypeStruct((most, width), F32),
            jax.ShapeDtypeStruct((most, width), BF),
            jax.ShapeDtypeStruct((most, 1), jnp.int32),
            jax.ShapeDtypeStruct((max(lay.taps), most, width), BF),
            jax.ShapeDtypeStruct((total, width), BF),
        ],
        in_specs=[smem_spec()] * 3 + [vmem_spec()] * 3 + [any_spec()] * count,
        out_specs=[vmem_spec()] * 4 + [any_spec()] * 2,
        scratch_shapes=[
            pltpu.VMEM((total, width), BF),
            pltpu.VMEM((max(lay.taps), most, width), BF),
            pltpu.SemaphoreType.DMA((4,)),
        ],
        compiler_params=pltpu.CompilerParams(vmem_limit_bytes=VMEM),
        cost_estimate=cost(2 * most * width * total, 4 * total * width),
        name="shrink_forward",
    )(where, kinds_own, kinds_other, gain, low_own, low_other, *si.arrays)


def stage(lay, b, copies):
    def view(ref, first, rows, middle):
        return ref.at[:, pl.ds(first, rows), :] if middle else ref.at[pl.ds(first, rows)]

    def run(i):
        for source, target, rows, sems, middle in copies:
            yield pltpu.make_async_copy(
                view(source, i * 4 * rows, 4 * rows, middle),
                view(target, i * 4 * rows, 4 * rows, middle),
                sems.at[i],
            )

    def start(i):
        for c in run(i):
            c.start()

    def wait(i):
        for c in run(i):
            c.wait()

    return start, wait


def grow_forward(lay, where, gf, part, mixed, season, order, gain):
    width = lay.width
    groups = season.shape[0]
    length = lay.length
    pieces_in = isinstance(gf, Pieces)
    arrays = gf.arrays if pieces_in else [gf]
    count = len(arrays)
    most = max(STRIDES) * width
    runs = max(STRIDES) // 4

    def kernel(where, gain_ref, order_ref, mixed_ref, season_in, *refs):
        pieces, rest = refs[:count], refs[count:]
        outs, up_out = rest[:groups], rest[groups]
        scratch = rest[groups + 1 + pieces_in :]
        rows_ref, whole, season_ref, up_ref, in_sems, w_sems, up_sems, sems = scratch

        def body(b):
            npos = lay.npos[b]
            m = groups * npos
            copies = [(season_in, season_ref, npos, in_sems, True)]
            if not pieces_in:
                copies.append((pieces[0], whole, width, w_sems, False))
            start, wait = stage(lay, b, copies)
            up_start, up_wait = stage(lay, b, [(up_ref, up_out, npos, up_sems, True)])
            if pieces_in:
                load_g(lay, b, where, gf.meta, pieces, whole, sems.at[0])
            for i in range(STRIDES[b] // 4):
                start(i)
            if pieces_in:
                wait_rows(whole, 0, STRIDES[b] * width, sems.at[0])
                pltpu.make_async_copy(whole, rest[groups + 1], sems.at[1]).start()
            x = mixed_ref[part * m : (part + 1) * m]
            gain = gain_ref[...]
            for s in range(STRIDES[b]):
                if s % 4 == 0:
                    wait(s // 4)
                cut = slice(s * npos, (s + 1) * npos)
                up = jnp.tanh(dot(x, whole[s * width : (s + 1) * width]))
                up_ref[:, cut, :] = up.reshape(groups, npos, width)
                hat, _ = normal(up + season_ref[:, cut, :].reshape(m, width))
                rows_ref[:, cut, :] = (hat * gain).astype(BF).reshape(groups, npos, width)
                if s % 4 == 3:
                    up_start(s // 4)
            for g in range(groups):
                outs[g][0] = dot_w(order_ref[...], rows_ref[g]).astype(BF)
            for i in range(STRIDES[b] // 4):
                up_wait(i)
            if pieces_in:
                pltpu.make_async_copy(whole, rest[groups + 1], sems.at[1]).wait()

        by_branch(where, body)

    shapes = [jax.ShapeDtypeStruct((1, length, width), BF)] * groups
    shapes.append(jax.ShapeDtypeStruct((groups, length, width), F32))
    if pieces_in:
        shapes.append(jax.ShapeDtypeStruct((most, width), BF))
    return pl.pallas_call(
        kernel,
        out_shape=shapes,
        in_specs=[smem_spec()] + [vmem_spec()] * 3 + [any_spec()] * (1 + count),
        out_specs=[vmem_spec()] * groups + [any_spec()] * (1 + pieces_in),
        scratch_shapes=[
            pltpu.VMEM((groups, length, width), BF),
            pltpu.VMEM((most, width), BF),
            pltpu.VMEM((groups, length, width), F32),
            pltpu.VMEM((groups, length, width), F32),
        ]
        + [pltpu.SemaphoreType.DMA((runs,))] * 3
        + [pltpu.SemaphoreType.DMA((2,))],
        compiler_params=pltpu.CompilerParams(vmem_limit_bytes=VMEM),
        cost_estimate=cost(
            2 * groups * length * width * (width + length),
            2 * most * width + 14 * groups * length * width,
        ),
        name="grow_forward",
    )(where, gain, order, mixed, season, *arrays)


def grow_backward(lay, where, whole, grads, up, season, order, gain):
    width = lay.width
    groups = season.shape[0]
    length = lay.length
    most = groups * max(lay.npos)
    runs = max(STRIDES) // 4

    def kernel(where, gain_ref, order_ref, up_in, season_in, whole_in, *refs):
        grad_refs, rest = refs[:groups], refs[groups:]
        pre_ref, back_ref, sum_out, gain_grad_ref = rest[:4]
        rows_ref, whole, up_ref, season_ref, sum_ref = rest[4:9]
        sems, sum_sems = rest[9:12], rest[12]

        def body(b):
            npos = lay.npos[b]
            m = groups * npos
            start, wait = stage(
                lay,
                b,
                [
                    (up_in, up_ref, npos, sems[0], True),
                    (season_in, season_ref, npos, sems[1], True),
                    (whole_in, whole, width, sems[2], False),
                ],
            )
            sum_start, sum_wait = stage(lay, b, [(sum_ref, sum_out, npos, sum_sems, True)])
            for i in range(STRIDES[b] // 4):
                start(i)
            for g in range(groups):
                rows_ref[g] = dot(order_ref[...], grad_refs[g][...]).astype(BF)
            total = jnp.zeros((m, width), F32)
            gains = jnp.zeros((1, width), F32)
            for s in range(STRIDES[b]):
                if s % 4 == 0:
                    wait(s // 4)
                cut = slice(s * npos, (s + 1) * npos)
                up = up_ref[:, cut, :].reshape(m, width)
                hat, inverse = normal(up + season_ref[:, cut, :].reshape(m, width))
                g = rows_ref[:, cut, :].reshape(m, width).astype(F32)
                gains += jnp.sum(g * hat, axis=0, keepdims=True)
                d = normal_back(g, hat, inverse, gain_ref[...])
                sum_ref[:, cut, :] = d.reshape(groups, npos, width)
                pre = (d * (1.0 - up * up)).astype(BF)
                pre_ref[:, cut, :] = pre.reshape(groups, npos, width)
                total += dot_t(pre, whole[s * width : (s + 1) * width])
                if s % 4 == 3:
                    sum_start(s // 4)
            back_ref[:m] = total
            gain_grad_ref[...] = gains
            for i in range(STRIDES[b] // 4):
                sum_wait(i)

        by_branch(where, body)

    return pl.pallas_call(
        kernel,
        out_shape=[
            jax.ShapeDtypeStruct((groups, length, width), BF),
            jax.ShapeDtypeStruct((most, width), F32),
            jax.ShapeDtypeStruct((groups, length, width), F32),
            jax.ShapeDtypeStruct((1, width), F32),
        ],
        in_specs=[smem_spec()] + [vmem_spec()] * 2 + [any_spec()] * 3 + [vmem_spec()] * groups,
        out_specs=[vmem_spec(), vmem_spec(), any_spec(), vmem_spec()],
        scratch_shapes=[
            pltpu.VMEM((groups, length, width), BF),
            pltpu.VMEM((whole.shape[0], width), BF),
            pltpu.VMEM((groups, length, width), F32),
            pltpu.VMEM((groups, length, width), F32),
            pltpu.VMEM((groups, length, width), F32),
        ]
        + [pltpu.SemaphoreType.DMA((runs,))] * 4,
        compiler_params=pltpu.CompilerParams(vmem_limit_bytes=VMEM),
        cost_estimate=cost(
            2 * groups * length * width * (width + length),
            2 * whole.shape[0] * width + 18 * groups * length * width,
        ),
        name="grow_backward",
    )(where, gain, order, up, season, whole, *grads)


class Outlet:
    def __init__(self, n, rows, width, cuts):
        self.n, self.rows, self.width = n, rows, width
        self.bounds = [(0, n)] if cuts is None else cuts

    def shapes(self):
        sizes = [self.n] + [hi - lo for lo, hi in self.bounds]
        return [jax.ShapeDtypeStruct((c, self.rows, self.width), BF) for c in sizes]

    def scratch(self):
        return [
            pltpu.VMEM((2, self.n, self.rows, self.width), BF),
            pltpu.SemaphoreType.DMA((1 + len(self.bounds),)),
        ]

    def copies(self, held_ref, outs, sems):
        found = [pltpu.make_async_copy(held_ref.at[0], outs[0], sems.at[0])]
        for i, (lo, hi) in enumerate(self.bounds):
            source = held_ref.at[1, pl.ds(lo, hi - lo)]
            found.append(pltpu.make_async_copy(source, outs[1 + i], sems.at[1 + i]))
        return found

    def flush(self, held_ref, outs, sems):
        for c in self.copies(held_ref, outs, sems):
            c.start()
        for c in self.copies(held_ref, outs, sems):
            c.wait()


def grow_weight(lay, where, places, mixed, pre_own, pre_other, outlet):
    n, width, k = lay.n, lay.width, lay.k
    groups = pre_own.shape[0]
    made = len(outlet.shapes())

    def kernel(where, places_ref, mixed_ref, own_ref, other_ref, *refs):
        outs, (out_ref, sems) = refs[:made], refs[made:]

        def body(b):
            npos = lay.npos[b]
            most = 2 * groups * max(lay.npos)
            x = filled(mixed_ref[: 2 * groups * npos], most)
            steps = STRIDES[b] // 2
            for s in range(STRIDES[b]):
                d = dot_w(x, filled(step_rows(own_ref, other_ref, s, npos), most)).astype(BF)
                side = jnp.where(where[1] == s // steps, 0, 1)
                at = (s % steps) * k
                for shard in range(n):
                    out_ref[side, places_ref[shard], at : at + k, :] = d[shard * k : (shard + 1) * k]
            rest = lay.g_half - steps * k
            if rest:
                out_ref[:, :, steps * k :, :] = jnp.zeros((2, n, rest, width), BF)

        by_branch(where, body)
        outlet.flush(out_ref, outs, sems)

    return pl.pallas_call(
        kernel,
        out_shape=outlet.shapes(),
        in_specs=[smem_spec(), smem_spec()] + [vmem_spec()] * 3,
        out_specs=[any_spec()] * made,
        scratch_shapes=outlet.scratch(),
        compiler_params=pltpu.CompilerParams(vmem_limit_bytes=VMEM),
        cost_estimate=cost(4 * groups * lay.length * width * width, 2 * 2 * n * lay.g_half * width),
        name="grow_weight",
    )(where, places, mixed, pre_own, pre_other)


def shrink_backward(lay, where, whole, back_own, back_other, shrunk, iso, age, gain):
    width = lay.width
    most = shrunk.shape[0]

    def kernel(where, age_ref, gain_ref, b0, b1, shrunk_ref, iso_ref, whole_in, *refs):
        pre_ref, iso_pre_ref, gain_grad_ref, whole, sem = refs

        def body(b):
            npos, taps = lay.npos[b], lay.taps[b]
            base = lay.shrink[b]
            source = whole_in.at[pl.ds(base, lay.iso[b])]
            fetch = pltpu.make_async_copy(source, whole.at[pl.ds(0, lay.iso[b])], sem)
            fetch.start()
            m = (most // max(lay.npos)) * npos
            mixed_back = jnp.concatenate([b0[: m // 2], b1[: m // 2]], axis=0)
            shrunk, iso = shrunk_ref[:m], iso_ref[:m]
            hat, inverse = normal(iso + shrunk)
            gain_grad_ref[...] = jnp.sum(mixed_back * hat, axis=0, keepdims=True)
            joint = normal_back(mixed_back, hat, inverse, gain_ref[...])
            iso_pre = (joint * (1.0 - iso * iso)).astype(BF)
            iso_pre_ref[:m] = iso_pre
            age = age_ref[:m]
            total = joint
            fetch.wait()
            for k in range(taps):
                tap = taps - 1 - k
                back = dot_t(iso_pre, whole[tap * width : (tap + 1) * width])
                if k:
                    back = pltpu.roll(jnp.where(age >= k, back, 0.0), m - k, 0)
                total += back
            pre_ref[:m] = (total * (1.0 - shrunk * shrunk)).astype(BF)

        by_branch(where, body)

    return pl.pallas_call(
        kernel,
        out_shape=[
            jax.ShapeDtypeStruct((most, width), BF),
            jax.ShapeDtypeStruct((most, width), BF),
            jax.ShapeDtypeStruct((1, width), F32),
        ],
        in_specs=[smem_spec()] + [vmem_spec()] * 6 + [any_spec()],
        out_specs=[vmem_spec()] * 3,
        scratch_shapes=[pltpu.VMEM((max(lay.iso), width), BF), pltpu.SemaphoreType.DMA],
        compiler_params=pltpu.CompilerParams(vmem_limit_bytes=VMEM),
        cost_estimate=cost(2 * most * width * lay.iso[0], 2 * lay.iso[0] * width),
        name="shrink_backward",
    )(where, age, gain, back_own, back_other, shrunk, iso, whole)


def shrink_weight(lay, where, places, iso_pre, pre, stacked, low_own, low_other, gains, outlet):
    width = lay.width
    most = stacked.shape[1]
    made = len(outlet.shapes())

    def kernel(where, places_ref, gains_ref, iso_pre_ref, pre_ref, own_ref, other_ref, *refs):
        stacked_in, outs = refs[0], refs[1 : 1 + made]
        grad_ref, sems, taps_ref, taps_sem = refs[1 + made :]
        fetch = pltpu.make_async_copy(stacked_in, taps_ref, taps_sem)
        fetch.start()
        extra = gains_ref[...].astype(BF)
        for side in range(2):
            for place in range(lay.n):
                grad_ref[side, place, lay.si_half :, :] = extra

        def body(b):
            npos, taps = lay.npos[b], lay.taps[b]
            m = (most // max(lay.npos)) * npos

            def store(part, row, d):
                first, half, _, shard = part
                d = d.astype(BF)
                lo = row
                while lo < row + width:
                    dp, h, r = lo // shard, (lo % shard) // half, lo % half
                    rows = min(half - r, row + width - lo)
                    side = jnp.where(where[1] == h, 0, 1)
                    grad_ref[side, places_ref[dp], first + r : first + r + rows, :] = d[
                        lo - row : lo - row + rows
                    ]
                    lo += rows

            part_s, part_i = lay.si_parts(b)
            iso_pre, pre = filled(iso_pre_ref[:m], most), filled(pre_ref[:m], most)
            for s in range(STRIDES[b]):
                x = filled(step_rows(own_ref, other_ref, s, npos), most)
                store(part_s, s * width, dot_w(x, pre))
            fetch.wait()
            for k in range(taps):
                store(part_i, (taps - 1 - k) * width, dot_w(taps_ref[k], iso_pre))

        by_branch(where, body)
        outlet.flush(grad_ref, outs, sems)

    return pl.pallas_call(
        kernel,
        out_shape=outlet.shapes(),
        in_specs=[smem_spec(), smem_spec()] + [vmem_spec()] * 5 + [any_spec()],
        out_specs=[any_spec()] * made,
        scratch_shapes=outlet.scratch()
        + [pltpu.VMEM(stacked.shape, BF), pltpu.SemaphoreType.DMA],
        compiler_params=pltpu.CompilerParams(vmem_limit_bytes=VMEM),
        cost_estimate=cost(2 * most * width * (lay.iso[0] + lay.shrink[0]), 30 * MIB),
        name="shrink_weight",
    )(where, places, gains, iso_pre, pre, low_own, low_other, stacked)


def season_backward(lay, where, whole, pre, sum_own, sum_other, order):
    width, length = lay.width, lay.length
    groups = sum_own.shape[0]
    most = max(lay.shrink)

    def kernel(where, order_ref, pre_ref, own_ref, other_ref, whole_in, *refs):
        outs, (whole, rows_ref, sem) = refs[:3], refs[3:]

        def body(b):
            fetch = pltpu.make_async_copy(
                whole_in.at[pl.ds(0, lay.shrink[b])], whole.at[pl.ds(0, lay.shrink[b])], sem
            )
            fetch.start()
            npos = lay.npos[b]
            m = groups * npos
            fetch.wait()
            for s in range(STRIDES[b]):
                cut = slice(s * npos, (s + 1) * npos)
                d = dot_t(pre_ref[: 2 * m], whole[s * width : (s + 1) * width])
                rows_ref[:groups, cut, :] = (
                    d[:m].reshape(groups, npos, width) + own_ref[:, cut, :]
                ).astype(BF)
                rows_ref[groups:, cut, :] = (
                    d[m:].reshape(groups, npos, width) + other_ref[:, cut, :]
                ).astype(BF)

        by_branch(where, body)
        for g in range(groups):
            outs[0][g] = dot_w(order_ref[...], rows_ref[g]).astype(BF)
            ref, i = (outs[1], 0) if g == 0 else (outs[2], g - 1)
            ref[i] = dot_w(order_ref[...], rows_ref[groups + g]).astype(BF)

    return pl.pallas_call(
        kernel,
        out_shape=[
            jax.ShapeDtypeStruct((c, length, width), BF) for c in (groups, 1, groups - 1)
        ],
        in_specs=[smem_spec()] + [vmem_spec()] * 4 + [any_spec()],
        out_specs=[vmem_spec()] * 3,
        scratch_shapes=[
            pltpu.VMEM((most, width), BF),
            pltpu.VMEM((2 * groups, length, width), BF),
            pltpu.SemaphoreType.DMA,
        ],
        compiler_params=pltpu.CompilerParams(vmem_limit_bytes=VMEM),
        cost_estimate=cost(
            4 * groups * length * width * (width + length),
            2 * most * width + 24 * groups * length * width,
        ),
        name="season_backward",
    )(where, order, pre, sum_own, sum_other, whole)


def give_out(lay, member_ids, mine, over_y, sibling, sibling_over_y):
    n, width = lay.n, lay.width

    def kernel(where, mine, over_y, sibling, sibling_over_y, *outs):
        for y in range(2):
            for core in range(2):

                @pl.when((where[0] == y) & (where[1] == core))
                def _(y=y, core=core):
                    for b in range(2):
                        own, other = (mine, sibling) if b == y else (over_y, sibling_over_y)
                        for i, (first, half, _, _) in enumerate(lay.si_parts(b)):
                            for h in range(2):
                                source = own if h == core else other
                                outs[2 * i + b][h * half : (h + 1) * half, :] = source[
                                    first : first + half, :
                                ].astype(F32)

    return pl.pallas_call(
        kernel,
        out_shape=[
            jax.ShapeDtypeStruct((rows // n, width), F32) for rows in (*lay.shrink, *lay.iso)
        ],
        in_specs=[smem_spec()] + [vmem_spec()] * 4,
        out_specs=[vmem_spec()] * 4,
        compiler_params=pltpu.CompilerParams(vmem_limit_bytes=VMEM),
        cost_estimate=cost(0, 12 * MIB),
        name="give_out",
    )(member_ids, mine, over_y, sibling, sibling_over_y)


def dense_whole(lay, where, gf):
    width, ff = lay.width, lay.width * lay.chunks
    count = len(gf.arrays)
    shapes = ((2 * width, width), (ff, width), (width, width), (width, ff))

    def kernel(where, *refs):
        pieces, wholes, sems = refs[:count], refs[count:-1], refs[-1]
        for c in range(2):
            pl.when(where[1] == c)(
                functools.partial(load_f, lay, c, where, gf.meta, pieces, wholes, sems)
            )
        for t in range(4):
            wait_rows(wholes[t], 0, shapes[t][0], sems.at[t])

    return pl.pallas_call(
        kernel,
        out_shape=[jax.ShapeDtypeStruct(v, BF) for v in shapes],
        in_specs=[smem_spec()] + [any_spec()] * count,
        out_specs=[vmem_spec()] * 4,
        scratch_shapes=[pltpu.SemaphoreType.DMA((4,))],
        compiler_params=pltpu.CompilerParams(vmem_limit_bytes=VMEM),
        cost_estimate=cost(0, 4 * sum(r * c for r, c in shapes)),
        name="dense_whole",
    )(where, *gf.arrays)


def dense(lay, where, tile, wholes, mine, received, trend_low, out_grad, gain_middle, gain_output):
    width, length, chunks = lay.width, lay.length, lay.chunks
    cuts = 2
    part = length // cuts
    ff = width * chunks
    strip = 32

    def kernel(where, tile_ref, gm_ref, go_ref, merge, contract, trend, expand, *refs):
        mine_ref, got_ref, trend_ref, grad_ref = refs[:4]
        (hid_ref, hg_ref, ml_ref, ll_ref, mg_ref, tb_ref, out_ref, jm_ref, js_ref) = refs[4:13]
        gains_ref, h_ref, slope_ref, a_ref, b_ref, c_ref = refs[13:]
        b = where[0]
        gm, go = gm_ref[...], go_ref[...]
        at_mine = pl.multiple_of(b * width, width)
        at_other = pl.multiple_of((1 - b) * width, width)

        def strips(body):
            for r in range(0, part, strip):
                body(slice(r, r + strip))

        a_ref[...] = dot(mine_ref[...], merge[pl.ds(at_mine, width)]) + dot(
            got_ref[...], merge[pl.ds(at_other, width)]
        )
        inverses = {}

        def middle_norm(r):
            hat, inverses[r.start] = normal(a_ref[r, :])
            a_ref[r, :] = hat
            ml_ref[r, :] = (hat * gm).astype(BF)

        strips(middle_norm)
        for j in range(chunks):
            cols = slice(j * width, (j + 1) * width)
            h_ref[:, cols] = dot(ml_ref[...], expand[:, cols])

            def gelu(r, cols=cols):
                h = h_ref[r, cols]
                phi, dens = erf_pair(h)
                hid_ref[r, cols] = (h * phi).astype(BF)
                slope_ref[r, cols] = phi + dens

            strips(gelu)
        b_ref[...] = dot(hid_ref[...], contract[...])
        c_ref[...] = dot(trend_ref[0], trend[...])
        sums = [jnp.zeros((8, width), F32), jnp.zeros((8, width), F32)]

        def rows8(v):
            return jnp.sum(v.reshape(strip // 8, 8, width), axis=0)

        def output_norm(r):
            hat, inverse = normal(a_ref[r, :] * gm + b_ref[r, :])
            out_ref[r, :] = (hat * go + c_ref[r, :]).astype(BF)
            g = grad_ref[0, r, :].astype(F32)
            sums[1] += rows8(g * hat)
            d = normal_back(g, hat, inverse, go)
            b_ref[r, :] = d
            ll_ref[r, :] = d.astype(BF)

        strips(output_norm)
        tb_ref[...] = dot_t(grad_ref[0], trend[...])
        for j in range(chunks):
            cols = slice(j * width, (j + 1) * width)
            h_ref[:, cols] = dot_t(ll_ref[...], contract[cols])

            def gelu_back(r, cols=cols):
                hg_ref[r, cols] = (h_ref[r, cols] * slope_ref[r, cols]).astype(BF)

            strips(gelu_back)
        c_ref[...] = dot_t(hg_ref[...], expand[...])

        def middle_back(r):
            hat = a_ref[r, :]
            back = b_ref[r, :] + c_ref[r, :]
            sums[0] += rows8(back * hat)
            mg_ref[r, :] = normal_back(back, hat, inverses[r.start], gm).astype(BF)

        strips(middle_back)
        jm_ref[...] = dot_t(mg_ref[...], merge[pl.ds(at_mine, width)]).astype(BF)
        js_ref[...] = dot_t(mg_ref[...], merge[pl.ds(at_other, width)]).astype(BF)

        @pl.when(pl.program_id(0) == 0)
        def _():
            gains_ref[...] = jnp.zeros_like(gains_ref)

        gains_ref[0:1, :] += jnp.sum(sums[0], axis=0, keepdims=True)
        gains_ref[1:2, :] += jnp.sum(sums[1], axis=0, keepdims=True)

    of_tile = pl.BlockSpec((1, part, width), lambda i, w, t: (t[0], i, 0))
    alone = pl.BlockSpec((part, width), lambda i, w, t: (i, 0))
    shapes = [(ff, BF)] * 2 + [(width, BF)] * 3 + [(width, F32)] + [(width, BF)] * 3
    return pl.pallas_call(
        kernel,
        grid_spec=pltpu.PrefetchScalarGridSpec(
            num_scalar_prefetch=2,
            grid=(cuts,),
            in_specs=[vmem_spec()] * 6 + [alone, alone, of_tile, of_tile],
            out_specs=[pl.BlockSpec((part, c), lambda i, w, t: (i, 0)) for c, _ in shapes]
            + [pl.BlockSpec((2, width), lambda i, w, t: (0, 0))],
            scratch_shapes=[pltpu.VMEM((part, ff), F32)] * 2 + [pltpu.VMEM((part, width), F32)] * 3,
        ),
        out_shape=[jax.ShapeDtypeStruct((length, w), t) for w, t in shapes]
        + [jax.ShapeDtypeStruct((2, width), F32)],
        compiler_params=pltpu.CompilerParams(vmem_limit_bytes=VMEM),
        cost_estimate=cost(
            2 * length * width * (4 * width + 4 * ff + 2 * width), 12 * MIB + 20 * MIB
        ),
        name="dense",
    )(where, tile, gain_middle, gain_output, *wholes, mine, received, trend_low, out_grad)


def dense_weights(lay, where, places, mine, received, trend_low, out_grad, saved, outlet):
    n, width, chunks, length = lay.n, lay.width, lay.chunks, lay.length
    groups = len(saved)
    made = len(outlet.shapes())
    base = lay.g_half
    (_, contract, _, _), (merge_at, merge, _, _) = lay.f_parts(0)
    merge_at -= base

    def kernel(where, places_ref, *refs):
        refs = list(refs)

        def take(count):
            out = refs[:count]
            del refs[:count]
            return out

        middle, lifted = take(groups), take(groups)
        hidden, slopes = take(groups), take(groups)
        late = take(3 * groups) + take(2)
        outs = take(made)
        out_ref, sems, mine_ref, got_ref, grad_ref, trend_ref, up_ref, late_sems = refs
        core, q = where[1], pl.program_id(0)

        def fetches():
            targets = [r.at[g] for r in (mine_ref, got_ref, grad_ref) for g in range(groups)]
            targets += [trend_ref, up_ref]
            return [
                pltpu.make_async_copy(x, y, late_sems.at[i])
                for i, (x, y) in enumerate(zip(late, targets))
            ]

        def side(h):
            return jnp.where(core == h, 0, 1)

        def total(xs, gs):
            d = None
            for x, g in zip(xs, gs):
                v = dot_w(x, g)
                d = v if d is None else d + v
            return d.astype(BF)

        @pl.when(q == 0)
        def _():
            for f in fetches():
                f.start()
            if merge_at + merge < lay.f_half:
                out_ref[side(0), :, merge_at + merge :, :] = jnp.zeros(
                    (n, lay.f_half - merge_at - merge, width), BF
                )

        d = total([r[...] for r in hidden], [r[...] for r in lifted])
        each = width // contract
        for i in range(each):
            out_ref[side(0), places_ref[q * each + i], 0:contract, :] = d[
                i * contract : (i + 1) * contract
            ]
        d = total([r[...] for r in middle], [r[...] for r in slopes])
        at = pl.ds(pl.multiple_of((1 + q) * lay.k, 16), lay.k)
        for dp in range(n):
            out_ref[side(1), places_ref[dp], at, :] = d[dp * lay.k : (dp + 1) * lay.k]

        @pl.when(q == chunks - 1)
        def _():
            for f in fetches():
                f.wait()
            d = total([trend_ref[g] for g in range(groups)], [up_ref[g] for g in range(groups)])
            for dp in range(n):
                out_ref[side(1), places_ref[dp], 0 : lay.k, :] = d[dp * lay.k : (dp + 1) * lay.k]
            each = width // merge
            for ref, first in ((mine_ref, where[0]), (got_ref, 1 - where[0])):
                d = total([ref[g] for g in range(groups)], [grad_ref[g] for g in range(groups)])
                for i in range(each):
                    out_ref[side(0), places_ref[first * each + i], merge_at : merge_at + merge, :] = d[
                        i * merge : (i + 1) * merge
                    ]
            used = (1 + chunks) * lay.k
            if used < lay.f_half:
                out_ref[side(1), :, used:, :] = jnp.zeros((n, lay.f_half - used, width), BF)
            outlet.flush(out_ref, outs, sems)

    whole = pl.BlockSpec((length, width), lambda q: (0, 0))
    column = pl.BlockSpec((length, width), lambda q: (0, q))
    arrays = [k[0] for k in saved] + [k[3] for k in saved]
    arrays += [k[1] for k in saved] + [k[2] for k in saved]
    arrays += [v.reshape(length, width) for v in mine] + list(received) + [k[4] for k in saved]
    arrays += [trend_low, out_grad]
    ff = chunks * width
    square = pltpu.VMEM((groups, length, width), BF)
    return pl.pallas_call(
        kernel,
        grid=(chunks,),
        out_shape=outlet.shapes(),
        in_specs=[smem_spec(), smem_spec()]
        + [whole] * (2 * groups)
        + [column] * (2 * groups)
        + [any_spec()] * (3 * groups + 2),
        out_specs=[any_spec()] * made,
        scratch_shapes=outlet.scratch()
        + [square] * 5
        + [pltpu.SemaphoreType.DMA((3 * groups + 2,))],
        compiler_params=pltpu.CompilerParams(vmem_limit_bytes=VMEM),
        cost_estimate=cost(
            2 * groups * length * width * (2 * width + 2 * ff + width), 45 * MIB
        ),
        name="dense_weights",
    )(where, places, *arrays)


def exchange(axis, size, step):
    return lambda v: lax.ppermute(v, axis, [(i, i ^ step) for i in range(size)])


def on_device(
    n,
    series_in,
    block_kinds,
    out_grad,
    fine_shrink,
    coarse_shrink,
    fine_isometric,
    coarse_isometric,
    fine_grow,
    coarse_grow,
    merge_weight,
    expand_weight,
    contract_weight,
    trend_weight,
    branch_gain,
    middle_gain,
    output_gain,
):
    ring = Ring(n)
    member = lax.axis_index("group")
    core, y = member % 2, member // 2
    block_count = block_kinds.shape[0]
    width = series_in.shape[1]
    block_len = series_in.shape[0] // block_count
    groups = block_count // GROUP
    lay = Layout(n, width, block_len, expand_weight.shape[1])
    length = lay.length
    share = branch_gain.shape[0]
    fine = y == 0

    def right(v):
        return lax.ppermute(v, "dp", ring.right)

    def left(v):
        return lax.ppermute(v, "dp", ring.left)

    shards = (fine_shrink, coarse_shrink, fine_isometric, coarse_isometric)
    shards += (fine_grow, coarse_grow)
    dense_shards = (contract_weight, merge_weight, trend_weight, expand_weight)
    member_ids = jnp.stack([y, core]).astype(jnp.int32)
    own = half_of(lay, member_ids, False, *shards, dense_shards)
    offsets = [0]
    pieces = Pieces()
    for k in range(1, n // 2):
        offsets += [-k, k]
    offsets.append(n // 2)

    def source(offset):
        return offsets.index(offset if abs(offset) < n // 2 else n // 2)

    where = jnp.stack([y, core] + [ring.index(o) for o in offsets]).astype(jnp.int32)

    x_own = series_in.reshape(groups, length, width)
    x_other = []
    last = n // 2

    def prepare_own(kinds, x):
        rows = jnp.arange(length, dtype=jnp.int32)
        npos = jnp.where(fine, lay.npos[0], lay.npos[1])
        stride = jnp.where(fine, STRIDES[0], STRIDES[1])
        step = ((rows % npos) * stride + rows // npos)[:, None]
        return (step, *season_kernel(lay, kinds, step, x, True))

    def prepare_other(step, kinds, *xs):
        kinds = kinds.astype(jnp.int32)
        return (kinds, *season_kernel(lay, kinds, step, jnp.stack(xs), False))

    def spread_gains(*parts):
        parts = jnp.stack(parts).astype(F32)
        return lax.dynamic_update_slice(
            jnp.zeros((3, width), F32), parts, (jnp.int32(0), ring.me * share)
        )

    doublings = []
    size = 1
    while size < n:
        doublings.append(size)
        size *= 2
    gains = spread_gains(branch_gain, middle_gain, output_gain)
    hops = [exchange("dp", n, d) for d in doublings]

    def hop(sends):
        if hops:
            sends["gain"] = (gains, hops.pop(0))

    whole_r = whole_l = own
    half_rows = (lay.g_half + lay.f_half) // 2
    si_rows = lay.si_half // 2
    for t in range(1, last):
        sends = {"r": (whole_r, right), "l": (whole_l, left)}
        if t > 1:
            sends["cr"], sends["cl"] = (whole_r, swap_core), (whole_l, swap_core)
        if t <= groups:
            sends["x"] = (x_own[t - 1], swap_y)
        work, given = None, ()
        if t == 1:
            sends["k"] = (block_kinds.astype(F32), swap_y)
            hop(sends)
            work = lambda *v: (half_of(lay, member_ids, True, *v[:6], v[6:]),)
            given = (*shards, *dense_shards)
        elif t == 2:
            work, given = prepare_own, (block_kinds, x_own)
        arrived, done = slot(sends, work, given)
        if t == 1:
            kinds_other = arrived["k"]
            pieces.add(0, 0, 0, own)
            pieces.add(0, 1, 0, done[0])
        elif t == 2:
            step, season_own, low_own, own_counts, trend_low, order = done
        if "x" in arrived:
            x_other.append(arrived["x"])
        if "gain" in arrived:
            gains = gains + arrived["gain"]
        if t > 1:
            pieces.add(source(1 - t), 1, 0, arrived["cr"])
            pieces.add(source(t - 1), 1, 0, arrived["cl"])
        whole_r, whole_l = arrived["r"], arrived["l"]
        pieces.add(source(-t), 0, 0, whole_r)
        pieces.add(source(t), 0, 0, whole_l)
    middle = lay.si_half
    sends = {"r": (whole_r[:si_rows], right), "l": (whole_l[si_rows:middle], left)}
    sends["cr"], sends["cl"] = (whole_r, swap_core), (whole_l, swap_core)
    hop(sends)
    arrived, done = slot(sends, prepare_other, (step, kinds_other, *x_other))
    kinds_other, season_other, low_other = done
    if "gain" in arrived:
        gains = gains + arrived["gain"]
    pieces.add(source(1 - last), 1, 0, arrived["cr"])
    pieces.add(source(last - 1), 1, 0, arrived["cl"])
    si_r, si_l = arrived["r"], arrived["l"]
    pieces.add(source(last), 0, 0, si_r)
    pieces.add(source(last), 0, si_rows, si_l)
    sends = {"cr": (si_r, swap_core), "cl": (si_l, swap_core)}
    hop(sends)
    arrived, _ = slot(sends)
    if "gain" in arrived:
        gains = gains + arrived["gain"]
    pieces.add(source(last), 1, 0, arrived["cr"])
    pieces.add(source(last), 1, si_rows, arrived["cl"])
    for move_gains in hops:
        gains = gains + move_gains(gains)
    gain_b, gain_m, gain_o = gains[0:1], gains[1:2], gains[2:3]

    def run_shrink(low_own, low_other, *arrays):
        pieces.arrays = list(arrays)
        return shrink_forward(
            lay, where, pieces, low_own, low_other, block_kinds, kinds_other, gain_b
        )

    cut_at = middle + half_rows
    sends = {"r": (whole_r[middle:cut_at], right), "l": (whole_l[cut_at:], left)}
    arrived, done = slot(sends, run_shrink, (low_own, low_other, *pieces.arrays))
    shrunk, iso, mixed, age, stacked_rows, si_whole = done
    gf_r, gf_l = arrived["r"], arrived["l"]
    pieces.add(source(last), 0, middle, gf_r)
    pieces.add(source(last), 0, cut_at, gf_l)
    arrived, _ = slot({"cr": (gf_r, swap_core), "cl": (gf_l, swap_core)})
    pieces.add(source(last), 1, middle, arrived["cr"])
    pieces.add(source(last), 1, cut_at, arrived["cl"])
    gf = pieces

    *branch_other, up_other, g_whole = grow_forward(
        lay, where, gf, 1, mixed, season_other, order, gain_b
    )
    branch_other = [v.reshape(length, width) for v in branch_other]
    grads_in = out_grad.reshape(groups, length, width)

    def grow_own(mixed, g_whole, season_own, *arrays):
        gf.arrays = list(arrays)
        made = grow_forward(lay, where, g_whole, 0, mixed, season_own, order, gain_b)
        return (*made, *dense_whole(lay, where, gf))

    arrived, done = slot(
        {"b": (branch_other[0], swap_y)}, grow_own, (mixed, g_whole, season_own, *gf.arrays)
    )
    branch_own = [v.reshape(length, width) for v in done[:groups]]
    up_own, wholes = done[groups], done[groups + 1 :]
    received = [arrived["b"]]
    outs, back_own, back_got, waiting, trend_back, saved, dense_gains = [], [], [], [], [], [], None
    for g in range(groups):
        sends = {}
        if g + 1 < groups:
            sends["b"] = (branch_other[g + 1], swap_y)
        elif waiting:
            sends["j"] = (waiting.pop(0), swap_y)

        def run_dense(mine, got, *wholes, g=g):
            tile = jnp.full((1,), g, jnp.int32)
            return dense(
                lay, where, tile, wholes, mine, got, trend_low, grads_in, gain_m, gain_o
            )

        arrived, made = slot(sends, run_dense, (branch_own[g], received[g], *wholes))
        if "b" in arrived:
            received.append(arrived["b"])
        if "j" in arrived:
            back_got.append(arrived["j"])
        outs.append(made[6])
        back_own.append(made[7])
        waiting.append(made[8])
        trend_back.append(made[5])
        saved.append((made[2], made[0], made[1], made[3], made[4]))
        dense_gains = made[9] if dense_gains is None else dense_gains + made[9]
    series_out = jnp.concatenate(outs)

    ring_order = [n // 2]
    for k in range(n // 2 - 1, 0, -1):
        ring_order += [k, -k]
    ring_order.append(0)
    spot = jnp.zeros((n,), jnp.int32)
    for place, offset in enumerate(ring_order):
        spot = jnp.where(jnp.arange(n) == ring.index(offset), place, spot)

    f_outlet = Outlet(n, lay.f_half, width, None)
    g_outlet = Outlet(n, lay.g_half, width, None)
    s_outlet = Outlet(n, lay.si_half + 16, width, None)

    def run_dense_weights(*arrays):
        mine, got, flat = arrays[:groups], arrays[groups : 2 * groups], arrays[2 * groups :]
        kept = [flat[5 * g : 5 * g + 5] for g in range(groups)]
        return dense_weights(
            lay, where, spot, mine, list(got), trend_low, grads_in, kept, f_outlet
        )

    class Chain:
        def __init__(self, keep):
            self.keep = keep
            self.got = []
            self.step = last
            self.r = self.l = None
            self.half = keep.shape[1] // 2

        def here(self, place):
            first = 0
            for v in self.got:
                if place < first + v.shape[0]:
                    got = v[place - first]
                    break
                first += v.shape[0]
            return self.keep[place].astype(F32) + got.astype(F32)

        def sends(self):
            k = self.step
            if k == last:
                part = self.here(0)
                return part[: self.half].astype(BF), part[self.half :].astype(BF)
            place = 1 + 2 * (last - 1 - k)
            a, b = self.here(place), self.here(place + 1)
            if k == last - 1:
                h = self.half
                a = jnp.concatenate([a[:h] + self.r.astype(F32), a[h:]])
                b = jnp.concatenate([b[:h], b[h:] + self.l.astype(F32)])
            else:
                a, b = a + self.r.astype(F32), b + self.l.astype(F32)
            return a.astype(BF), b.astype(BF)

        def total(self):
            return (self.here(n - 1) + self.r.astype(F32) + self.l.astype(F32)).astype(BF)

    def back_of(grads, g_whole, up, season):
        return grow_backward(lay, where, g_whole, grads, up, season, order, gain_b)

    def weights_and_own(g_whole, up, season, *rest):
        return (
            *run_dense_weights(*rest[groups:]),
            *back_of(rest[:groups], g_whole, up, season),
        )

    sends = {"j%d" % i: (v, swap_y) for i, v in enumerate(waiting)}
    arrived, done = slot(
        sends,
        weights_and_own,
        (g_whole, up_own, season_own, *back_own, *branch_own, *received)
        + tuple(v for k in saved for v in k),
    )
    back_got += [arrived[k] for k in sends]
    f_keep, f_give = done[:2]
    pre_own, mixed_back_own, sum_own, gains_own = done[2:]
    chains = {}
    kept = {}
    finals = {}
    t = 0
    while True:
        active = {k: c for k, c in chains.items() if c.step > 0}
        finishing = [k for k, c in chains.items() if c.step == 0 and k + "mine" not in finals]
        if len(active) > 1:
            finishing = []
        if not active and not finishing and "smine" in finals:
            break
        sends, work, given = {}, None, ()
        for name, chain in active.items():
            a, b = chain.sends()
            sends[name + "r"], sends[name + "l"] = (a, right), (b, left)
        for name in finishing:
            mine = chains[name].total()
            finals[name + "mine"] = mine
            sends[name + "y"] = (mine, swap_y)
            if name != "f":
                sends[name + "c"] = (mine, swap_core)
        for name in ("f", "g"):
            if name + "late" in finals and name + "sent" not in finals:
                sends[name + "d"] = (finals[name + "late"], swap_core)
                finals[name + "sent"] = True
        if t == 0:
            work = lambda g_whole, up, season, *grads: back_of(grads, g_whole, up, season)
            given = (g_whole, up_other, season_other, *back_got)
            sends["f0"] = (f_give, swap_core)
        elif t == 1:
            work = lambda *v: grow_weight(lay, where, spot, *v, g_outlet)
            given = (mixed, pre_own, pre_other)
        elif t == 2:
            work = lambda *v: shrink_backward(lay, where, *v, age, gain_b)
            given = (si_whole, mixed_back_own, mixed_back_other, shrunk, iso)
            sends["g"] = (g_give, swap_core)
        elif t == 3:
            work = lambda *v: shrink_weight(lay, where, spot, *v, s_outlet)
            given = (iso_pre, shrink_pre, stacked_rows, low_own, low_other, grad_gains)
        elif t == 4:
            work = lambda *v: season_backward(lay, where, *v, order)
            given = (si_whole, shrink_pre, sum_own, sum_other)
            sends["s0"] = (s_give, swap_core)
        if t in (5, 6):
            sends["x"] = (tail_sends[t - 5], swap_y)
        if "s" in finishing:
            work, given = finish, (season_mine, own_counts, *trend_back, *tail)
        arrived, done = slot(sends, work, given)
        if t == 0:
            pre_other, mixed_back_other, sum_other, gains_other = done
            chains["f"] = Chain(f_keep)
            chains["f"].got = [arrived["f0"]]
        elif t == 1:
            g_keep, g_give = done
            chains["g"] = None
        elif t == 2:
            shrink_pre, iso_pre, gains_si = done
            chains["g"] = Chain(g_keep)
            chains["g"].got = [arrived["g"]]
            grad_gains = jnp.concatenate(
                [gains_own + gains_other + gains_si, dense_gains, jnp.zeros((13, width), F32)]
            )
        elif t == 3:
            s_keep, s_give = done
        elif t == 4:
            season_mine, *tail_sends = done
            tail = []
            chains["s"] = Chain(s_keep)
            chains["s"].got = [arrived["s0"]]

            def finish(season_mine, own_counts, *rest):
                backs, tail = rest[:groups], rest[groups:]
                total = season_mine.astype(F32) + jnp.concatenate(tail).astype(F32)
                rest = jnp.stack(backs) - total
                spread = (rest * (1.0 / WINDOW)).astype(BF)
                averaged = jnp.einsum(
                    "gij,gid->gjd", own_counts, spread, preferred_element_type=F32
                )
                return ((total + averaged).astype(BF),)

        if "x" in arrived:
            tail.append(arrived["x"])
        for name, chain in active.items():
            chain.r, chain.l = arrived[name + "r"], arrived[name + "l"]
            chain.step -= 1
        for name in ("f", "g"):
            if name + "d" in arrived:
                finals[name + "d"] = arrived[name + "d"]
        for name in finishing:
            finals[name + "y"] = arrived[name + "y"]
            if name != "f":
                finals[name + "c"] = arrived[name + "c"]
            if name == "f":
                mine = finals["fmine"].astype(F32) + arrived["fy"].astype(F32)
                finals["flate"] = mine.astype(BF)
            elif name == "g":
                finals["glate"] = arrived["gy"]
            else:
                (series_grad,) = done
        if chains.get("g", 0) is None:
            del chains["g"]
        t += 1
    s_mine, s_y = finals["smine"], finals["sy"]
    s_core = (finals["sc"], swap_core(s_y))
    f_half, f_other = finals["flate"], finals["fd"]
    g_mine, g_y = finals["gmine"], finals["gy"]
    g_core = (finals["gc"], finals["gd"])

    def both(mine, other):
        return jnp.where(core == 0, mine, other), jnp.where(core == 0, other, mine)

    def branches(mine, over_y):
        return jnp.where(fine, mine, over_y), jnp.where(fine, over_y, mine)

    g_fine, g_coarse = branches(g_mine, g_y)
    h_fine, h_coarse = branches(*g_core)

    def g_out(b, mine, other):
        lo, hi = both(mine, other)
        cols = [v[r : r + k] for v in (lo, hi) for r, k, _ in lay.g_parts(b)]
        return jnp.concatenate(cols, axis=1).astype(F32)

    fine_shrink_grad, coarse_shrink_grad, fine_iso_grad, coarse_iso_grad = give_out(
        lay, member_ids, s_mine, s_y, *s_core
    )
    fine_grow_grad, coarse_grow_grad = g_out(0, g_fine, h_fine), g_out(1, g_coarse, h_coarse)
    lo, hi = both(f_half, f_other)
    (a0, a1, _, _), (b0, b1, _, _) = lay.f_parts(0)
    z = lay.g_half
    contract_grad = lo[a0 - z : a0 - z + a1].astype(F32)
    merge_grad = lo[b0 - z : b0 - z + b1].astype(F32)
    rest = [hi[a - z : a - z + rows].astype(F32) for a, rows, _, _ in lay.f_parts(1)]
    trend_grad, expand_grad = rest[0], jnp.concatenate(rest[1:], axis=1)

    at = lay.si_half
    gain_grads = s_mine[at : at + 3].astype(F32) + s_y[at : at + 3].astype(F32)
    gain_grads = lax.dynamic_slice(gain_grads, (jnp.int32(0), ring.me * share), (3, share))
    return (
        series_out,
        series_grad.reshape(series_in.shape),
        fine_shrink_grad,
        coarse_shrink_grad,
        fine_iso_grad,
        coarse_iso_grad,
        fine_grow_grad,
        coarse_grow_grad,
        merge_grad,
        expand_grad,
        contract_grad,
        trend_grad,
        gain_grads[0],
        gain_grads[1],
        gain_grads[2],
    )


def solution(mesh):
    n = mesh.shape["dp"]
    rows = P(("dp", "group"), None)
    weight = P("dp", None)
    return jax.shard_map(
        lambda *args: on_device(n, *args),
        mesh=mesh,
        in_specs=(rows, P(("dp", "group")), rows) + (weight,) * 10 + (P("dp"),) * 3,
        out_specs=(rows, rows) + (weight,) * 10 + (P("dp"),) * 3,
        check_vma=False,
    )
```

```python
import functools
import math

import jax
import jax.numpy as jnp
from jax import lax
from jax.experimental import pallas as pl
from jax.experimental.pallas import tpu as pltpu
from jax.sharding import PartitionSpec as P

STRIDES = (12, 16)
WINDOW = 25
HALF = WINDOW // 2
GROUP = 4
BF = jnp.bfloat16
F32 = jnp.float32
MIB = 1024 * 1024
VMEM = 127 * MIB // 2
CORE_SWAP = ((0, 1), (1, 0), (2, 3), (3, 2))
Y_SWAP = ((0, 2), (2, 0), (1, 3), (3, 1))


class Layout:
    def __init__(self, n, width, block_len, ff):
        self.n, self.width, self.block_len = n, width, block_len
        self.length = GROUP * block_len
        self.taps = tuple(block_len // s for s in STRIDES)
        self.shrink = tuple(s * width for s in STRIDES)
        self.iso = tuple(p * width for p in self.taps)
        self.si_half = (self.shrink[0] + self.iso[0]) // (2 * n)
        self.k = width // n
        self.g_half = max(STRIDES) // 2 * self.k
        self.chunks = ff // width
        self.merge, self.contract = 2 * width // n, ff // n
        self.f_half = max(self.contract + self.merge, self.k * (1 + self.chunks))
        self.npos = tuple(GROUP * p for p in self.taps)

    def si_parts(self, b):
        s, i = self.shrink[b] // self.n, self.iso[b] // self.n
        return [(0, s // 2, 0, s), (s // 2, i // 2, self.shrink[b], i)]

    def g_parts(self, b):
        return [(j * self.k, self.k, j) for j in range(STRIDES[b] // 2)]

    def f_parts(self, h):
        base = self.g_half
        if h == 0:
            return [
                (base, self.contract, "contract", 0),
                (base + self.contract, self.merge, "merge", 0),
            ]
        found = [(base, self.k, "trend", 0)]
        for j in range(self.chunks):
            found.append((base + (1 + j) * self.k, self.k, "expand", j))
        return found


def held(*values):
    return lax.optimization_barrier(values)


class Ring:
    def __init__(self, n):
        self.n = n
        order = list(range(0, n, 2)) + list(range(n - 1, 0, -2))
        self.right = [(order[k], order[(k + 1) % n]) for k in range(n)]
        self.left = [(b, a) for a, b in self.right]
        d = lax.axis_index("dp")
        self.me = d
        self.pos = jnp.where(d % 2 == 0, d // 2, n - 1 - d // 2)

    def index(self, offset):
        if offset == 0:
            return self.me
        r = (self.pos + offset) % self.n
        return jnp.where(r < self.n // 2, 2 * r, 2 * (self.n - 1 - r) + 1)


def slot(sends, work=None, given=()):
    names = list(sends)
    tied = held(*[sends[k][0] for k in names], *given)
    moved = [sends[k][1](v) for k, v in zip(names, tied)]
    done = tuple(work(*tied[len(names) :])) if work is not None else ()
    out = held(*moved, *done)
    return dict(zip(names, out[: len(names)])), out[len(names) :]


def swap_core(v):
    return lax.ppermute(v, "group", CORE_SWAP)


def swap_y(v):
    return lax.ppermute(v, "group", Y_SWAP)


def dot(a, b):
    return jnp.dot(a, b, preferred_element_type=F32)


def dot_t(a, b):
    return lax.dot_general(a, b, (((1,), (1,)), ((), ())), preferred_element_type=F32)


def dot_w(a, b):
    return lax.dot_general(a, b, (((0,), (0,)), ((), ())), preferred_element_type=F32)


def normal(v):
    center = jnp.mean(v, axis=-1, keepdims=True)
    centered = v - center
    inverse = lax.rsqrt(jnp.mean(centered * centered, axis=-1, keepdims=True) + 1e-05)
    return centered * inverse, inverse


def normal_back(grad, hat, inverse, gain):
    g = grad * gain
    a = jnp.mean(g, axis=-1, keepdims=True)
    b = jnp.mean(g * hat, axis=-1, keepdims=True)
    return inverse * (g - a - hat * b)


def erf_pair(h):
    d = 1.0 + (0.3275911 / math.sqrt(2.0)) * jnp.abs(h)
    t = pl.reciprocal(d, approx=True)
    t = t * (2.0 - d * t)
    e = jnp.exp(-0.5 * (h * h))
    p = 0.5 * -1.453152027 + t * (0.5 * 1.061405429)
    p = 0.5 * 1.421413741 + t * p
    p = 0.5 * -0.284496736 + t * p
    q = (0.5 * 0.254829592 + t * p) * (t * e)
    return jnp.where(h >= 0, 1.0 - q, q), (h * e) * (1.0 / math.sqrt(2.0 * math.pi))


def over(parts, first, rows):
    for part in parts:
        lo, hi = max(first, part[0]), min(first + rows, part[0] + part[1])
        if lo < hi:
            yield lo - first, hi - lo, lo - part[0], part


def start_copy(piece, row, rows, whole, at, sem):
    at = at if isinstance(at, int) else pl.multiple_of(at, 16)
    pltpu.make_async_copy(
        piece.at[pl.ds(row, rows)], whole.at[pl.ds(at, rows)], sem
    ).start()


def wait_rows(whole, first, rows, sem):
    view = whole.at[pl.ds(first, rows)]
    pltpu.make_async_copy(view, view, sem).wait()


class Pieces:
    def __init__(self):
        self.meta, self.arrays = [], []

    def add(self, source, other, first, array):
        self.meta.append((source, other, first, array.shape[0]))
        self.arrays.append(array)


def load_si(lay, b, where, meta, refs, whole, sems):
    core = where[1]
    for (source, other, first, rows), ref in zip(meta, refs):
        src = where[2 + source]
        h = 1 - core if other else core
        for row, count, inside, part in over(lay.si_parts(b), first, rows):
            _, half, base, shard = part
            at = base + src * shard + h * half + inside
            start_copy(ref, row, count, whole, at, sems.at[0 if base == 0 else 1])


def load_g(lay, b, where, meta, refs, whole, sem):
    core = where[1]
    for (source, other, first, rows), ref in zip(meta, refs):
        src = where[2 + source]
        h = 1 - core if other else core
        for row, count, inside, part in over(lay.g_parts(b), first - lay.si_half, rows):
            at = (h * (STRIDES[b] // 2) + part[2]) * lay.width + src * lay.k + inside
            start_copy(ref, row, count, whole, at, sem)


def load_f(lay, c, where, meta, refs, wholes, sems):
    names = ("merge", "contract", "trend", "expand")
    width = lay.width
    for (source, other, first, rows), ref in zip(meta, refs):
        src = where[2 + source]
        h = 1 - c if other else c
        for row, count, inside, part in over(lay.f_parts(h), first - lay.si_half, rows):
            t = names.index(part[2])
            at = pl.multiple_of(src * part[1] + inside, 16)
            target = wholes[t].at[pl.ds(at, count), pl.ds(part[3] * width, width)]
            pltpu.make_async_copy(ref.at[pl.ds(row, count)], target, sems.at[t]).start()


def any_spec():
    return pl.BlockSpec(memory_space=pl.ANY)


def vmem_spec():
    return pl.BlockSpec(memory_space=pltpu.VMEM)


def smem_spec():
    return pl.BlockSpec(memory_space=pltpu.SMEM)


def cost(flops, moved):
    return pl.CostEstimate(flops=int(flops), bytes_accessed=int(moved), transcendentals=0)


def by_branch(where, body):
    for b in range(2):
        pl.when(where[0] == b)(functools.partial(body, b))


def half_of(lay, where, sibling, fs, cs, fi, ci, fg, cg, weights):
    width, k = lay.width, lay.k
    base = lay.si_half
    rows = base + lay.g_half + lay.f_half

    def kernel(where, fs, cs, fi, ci, fg, cg, contract, merge, trend, expand, out, sems):
        def moves(b, h):
            found = []
            for i, (first, half, _, _) in enumerate(lay.si_parts(b)):
                source = ((fs, fi), (cs, ci))[b][i]
                found.append((source.at[pl.ds(h * half, half)], out.at[pl.ds(first, half)]))
            for first, count, j in lay.g_parts(b):
                col = (h * (STRIDES[b] // 2) + j) * width
                source = (fg, cg)[b].at[:, pl.ds(col, width)]
                found.append((source, out.at[pl.ds(base + first, count)]))
            named = {"contract": contract, "merge": merge, "trend": trend}
            for first, count, name, j in lay.f_parts(h):
                source = expand.at[:, pl.ds(j * width, width)] if name == "expand" else named[name]
                found.append((source, out.at[pl.ds(base + first, count)]))
            return [(x, y, sems.at[i]) for i, (x, y) in enumerate(found)]

        for b in range(2):
            for h in range(2):

                @pl.when((where[0] == b) & (where[1] == (1 - h if sibling else h)))
                def _(b=b, h=h):
                    used = lay.g_parts(b)[-1][0] + k
                    if used < lay.g_half:
                        out[base + used : base + lay.g_half, :] = jnp.zeros(
                            (lay.g_half - used, width), BF
                        )
                    used = lay.f_parts(h)[-1][0] + lay.f_parts(h)[-1][1]
                    if used < lay.g_half + lay.f_half:
                        out[base + used :, :] = jnp.zeros((rows - base - used, width), BF)
                    for x, y, sem in moves(b, h):
                        pltpu.make_async_copy(x, y, sem).start()
                    for x, y, sem in moves(b, h):
                        pltpu.make_async_copy(x, y, sem).wait()

    return pl.pallas_call(
        kernel,
        out_shape=jax.ShapeDtypeStruct((rows, width), BF),
        in_specs=[smem_spec()] + [any_spec()] * 10,
        out_specs=vmem_spec(),
        scratch_shapes=[pltpu.SemaphoreType.DMA((8 + max(STRIDES),))],
        compiler_params=pltpu.CompilerParams(vmem_limit_bytes=VMEM),
        cost_estimate=cost(0, 4 * rows * width),
        name="sibling_half" if sibling else "own_half",
    )(where, fs, cs, fi, ci, fg, cg, *weights)


def bounds_of(kinds, base):
    firsts, lasts = [jnp.int32(0)], [jnp.int32(GROUP - 1)]
    for b in range(1, GROUP):
        firsts.append(jnp.where(kinds[base + b] == 2, firsts[-1], b))
    for b in reversed(range(GROUP - 1)):
        lasts.insert(0, jnp.where(kinds[base + b + 1] == 2, lasts[0], b))
    return firsts, lasts


def counts_of(lay, kinds, base, step):
    firsts, lasts = bounds_of(kinds, base)
    length = lay.length
    first = jnp.zeros_like(step)
    last = jnp.full_like(step, length - 1)
    for b in range(GROUP):
        inside = (step >= b * lay.block_len) & (step < (b + 1) * lay.block_len)
        first = jnp.where(inside, firsts[b] * lay.block_len, first)
        last = jnp.where(inside, lasts[b] * lay.block_len + (lay.block_len - 1), last)
    j = lax.broadcasted_iota(jnp.int32, (length, length), 1)
    low = jnp.maximum(step - HALF, first)
    high = jnp.minimum(step + HALF, last)
    count = jnp.where((j >= low) & (j <= high), 1.0, 0.0)
    before = jnp.maximum(first - step + HALF, 0).astype(F32)
    after = jnp.maximum(step + HALF - last, 0).astype(F32)
    count += jnp.where(j == first, before, 0.0)
    count += jnp.where(j == last, after, 0.0)
    return count.astype(BF)


def season_kernel(lay, kinds, step, x, with_trend):
    width, length = lay.width, lay.length
    groups = x.shape[0]

    def kernel(kinds_ref, step_ref, x_ref, season_ref, low_ref, *refs):
        base = pl.program_id(0) * GROUP
        step = step_ref[...]
        x = x_ref[0]
        j = lax.broadcasted_iota(jnp.int32, (length, length), 1)
        order = jnp.where(j == step, 1.0, 0.0).astype(BF)
        season = dot(order, x) - dot(counts_of(lay, kinds_ref, base, step), x) * (1.0 / WINDOW)
        season_ref[0] = season
        low_ref[0] = season.astype(BF)
        if with_trend:
            counts_ref, trend_ref, order_ref = refs
            order_ref[...] = order
            plain = lax.broadcasted_iota(jnp.int32, (length, 1), 0)
            counts = counts_of(lay, kinds_ref, base, plain)
            counts_ref[0] = counts
            trend_ref[0] = (dot(counts, x) * (1.0 / WINDOW)).astype(BF)

    group = pl.BlockSpec((1, length, width), lambda g: (g, 0, 0))
    square = pl.BlockSpec((1, length, length), lambda g: (g, 0, 0))
    shapes = [
        jax.ShapeDtypeStruct((groups, length, width), F32),
        jax.ShapeDtypeStruct((groups, length, width), BF),
    ]
    specs = [group, group]
    if with_trend:
        shapes += [
            jax.ShapeDtypeStruct((groups, length, length), BF),
            jax.ShapeDtypeStruct((groups, length, width), BF),
            jax.ShapeDtypeStruct((length, length), BF),
        ]
        specs += [square, group, pl.BlockSpec((length, length), lambda g: (0, 0))]
    return pl.pallas_call(
        kernel,
        grid=(groups,),
        out_shape=shapes,
        in_specs=[smem_spec(), pl.BlockSpec((length, 1), lambda g: (0, 0)), group],
        out_specs=specs,
        compiler_params=pltpu.CompilerParams(vmem_limit_bytes=VMEM),
        cost_estimate=cost(6 * groups * length * length * width, 12 * groups * length * width),
        name="season_trend" if with_trend else "season",
    )(kinds, step, x)


def all_taps(x, age, taps):
    rolled = [x] + [pltpu.roll(x, k, 0) for k in range(1, min(8, taps))]
    for k in range(taps):
        v = rolled[k % 8]
        if k >= 8:
            v = jnp.concatenate([jnp.zeros_like(v[: k - k % 8]), v[: v.shape[0] - (k - k % 8)]])
        yield k, jnp.where(age >= k, v, 0.0) if k else v


def step_rows(own, other, s, npos):
    cut = slice(s * npos, (s + 1) * npos)
    x = jnp.concatenate([own[:, cut, :], other[:, cut, :]], axis=0)
    return x.reshape(x.shape[0] * npos, x.shape[2])


def filled(x, rows):
    if x.shape[0] == rows:
        return x
    return jnp.concatenate([x, jnp.zeros((rows - x.shape[0], x.shape[1]), x.dtype)], axis=0)


def shrink_forward(lay, where, si, low_own, low_other, kinds_own, kinds_other, gain):
    n, width = lay.n, lay.width
    groups = 2 * low_own.shape[0]
    most = groups * max(lay.npos)
    count = len(si.arrays)
    total = lay.shrink[0] + lay.iso[0]

    def kernel(where, kinds_own, kinds_other, gain_ref, own_ref, other_ref, *refs):
        pieces, rest = refs[:count], refs[count:]
        shrunk_ref, iso_ref, mixed_ref, age_ref, taps_out, whole_out, whole, taps_ref, sems = rest

        def body(b):
            load_si(lay, b, where, si.meta, pieces, whole, sems)
            npos = lay.npos[b]
            m = groups * npos
            wait_rows(whole, 0, lay.shrink[b], sems.at[0])
            z = jnp.zeros((m, width), F32)
            for s in range(STRIDES[b]):
                z += dot(step_rows(own_ref, other_ref, s, npos), whole[s * width : (s + 1) * width])
            shrunk = jnp.tanh(z)
            shrunk_ref[:m] = shrunk
            low = shrunk.astype(BF).astype(F32)
            wait_rows(whole, lay.shrink[b], lay.iso[b], sems.at[1])
            pltpu.make_async_copy(whole, whole_out, sems.at[2]).start()
            taps = lay.taps[b]
            base = lay.shrink[b]
            row = lax.broadcasted_iota(jnp.int32, (m, 1), 0)
            age = jnp.zeros_like(row)
            for g in range(groups):
                own = g < groups // 2
                kinds = kinds_own if own else kinds_other
                firsts, _ = bounds_of(kinds, (g if own else g - groups // 2) * GROUP)
                for i in range(GROUP):
                    lo = g * npos + i * taps
                    inside = (row >= lo) & (row < lo + taps)
                    age = jnp.where(inside, row - lo + (i - firsts[i]) * taps, age)
            age_ref[:m] = age
            e = jnp.zeros((m, width), F32)
            for k, x in all_taps(low, age, taps):
                at = base + (taps - 1 - k) * width
                x = x.astype(BF)
                taps_ref[k, :m, :] = x
                if m < most:
                    taps_ref[k, m:, :] = jnp.zeros((most - m, width), BF)
                e += dot(x, whole[at : at + width])
            keep = pltpu.make_async_copy(taps_ref, taps_out, sems.at[3])
            keep.start()
            iso = jnp.tanh(e)
            iso_ref[:m] = iso
            hat, _ = normal(iso + shrunk)
            mixed_ref[:m] = (hat * gain_ref[...]).astype(BF)
            pltpu.make_async_copy(whole, whole_out, sems.at[2]).wait()
            keep.wait()

        by_branch(where, body)

    return pl.pallas_call(
        kernel,
        out_shape=[
            jax.ShapeDtypeStruct((most, width), F32),
            jax.ShapeDtypeStruct((most, width), F32),
            jax.ShapeDtypeStruct((most, width), BF),
            jax.ShapeDtypeStruct((most, 1), jnp.int32),
            jax.ShapeDtypeStruct((max(lay.taps), most, width), BF),
            jax.ShapeDtypeStruct((total, width), BF),
        ],
        in_specs=[smem_spec()] * 3 + [vmem_spec()] * 3 + [any_spec()] * count,
        out_specs=[vmem_spec()] * 4 + [any_spec()] * 2,
        scratch_shapes=[
            pltpu.VMEM((total, width), BF),
            pltpu.VMEM((max(lay.taps), most, width), BF),
            pltpu.SemaphoreType.DMA((4,)),
        ],
        compiler_params=pltpu.CompilerParams(vmem_limit_bytes=VMEM),
        cost_estimate=cost(2 * most * width * total, 4 * total * width),
        name="shrink_forward",
    )(where, kinds_own, kinds_other, gain, low_own, low_other, *si.arrays)


def stage(lay, b, copies):
    def view(ref, first, rows, middle):
        return ref.at[:, pl.ds(first, rows), :] if middle else ref.at[pl.ds(first, rows)]

    def run(i):
        for source, target, rows, sems, middle in copies:
            yield pltpu.make_async_copy(
                view(source, i * 4 * rows, 4 * rows, middle),
                view(target, i * 4 * rows, 4 * rows, middle),
                sems.at[i],
            )

    def start(i):
        for c in run(i):
            c.start()

    def wait(i):
        for c in run(i):
            c.wait()

    return start, wait


def grow_forward(lay, where, gf, part, mixed, season, order, gain):
    width = lay.width
    groups = season.shape[0]
    length = lay.length
    pieces_in = isinstance(gf, Pieces)
    arrays = gf.arrays if pieces_in else [gf]
    count = len(arrays)
    most = max(STRIDES) * width
    runs = max(STRIDES) // 4

    def kernel(where, gain_ref, order_ref, mixed_ref, season_in, *refs):
        pieces, rest = refs[:count], refs[count:]
        outs, up_out = rest[:groups], rest[groups]
        scratch = rest[groups + 1 + pieces_in :]
        rows_ref, whole, season_ref, up_ref, in_sems, w_sems, up_sems, sems = scratch

        def body(b):
            npos = lay.npos[b]
            m = groups * npos
            copies = [(season_in, season_ref, npos, in_sems, True)]
            if not pieces_in:
                copies.append((pieces[0], whole, width, w_sems, False))
            start, wait = stage(lay, b, copies)
            up_start, up_wait = stage(lay, b, [(up_ref, up_out, npos, up_sems, True)])
            if pieces_in:
                load_g(lay, b, where, gf.meta, pieces, whole, sems.at[0])
            for i in range(STRIDES[b] // 4):
                start(i)
            if pieces_in:
                wait_rows(whole, 0, STRIDES[b] * width, sems.at[0])
                pltpu.make_async_copy(whole, rest[groups + 1], sems.at[1]).start()
            x = mixed_ref[part * m : (part + 1) * m]
            gain = gain_ref[...]
            for s in range(STRIDES[b]):
                if s % 4 == 0:
                    wait(s // 4)
                cut = slice(s * npos, (s + 1) * npos)
                up = jnp.tanh(dot(x, whole[s * width : (s + 1) * width]))
                up_ref[:, cut, :] = up.reshape(groups, npos, width)
                hat, _ = normal(up + season_ref[:, cut, :].reshape(m, width))
                rows_ref[:, cut, :] = (hat * gain).astype(BF).reshape(groups, npos, width)
                if s % 4 == 3:
                    up_start(s // 4)
            for g in range(groups):
                outs[g][0] = dot_w(order_ref[...], rows_ref[g]).astype(BF)
            for i in range(STRIDES[b] // 4):
                up_wait(i)
            if pieces_in:
                pltpu.make_async_copy(whole, rest[groups + 1], sems.at[1]).wait()

        by_branch(where, body)

    shapes = [jax.ShapeDtypeStruct((1, length, width), BF)] * groups
    shapes.append(jax.ShapeDtypeStruct((groups, length, width), F32))
    if pieces_in:
        shapes.append(jax.ShapeDtypeStruct((most, width), BF))
    return pl.pallas_call(
        kernel,
        out_shape=shapes,
        in_specs=[smem_spec()] + [vmem_spec()] * 3 + [any_spec()] * (1 + count),
        out_specs=[vmem_spec()] * groups + [any_spec()] * (1 + pieces_in),
        scratch_shapes=[
            pltpu.VMEM((groups, length, width), BF),
            pltpu.VMEM((most, width), BF),
            pltpu.VMEM((groups, length, width), F32),
            pltpu.VMEM((groups, length, width), F32),
        ]
        + [pltpu.SemaphoreType.DMA((runs,))] * 3
        + [pltpu.SemaphoreType.DMA((2,))],
        compiler_params=pltpu.CompilerParams(vmem_limit_bytes=VMEM),
        cost_estimate=cost(
            2 * groups * length * width * (width + length),
            2 * most * width + 14 * groups * length * width,
        ),
        name="grow_forward",
    )(where, gain, order, mixed, season, *arrays)


def grow_backward(lay, where, whole, grads, up, season, order, gain):
    width = lay.width
    groups = season.shape[0]
    length = lay.length
    most = groups * max(lay.npos)
    runs = max(STRIDES) // 4

    def kernel(where, gain_ref, order_ref, up_in, season_in, whole_in, *refs):
        grad_refs, rest = refs[:groups], refs[groups:]
        pre_ref, back_ref, sum_out, gain_grad_ref = rest[:4]
        rows_ref, whole, up_ref, season_ref, sum_ref = rest[4:9]
        sems, sum_sems = rest[9:12], rest[12]

        def body(b):
            npos = lay.npos[b]
            m = groups * npos
            start, wait = stage(
                lay,
                b,
                [
                    (up_in, up_ref, npos, sems[0], True),
                    (season_in, season_ref, npos, sems[1], True),
                    (whole_in, whole, width, sems[2], False),
                ],
            )
            sum_start, sum_wait = stage(lay, b, [(sum_ref, sum_out, npos, sum_sems, True)])
            for i in range(STRIDES[b] // 4):
                start(i)
            for g in range(groups):
                rows_ref[g] = dot(order_ref[...], grad_refs[g][...]).astype(BF)
            total = jnp.zeros((m, width), F32)
            gains = jnp.zeros((1, width), F32)
            for s in range(STRIDES[b]):
                if s % 4 == 0:
                    wait(s // 4)
                cut = slice(s * npos, (s + 1) * npos)
                up = up_ref[:, cut, :].reshape(m, width)
                hat, inverse = normal(up + season_ref[:, cut, :].reshape(m, width))
                g = rows_ref[:, cut, :].reshape(m, width).astype(F32)
                gains += jnp.sum(g * hat, axis=0, keepdims=True)
                d = normal_back(g, hat, inverse, gain_ref[...])
                sum_ref[:, cut, :] = d.reshape(groups, npos, width)
                pre = (d * (1.0 - up * up)).astype(BF)
                pre_ref[:, cut, :] = pre.reshape(groups, npos, width)
                total += dot_t(pre, whole[s * width : (s + 1) * width])
                if s % 4 == 3:
                    sum_start(s // 4)
            back_ref[:m] = total
            gain_grad_ref[...] = gains
            for i in range(STRIDES[b] // 4):
                sum_wait(i)

        by_branch(where, body)

    return pl.pallas_call(
        kernel,
        out_shape=[
            jax.ShapeDtypeStruct((groups, length, width), BF),
            jax.ShapeDtypeStruct((most, width), F32),
            jax.ShapeDtypeStruct((groups, length, width), F32),
            jax.ShapeDtypeStruct((1, width), F32),
        ],
        in_specs=[smem_spec()] + [vmem_spec()] * 2 + [any_spec()] * 3 + [vmem_spec()] * groups,
        out_specs=[vmem_spec(), vmem_spec(), any_spec(), vmem_spec()],
        scratch_shapes=[
            pltpu.VMEM((groups, length, width), BF),
            pltpu.VMEM((whole.shape[0], width), BF),
            pltpu.VMEM((groups, length, width), F32),
            pltpu.VMEM((groups, length, width), F32),
            pltpu.VMEM((groups, length, width), F32),
        ]
        + [pltpu.SemaphoreType.DMA((runs,))] * 4,
        compiler_params=pltpu.CompilerParams(vmem_limit_bytes=VMEM),
        cost_estimate=cost(
            2 * groups * length * width * (width + length),
            2 * whole.shape[0] * width + 18 * groups * length * width,
        ),
        name="grow_backward",
    )(where, gain, order, up, season, whole, *grads)


class Outlet:
    def __init__(self, n, rows, width):
        self.n, self.rows, self.width = n, rows, width
        self.bounds = [(0, 1)] + [(i, i + 2) for i in range(1, n - 1, 2)] + [(n - 1, n)]

    def shapes(self):
        sizes = [hi - lo for lo, hi in self.bounds] + [self.n]
        return [jax.ShapeDtypeStruct((c, self.rows, self.width), BF) for c in sizes]

    def scratch(self):
        return [
            pltpu.VMEM((2, self.n, self.rows, self.width), BF),
            pltpu.SemaphoreType.DMA((1 + len(self.bounds),)),
        ]

    def copies(self, held_ref, outs, sems):
        found = []
        for i, (lo, hi) in enumerate(self.bounds):
            source = held_ref.at[0, pl.ds(lo, hi - lo)]
            found.append(pltpu.make_async_copy(source, outs[i], sems.at[i]))
        last = len(self.bounds)
        found.append(pltpu.make_async_copy(held_ref.at[1], outs[last], sems.at[last]))
        return found

    def flush(self, held_ref, outs, sems):
        for c in self.copies(held_ref, outs, sems):
            c.start()
        for c in self.copies(held_ref, outs, sems):
            c.wait()


def grow_weight(lay, where, places, mixed, pre_own, pre_other, outlet):
    n, width, k = lay.n, lay.width, lay.k
    groups = pre_own.shape[0]
    made = len(outlet.shapes())

    def kernel(where, places_ref, mixed_ref, own_ref, other_ref, *refs):
        outs, (out_ref, sems) = refs[:made], refs[made:]

        def body(b):
            npos = lay.npos[b]
            most = 2 * groups * max(lay.npos)
            x = filled(mixed_ref[: 2 * groups * npos], most)
            steps = STRIDES[b] // 2
            for s in range(STRIDES[b]):
                d = dot_w(x, filled(step_rows(own_ref, other_ref, s, npos), most)).astype(BF)
                side = jnp.where(where[1] == s // steps, 0, 1)
                at = (s % steps) * k
                for shard in range(n):
                    out_ref[side, places_ref[shard], at : at + k, :] = d[shard * k : (shard + 1) * k]
            rest = lay.g_half - steps * k
            if rest:
                out_ref[:, :, steps * k :, :] = jnp.zeros((2, n, rest, width), BF)

        by_branch(where, body)
        outlet.flush(out_ref, outs, sems)

    return pl.pallas_call(
        kernel,
        out_shape=outlet.shapes(),
        in_specs=[smem_spec(), smem_spec()] + [vmem_spec()] * 3,
        out_specs=[any_spec()] * made,
        scratch_shapes=outlet.scratch(),
        compiler_params=pltpu.CompilerParams(vmem_limit_bytes=VMEM),
        cost_estimate=cost(4 * groups * lay.length * width * width, 2 * 2 * n * lay.g_half * width),
        name="grow_weight",
    )(where, places, mixed, pre_own, pre_other)


def shrink_backward(lay, where, whole, back_own, back_other, shrunk, iso, age, gain):
    width = lay.width
    most = shrunk.shape[0]

    def kernel(where, age_ref, gain_ref, b0, b1, shrunk_ref, iso_ref, whole_in, *refs):
        pre_ref, iso_pre_ref, gain_grad_ref, whole, sem = refs

        def body(b):
            npos, taps = lay.npos[b], lay.taps[b]
            base = lay.shrink[b]
            source = whole_in.at[pl.ds(base, lay.iso[b])]
            fetch = pltpu.make_async_copy(source, whole.at[pl.ds(0, lay.iso[b])], sem)
            fetch.start()
            m = (most // max(lay.npos)) * npos
            mixed_back = jnp.concatenate([b0[: m // 2], b1[: m // 2]], axis=0)
            shrunk, iso = shrunk_ref[:m], iso_ref[:m]
            hat, inverse = normal(iso + shrunk)
            gain_grad_ref[...] = jnp.sum(mixed_back * hat, axis=0, keepdims=True)
            joint = normal_back(mixed_back, hat, inverse, gain_ref[...])
            iso_pre = (joint * (1.0 - iso * iso)).astype(BF)
            iso_pre_ref[:m] = iso_pre
            age = age_ref[:m]
            total = joint
            fetch.wait()
            for r in range(min(8, taps)):
                both = None
                for k in range(r, taps, 8):
                    tap = taps - 1 - k
                    back = dot_t(iso_pre, whole[tap * width : (tap + 1) * width])
                    if k:
                        back = jnp.where(age >= k, back, 0.0)
                    if k >= 8:
                        back = jnp.concatenate([back[k - r :], jnp.zeros_like(back[: k - r])])
                    both = back if both is None else both + back
                total += pltpu.roll(both, m - r, 0) if r else both
            pre_ref[:m] = (total * (1.0 - shrunk * shrunk)).astype(BF)

        by_branch(where, body)

    return pl.pallas_call(
        kernel,
        out_shape=[
            jax.ShapeDtypeStruct((most, width), BF),
            jax.ShapeDtypeStruct((most, width), BF),
            jax.ShapeDtypeStruct((1, width), F32),
        ],
        in_specs=[smem_spec()] + [vmem_spec()] * 6 + [any_spec()],
        out_specs=[vmem_spec()] * 3,
        scratch_shapes=[pltpu.VMEM((max(lay.iso), width), BF), pltpu.SemaphoreType.DMA],
        compiler_params=pltpu.CompilerParams(vmem_limit_bytes=VMEM),
        cost_estimate=cost(2 * most * width * lay.iso[0], 2 * lay.iso[0] * width),
        name="shrink_backward",
    )(where, age, gain, back_own, back_other, shrunk, iso, whole)


def shrink_weight(lay, where, places, iso_pre, pre, stacked, low_own, low_other, gains, outlet):
    width = lay.width
    most = stacked.shape[1]
    made = len(outlet.shapes())

    def kernel(where, places_ref, gains_ref, iso_pre_ref, pre_ref, own_ref, other_ref, *refs):
        stacked_in, outs = refs[0], refs[1 : 1 + made]
        grad_ref, sems, taps_ref, taps_sem = refs[1 + made :]
        fetch = pltpu.make_async_copy(stacked_in, taps_ref, taps_sem)
        fetch.start()
        extra = gains_ref[...].astype(BF)
        for side in range(2):
            for place in range(lay.n):
                grad_ref[side, place, lay.si_half :, :] = extra

        def body(b):
            npos, taps = lay.npos[b], lay.taps[b]
            m = (most // max(lay.npos)) * npos

            def store(part, row, d):
                first, half, _, shard = part
                d = d.astype(BF)
                lo = row
                while lo < row + width:
                    dp, h, r = lo // shard, (lo % shard) // half, lo % half
                    rows = min(half - r, row + width - lo)
                    side = jnp.where(where[1] == h, 0, 1)
                    grad_ref[side, places_ref[dp], first + r : first + r + rows, :] = d[
                        lo - row : lo - row + rows
                    ]
                    lo += rows

            part_s, part_i = lay.si_parts(b)
            iso_pre, pre = filled(iso_pre_ref[:m], most), filled(pre_ref[:m], most)
            for s in range(STRIDES[b]):
                x = filled(step_rows(own_ref, other_ref, s, npos), most)
                store(part_s, s * width, dot_w(x, pre))
            fetch.wait()
            for k in range(taps):
                store(part_i, (taps - 1 - k) * width, dot_w(taps_ref[k], iso_pre))

        by_branch(where, body)
        outlet.flush(grad_ref, outs, sems)

    return pl.pallas_call(
        kernel,
        out_shape=outlet.shapes(),
        in_specs=[smem_spec(), smem_spec()] + [vmem_spec()] * 5 + [any_spec()],
        out_specs=[any_spec()] * made,
        scratch_shapes=outlet.scratch()
        + [pltpu.VMEM(stacked.shape, BF), pltpu.SemaphoreType.DMA],
        compiler_params=pltpu.CompilerParams(vmem_limit_bytes=VMEM),
        cost_estimate=cost(2 * most * width * (lay.iso[0] + lay.shrink[0]), 30 * MIB),
        name="shrink_weight",
    )(where, places, gains, iso_pre, pre, low_own, low_other, stacked)


def season_backward(lay, where, whole, pre, sum_own, sum_other, order):
    width, length = lay.width, lay.length
    groups = sum_own.shape[0]
    most = max(lay.shrink)

    def kernel(where, order_ref, pre_ref, own_ref, other_ref, whole_in, *refs):
        outs, (whole, rows_ref, sem) = refs[:3], refs[3:]

        def body(b):
            fetch = pltpu.make_async_copy(
                whole_in.at[pl.ds(0, lay.shrink[b])], whole.at[pl.ds(0, lay.shrink[b])], sem
            )
            fetch.start()
            npos = lay.npos[b]
            m = groups * npos
            fetch.wait()
            for s in range(STRIDES[b]):
                cut = slice(s * npos, (s + 1) * npos)
                d = dot_t(pre_ref[: 2 * m], whole[s * width : (s + 1) * width])
                rows_ref[:groups, cut, :] = (
                    d[:m].reshape(groups, npos, width) + own_ref[:, cut, :]
                ).astype(BF)
                rows_ref[groups:, cut, :] = (
                    d[m:].reshape(groups, npos, width) + other_ref[:, cut, :]
                ).astype(BF)

        by_branch(where, body)
        for g in range(groups):
            outs[0][g] = dot_w(order_ref[...], rows_ref[g]).astype(BF)
            ref, i = (outs[1], 0) if g == 0 else (outs[2], g - 1)
            ref[i] = dot_w(order_ref[...], rows_ref[groups + g]).astype(BF)

    return pl.pallas_call(
        kernel,
        out_shape=[
            jax.ShapeDtypeStruct((c, length, width), BF) for c in (groups, 1, groups - 1)
        ],
        in_specs=[smem_spec()] + [vmem_spec()] * 4 + [any_spec()],
        out_specs=[vmem_spec()] * 3,
        scratch_shapes=[
            pltpu.VMEM((most, width), BF),
            pltpu.VMEM((2 * groups, length, width), BF),
            pltpu.SemaphoreType.DMA,
        ],
        compiler_params=pltpu.CompilerParams(vmem_limit_bytes=VMEM),
        cost_estimate=cost(
            4 * groups * length * width * (width + length),
            2 * most * width + 24 * groups * length * width,
        ),
        name="season_backward",
    )(where, order, pre, sum_own, sum_other, whole)


def ring_add(jobs):
    specs, arrays, shapes = [], [], []
    for first, rows, terms in jobs:
        width = terms[0][0].shape[-1]
        shapes.append(jax.ShapeDtypeStruct((rows, width), BF))
        for array, place, _ in terms:
            arrays.append(array)
            if place is None:
                specs.append(vmem_spec())
            else:
                index = functools.partial(lambda p, q, g: (p, q, 0), place, first // rows)
                specs.append(pl.BlockSpec((1, rows, width), index))

    def kernel(*refs):
        ins, outs = list(refs[: len(arrays)]), refs[len(arrays) :]
        for (first, rows, terms), out in zip(jobs, outs):
            mine = [ins.pop(0) for _ in terms]
            for r in range(0, rows, 16):
                total = None
                for (array, place, at), ref in zip(terms, mine):
                    count = rows if place is not None else array.shape[0]
                    if not at <= r < at + count:
                        continue
                    v = ref[0, r : r + 16, :] if place is not None else ref[r - at : r - at + 16, :]
                    v = v.astype(F32)
                    total = v if total is None else total + v
                out[r : r + 16, :] = total.astype(BF)

    moved = sum(2 * s.shape[0] * s.shape[1] for s in shapes) * 4
    return pl.pallas_call(
        kernel,
        grid=(1,),
        out_shape=shapes,
        in_specs=specs,
        out_specs=[vmem_spec()] * len(shapes),
        compiler_params=pltpu.CompilerParams(vmem_limit_bytes=VMEM),
        cost_estimate=cost(0, moved),
        name="ring_add",
    )(*arrays)


def plain_add(jobs):
    found = []
    for first, rows, terms in jobs:
        total, late = None, None
        for array, place, at in terms:
            v = array if place is None else array[place, first : first + rows]
            v = v.astype(F32)
            if v.shape[0] < rows:
                late = (v, at)
            else:
                total = v if total is None else total + v
        if late is not None:
            v, at = late
            lo, hi = total[:at], total[at + v.shape[0] :]
            total = jnp.concatenate([lo, total[at : at + v.shape[0]] + v, hi])
        found.append(total.astype(BF))
    return found


def give_out(lay, member_ids, mine, over_y, sibling, sibling_over_y):
    n, width = lay.n, lay.width

    def kernel(where, mine, over_y, sibling, sibling_over_y, *outs):
        for y in range(2):
            for core in range(2):

                @pl.when((where[0] == y) & (where[1] == core))
                def _(y=y, core=core):
                    for b in range(2):
                        own, other = (mine, sibling) if b == y else (over_y, sibling_over_y)
                        for i, (first, half, _, _) in enumerate(lay.si_parts(b)):
                            for h in range(2):
                                source = own if h == core else other
                                outs[2 * i + b][h * half : (h + 1) * half, :] = source[
                                    first : first + half, :
                                ].astype(F32)

    return pl.pallas_call(
        kernel,
        out_shape=[
            jax.ShapeDtypeStruct((rows // n, width), F32) for rows in (*lay.shrink, *lay.iso)
        ],
        in_specs=[smem_spec()] + [vmem_spec()] * 4,
        out_specs=[vmem_spec()] * 4,
        compiler_params=pltpu.CompilerParams(vmem_limit_bytes=VMEM),
        cost_estimate=cost(0, 12 * MIB),
        name="give_out",
    )(member_ids, mine, over_y, sibling, sibling_over_y)


def dense_whole(lay, where, gf):
    width, ff = lay.width, lay.width * lay.chunks
    count = len(gf.arrays)
    shapes = ((2 * width, width), (ff, width), (width, width), (width, ff))

    def kernel(where, *refs):
        pieces, wholes, sems = refs[:count], refs[count:-1], refs[-1]
        for c in range(2):
            pl.when(where[1] == c)(
                functools.partial(load_f, lay, c, where, gf.meta, pieces, wholes, sems)
            )
        for t in range(4):
            wait_rows(wholes[t], 0, shapes[t][0], sems.at[t])

    return pl.pallas_call(
        kernel,
        out_shape=[jax.ShapeDtypeStruct(v, BF) for v in shapes],
        in_specs=[smem_spec()] + [any_spec()] * count,
        out_specs=[vmem_spec()] * 4,
        scratch_shapes=[pltpu.SemaphoreType.DMA((4,))],
        compiler_params=pltpu.CompilerParams(vmem_limit_bytes=VMEM),
        cost_estimate=cost(0, 4 * sum(r * c for r, c in shapes)),
        name="dense_whole",
    )(where, *gf.arrays)


def dense(lay, where, tile, wholes, mine, received, trend_low, out_grad, gain_middle, gain_output):
    width, length, chunks = lay.width, lay.length, lay.chunks
    cuts = 2
    part = length // cuts
    ff = width * chunks
    strip = 32

    def kernel(where, tile_ref, gm_ref, go_ref, merge, contract, trend, expand, *refs):
        mine_ref, got_ref, trend_ref, grad_ref = refs[:4]
        (hid_ref, hg_ref, ml_ref, ll_ref, mg_ref, tb_ref, out_ref, jm_ref, js_ref) = refs[4:13]
        gains_ref, h_ref, slope_ref, a_ref, b_ref, c_ref = refs[13:]
        b = where[0]
        gm, go = gm_ref[...], go_ref[...]
        at_mine = pl.multiple_of(b * width, width)
        at_other = pl.multiple_of((1 - b) * width, width)

        def strips(body):
            for r in range(0, part, strip):
                body(slice(r, r + strip))

        a_ref[...] = dot(mine_ref[...], merge[pl.ds(at_mine, width)]) + dot(
            got_ref[...], merge[pl.ds(at_other, width)]
        )
        inverses = {}

        def middle_norm(r):
            hat, inverses[r.start] = normal(a_ref[r, :])
            a_ref[r, :] = hat
            ml_ref[r, :] = (hat * gm).astype(BF)

        strips(middle_norm)
        for j in range(chunks):
            cols = slice(j * width, (j + 1) * width)
            h_ref[:, cols] = dot(ml_ref[...], expand[:, cols])

            def gelu(r, cols=cols):
                h = h_ref[r, cols]
                phi, dens = erf_pair(h)
                hid_ref[r, cols] = (h * phi).astype(BF)
                slope_ref[r, cols] = phi + dens

            strips(gelu)
        b_ref[...] = dot(hid_ref[...], contract[...])
        c_ref[...] = dot(trend_ref[0], trend[...])
        sums = [jnp.zeros((8, width), F32), jnp.zeros((8, width), F32)]

        def rows8(v):
            return jnp.sum(v.reshape(strip // 8, 8, width), axis=0)

        def output_norm(r):
            hat, inverse = normal(a_ref[r, :] * gm + b_ref[r, :])
            out_ref[r, :] = (hat * go + c_ref[r, :]).astype(BF)
            g = grad_ref[0, r, :].astype(F32)
            sums[1] += rows8(g * hat)
            d = normal_back(g, hat, inverse, go)
            b_ref[r, :] = d
            ll_ref[r, :] = d.astype(BF)

        strips(output_norm)
        tb_ref[...] = dot_t(grad_ref[0], trend[...])
        for j in range(chunks):
            cols = slice(j * width, (j + 1) * width)
            h_ref[:, cols] = dot_t(ll_ref[...], contract[cols])

            def gelu_back(r, cols=cols):
                hg_ref[r, cols] = (h_ref[r, cols] * slope_ref[r, cols]).astype(BF)

            strips(gelu_back)
        c_ref[...] = dot_t(hg_ref[...], expand[...])

        def middle_back(r):
            hat = a_ref[r, :]
            back = b_ref[r, :] + c_ref[r, :]
            sums[0] += rows8(back * hat)
            mg_ref[r, :] = normal_back(back, hat, inverses[r.start], gm).astype(BF)

        strips(middle_back)
        jm_ref[...] = dot_t(mg_ref[...], merge[pl.ds(at_mine, width)]).astype(BF)
        js_ref[...] = dot_t(mg_ref[...], merge[pl.ds(at_other, width)]).astype(BF)

        @pl.when(pl.program_id(0) == 0)
        def _():
            gains_ref[...] = jnp.zeros_like(gains_ref)

        gains_ref[0:1, :] += jnp.sum(sums[0], axis=0, keepdims=True)
        gains_ref[1:2, :] += jnp.sum(sums[1], axis=0, keepdims=True)

    of_tile = pl.BlockSpec((1, part, width), lambda i, w, t: (t[0], i, 0))
    alone = pl.BlockSpec((part, width), lambda i, w, t: (i, 0))
    shapes = [(ff, BF)] * 2 + [(width, BF)] * 3 + [(width, F32)] + [(width, BF)] * 3
    return pl.pallas_call(
        kernel,
        grid_spec=pltpu.PrefetchScalarGridSpec(
            num_scalar_prefetch=2,
            grid=(cuts,),
            in_specs=[vmem_spec()] * 6 + [alone, alone, of_tile, of_tile],
            out_specs=[pl.BlockSpec((part, c), lambda i, w, t: (i, 0)) for c, _ in shapes]
            + [pl.BlockSpec((2, width), lambda i, w, t: (0, 0))],
            scratch_shapes=[pltpu.VMEM((part, ff), F32)] * 2 + [pltpu.VMEM((part, width), F32)] * 3,
        ),
        out_shape=[jax.ShapeDtypeStruct((length, w), t) for w, t in shapes]
        + [jax.ShapeDtypeStruct((2, width), F32)],
        compiler_params=pltpu.CompilerParams(vmem_limit_bytes=VMEM),
        cost_estimate=cost(
            2 * length * width * (4 * width + 4 * ff + 2 * width), 12 * MIB + 20 * MIB
        ),
        name="dense",
    )(where, tile, gain_middle, gain_output, *wholes, mine, received, trend_low, out_grad)


def dense_weights(lay, where, places, mine, received, trend_low, out_grad, saved, outlet):
    n, width, chunks, length = lay.n, lay.width, lay.chunks, lay.length
    groups = len(saved)
    made = len(outlet.shapes())
    base = lay.g_half
    (_, contract, _, _), (merge_at, merge, _, _) = lay.f_parts(0)
    merge_at -= base

    def kernel(where, places_ref, *refs):
        refs = list(refs)

        def take(count):
            out = refs[:count]
            del refs[:count]
            return out

        middle, lifted = take(groups), take(groups)
        hidden, slopes = take(groups), take(groups)
        late = take(3 * groups) + take(2)
        outs = take(made)
        out_ref, sems, mine_ref, got_ref, grad_ref, trend_ref, up_ref, late_sems = refs
        core, q = where[1], pl.program_id(0)

        def fetches():
            targets = [r.at[g] for r in (mine_ref, got_ref, grad_ref) for g in range(groups)]
            targets += [trend_ref, up_ref]
            return [
                pltpu.make_async_copy(x, y, late_sems.at[i])
                for i, (x, y) in enumerate(zip(late, targets))
            ]

        def side(h):
            return jnp.where(core == h, 0, 1)

        def total(xs, gs):
            d = None
            for x, g in zip(xs, gs):
                v = dot_w(x, g)
                d = v if d is None else d + v
            return d.astype(BF)

        @pl.when(q == 0)
        def _():
            for f in fetches():
                f.start()
            if merge_at + merge < lay.f_half:
                out_ref[side(0), :, merge_at + merge :, :] = jnp.zeros(
                    (n, lay.f_half - merge_at - merge, width), BF
                )

        d = total([r[...] for r in hidden], [r[...] for r in lifted])
        each = width // contract
        for i in range(each):
            out_ref[side(0), places_ref[q * each + i], 0:contract, :] = d[
                i * contract : (i + 1) * contract
            ]
        d = total([r[...] for r in middle], [r[...] for r in slopes])
        at = pl.ds(pl.multiple_of((1 + q) * lay.k, 16), lay.k)
        for dp in range(n):
            out_ref[side(1), places_ref[dp], at, :] = d[dp * lay.k : (dp + 1) * lay.k]

        @pl.when(q == chunks - 1)
        def _():
            for f in fetches():
                f.wait()
            d = total([trend_ref[g] for g in range(groups)], [up_ref[g] for g in range(groups)])
            for dp in range(n):
                out_ref[side(1), places_ref[dp], 0 : lay.k, :] = d[dp * lay.k : (dp + 1) * lay.k]
            each = width // merge
            for ref, first in ((mine_ref, where[0]), (got_ref, 1 - where[0])):
                d = total([ref[g] for g in range(groups)], [grad_ref[g] for g in range(groups)])
                for i in range(each):
                    out_ref[side(0), places_ref[first * each + i], merge_at : merge_at + merge, :] = d[
                        i * merge : (i + 1) * merge
                    ]
            used = (1 + chunks) * lay.k
            if used < lay.f_half:
                out_ref[side(1), :, used:, :] = jnp.zeros((n, lay.f_half - used, width), BF)
            outlet.flush(out_ref, outs, sems)

    whole = pl.BlockSpec((length, width), lambda q: (0, 0))
    column = pl.BlockSpec((length, width), lambda q: (0, q))
    arrays = [k[0] for k in saved] + [k[3] for k in saved]
    arrays += [k[1] for k in saved] + [k[2] for k in saved]
    arrays += [v.reshape(length, width) for v in mine] + list(received) + [k[4] for k in saved]
    arrays += [trend_low, out_grad]
    ff = chunks * width
    square = pltpu.VMEM((groups, length, width), BF)
    return pl.pallas_call(
        kernel,
        grid=(chunks,),
        out_shape=outlet.shapes(),
        in_specs=[smem_spec(), smem_spec()]
        + [whole] * (2 * groups)
        + [column] * (2 * groups)
        + [any_spec()] * (3 * groups + 2),
        out_specs=[any_spec()] * made,
        scratch_shapes=outlet.scratch()
        + [square] * 5
        + [pltpu.SemaphoreType.DMA((3 * groups + 2,))],
        compiler_params=pltpu.CompilerParams(vmem_limit_bytes=VMEM),
        cost_estimate=cost(
            2 * groups * length * width * (2 * width + 2 * ff + width), 45 * MIB
        ),
        name="dense_weights",
    )(where, places, *arrays)


def exchange(axis, size, step):
    return lambda v: lax.ppermute(v, axis, [(i, i ^ step) for i in range(size)])


def on_device(
    n,
    series_in,
    block_kinds,
    out_grad,
    fine_shrink,
    coarse_shrink,
    fine_isometric,
    coarse_isometric,
    fine_grow,
    coarse_grow,
    merge_weight,
    expand_weight,
    contract_weight,
    trend_weight,
    branch_gain,
    middle_gain,
    output_gain,
):
    ring = Ring(n)
    member = lax.axis_index("group")
    core, y = member % 2, member // 2
    block_count = block_kinds.shape[0]
    width = series_in.shape[1]
    block_len = series_in.shape[0] // block_count
    groups = block_count // GROUP
    lay = Layout(n, width, block_len, expand_weight.shape[1])
    length = lay.length
    share = branch_gain.shape[0]
    fine = y == 0

    def right(v):
        return lax.ppermute(v, "dp", ring.right)

    def left(v):
        return lax.ppermute(v, "dp", ring.left)

    shards = (fine_shrink, coarse_shrink, fine_isometric, coarse_isometric)
    shards += (fine_grow, coarse_grow)
    dense_shards = (contract_weight, merge_weight, trend_weight, expand_weight)
    member_ids = jnp.stack([y, core]).astype(jnp.int32)
    own = half_of(lay, member_ids, False, *shards, dense_shards)
    offsets = [0]
    pieces = Pieces()
    for k in range(1, n // 2):
        offsets += [-k, k]
    offsets.append(n // 2)

    def source(offset):
        return offsets.index(offset if abs(offset) < n // 2 else n // 2)

    where = jnp.stack([y, core] + [ring.index(o) for o in offsets]).astype(jnp.int32)

    x_own = series_in.reshape(groups, length, width)
    x_other = []
    last = n // 2

    def prepare_own(kinds, x):
        rows = jnp.arange(length, dtype=jnp.int32)
        npos = jnp.where(fine, lay.npos[0], lay.npos[1])
        stride = jnp.where(fine, STRIDES[0], STRIDES[1])
        step = ((rows % npos) * stride + rows // npos)[:, None]
        return (step, *season_kernel(lay, kinds, step, x, True))

    def prepare_other(step, kinds, *xs):
        kinds = kinds.astype(jnp.int32)
        return (kinds, *season_kernel(lay, kinds, step, jnp.stack(xs), False))

    def spread_gains(*parts):
        parts = jnp.stack(parts).astype(F32)
        return lax.dynamic_update_slice(
            jnp.zeros((3, width), F32), parts, (jnp.int32(0), ring.me * share)
        )

    doublings = []
    size = 1
    while size < n:
        doublings.append(size)
        size *= 2
    gains = spread_gains(branch_gain, middle_gain, output_gain)
    hops = [exchange("dp", n, d) for d in doublings]

    def hop(sends):
        if hops:
            sends["gain"] = (gains, hops.pop(0))

    whole_r = whole_l = own
    half_rows = (lay.g_half + lay.f_half) // 2
    si_rows = lay.si_half // 2
    for t in range(1, last):
        sends = {"r": (whole_r, right), "l": (whole_l, left)}
        if t > 1:
            sends["cr"], sends["cl"] = (whole_r, swap_core), (whole_l, swap_core)
        if t <= groups:
            sends["x"] = (x_own[t - 1], swap_y)
        work, given = None, ()
        if t == 1:
            sends["k"] = (block_kinds.astype(F32), swap_y)
            hop(sends)
            work = lambda *v: (half_of(lay, member_ids, True, *v[:6], v[6:]),)
            given = (*shards, *dense_shards)
        elif t == 2:
            work, given = prepare_own, (block_kinds, x_own)
        arrived, done = slot(sends, work, given)
        if t == 1:
            kinds_other = arrived["k"]
            pieces.add(0, 0, 0, own)
            pieces.add(0, 1, 0, done[0])
        elif t == 2:
            step, season_own, low_own, own_counts, trend_low, order = done
        if "x" in arrived:
            x_other.append(arrived["x"])
        if "gain" in arrived:
            gains = gains + arrived["gain"]
        if t > 1:
            pieces.add(source(1 - t), 1, 0, arrived["cr"])
            pieces.add(source(t - 1), 1, 0, arrived["cl"])
        whole_r, whole_l = arrived["r"], arrived["l"]
        pieces.add(source(-t), 0, 0, whole_r)
        pieces.add(source(t), 0, 0, whole_l)
    middle = lay.si_half
    sends = {"r": (whole_r[:si_rows], right), "l": (whole_l[si_rows:middle], left)}
    sends["cr"], sends["cl"] = (whole_r, swap_core), (whole_l, swap_core)
    hop(sends)
    arrived, done = slot(sends, prepare_other, (step, kinds_other, *x_other))
    kinds_other, season_other, low_other = done
    if "gain" in arrived:
        gains = gains + arrived["gain"]
    pieces.add(source(1 - last), 1, 0, arrived["cr"])
    pieces.add(source(last - 1), 1, 0, arrived["cl"])
    si_r, si_l = arrived["r"], arrived["l"]
    pieces.add(source(last), 0, 0, si_r)
    pieces.add(source(last), 0, si_rows, si_l)
    sends = {"cr": (si_r, swap_core), "cl": (si_l, swap_core)}
    hop(sends)
    arrived, _ = slot(sends)
    if "gain" in arrived:
        gains = gains + arrived["gain"]
    pieces.add(source(last), 1, 0, arrived["cr"])
    pieces.add(source(last), 1, si_rows, arrived["cl"])
    for move_gains in hops:
        gains = gains + move_gains(gains)
    gain_b, gain_m, gain_o = gains[0:1], gains[1:2], gains[2:3]

    def run_shrink(low_own, low_other, *arrays):
        pieces.arrays = list(arrays)
        return shrink_forward(
            lay, where, pieces, low_own, low_other, block_kinds, kinds_other, gain_b
        )

    cut_at = middle + half_rows
    sends = {"r": (whole_r[middle:cut_at], right), "l": (whole_l[cut_at:], left)}
    arrived, done = slot(sends, run_shrink, (low_own, low_other, *pieces.arrays))
    shrunk, iso, mixed, age, stacked_rows, si_whole = done
    gf_r, gf_l = arrived["r"], arrived["l"]
    pieces.add(source(last), 0, middle, gf_r)
    pieces.add(source(last), 0, cut_at, gf_l)
    arrived, _ = slot({"cr": (gf_r, swap_core), "cl": (gf_l, swap_core)})
    pieces.add(source(last), 1, middle, arrived["cr"])
    pieces.add(source(last), 1, cut_at, arrived["cl"])
    gf = pieces

    *branch_other, up_other, g_whole = grow_forward(
        lay, where, gf, 1, mixed, season_other, order, gain_b
    )
    branch_other = [v.reshape(length, width) for v in branch_other]
    grads_in = out_grad.reshape(groups, length, width)

    def grow_own(mixed, g_whole, season_own, *arrays):
        gf.arrays = list(arrays)
        made = grow_forward(lay, where, g_whole, 0, mixed, season_own, order, gain_b)
        return (*made, *dense_whole(lay, where, gf))

    arrived, done = slot(
        {"b": (branch_other[0], swap_y)}, grow_own, (mixed, g_whole, season_own, *gf.arrays)
    )
    branch_own = [v.reshape(length, width) for v in done[:groups]]
    up_own, wholes = done[groups], done[groups + 1 :]
    received = [arrived["b"]]
    outs, back_own, back_got, waiting, trend_back, saved, dense_gains = [], [], [], [], [], [], None
    for g in range(groups):
        sends = {}
        if g + 1 < groups:
            sends["b"] = (branch_other[g + 1], swap_y)
        elif waiting:
            sends["j"] = (waiting.pop(0), swap_y)

        def run_dense(mine, got, *wholes, g=g):
            tile = jnp.full((1,), g, jnp.int32)
            return dense(
                lay, where, tile, wholes, mine, got, trend_low, grads_in, gain_m, gain_o
            )

        arrived, made = slot(sends, run_dense, (branch_own[g], received[g], *wholes))
        if "b" in arrived:
            received.append(arrived["b"])
        if "j" in arrived:
            back_got.append(arrived["j"])
        outs.append(made[6])
        back_own.append(made[7])
        waiting.append(made[8])
        trend_back.append(made[5])
        saved.append((made[2], made[0], made[1], made[3], made[4]))
        dense_gains = made[9] if dense_gains is None else dense_gains + made[9]
    series_out = jnp.concatenate(outs)

    ring_order = [n // 2]
    for k in range(n // 2 - 1, 0, -1):
        ring_order += [k, -k]
    ring_order.append(0)
    spot = jnp.zeros((n,), jnp.int32)
    for place, offset in enumerate(ring_order):
        spot = jnp.where(jnp.arange(n) == ring.index(offset), place, spot)

    f_outlet = Outlet(n, lay.f_half, width)
    g_outlet = Outlet(n, lay.g_half, width)
    s_outlet = Outlet(n, lay.si_half + 32, width)

    def run_dense_weights(*arrays):
        mine, got, flat = arrays[:groups], arrays[groups : 2 * groups], arrays[2 * groups :]
        kept = [flat[5 * g : 5 * g + 5] for g in range(groups)]
        return dense_weights(
            lay, where, spot, mine, list(got), trend_low, grads_in, kept, f_outlet
        )

    class Chain:
        def __init__(self, keep, got, halved=True):
            self.keep, self.got, self.halved = keep, got, halved
            self.step = last
            self.r = self.l = None
            self.half = got.shape[1] // 2

        def here(self, place, first=0, rows=None):
            array, i = (place + 1) // 2, 0 if place == 0 else (place - 1) % 2
            rows = self.got.shape[1] if rows is None else rows
            return (first, rows, [(self.keep[array], i, 0), (self.got, place, 0)])

        def jobs(self):
            k, h = self.step, self.half
            if k == 0:
                job = self.here(n - 1)
                job[2].extend([(self.r, None, 0), (self.l, None, 0)])
                return [job]
            if k == last:
                return [self.here(0, 0, h), self.here(0, h, h)] if self.halved else [self.here(0)]
            place = 1 + 2 * (last - 1 - k)
            a, b = self.here(place), self.here(place + 1)
            a[2].append((self.r, None, 0))
            if self.l is not None:
                b[2].append((self.l, None, h if k == last - 1 else 0))
            return [a, b]

    def back_of(grads, g_whole, up, season):
        return grow_backward(lay, where, g_whole, grads, up, season, order, gain_b)

    def weights_and_own(g_whole, up, season, *rest):
        return (
            *run_dense_weights(*rest[groups:]),
            *back_of(rest[:groups], g_whole, up, season),
        )

    sends = {"j%d" % i: (v, swap_y) for i, v in enumerate(waiting)}
    arrived, done = slot(
        sends,
        weights_and_own,
        (g_whole, up_own, season_own, *back_own, *branch_own, *received)
        + tuple(v for k in saved for v in k),
    )
    back_got += [arrived[k] for k in sends]
    steps = last + 1
    f_keep, f_give = done[:steps], done[steps]
    pre_own, mixed_back_own, sum_own, gains_own = done[steps + 1 :]
    chains = {}
    kept = {}
    finals = {}
    t = 0
    while True:
        active = {k: c for k, c in chains.items() if c.step > 0}
        finishing = [k for k, c in chains.items() if c.step == 0 and k + "mine" not in finals]
        if len(active) > 1:
            finishing = []
        if not active and not finishing and "smine" in finals:
            break
        sends, work, given = {}, None, ()
        names = [*active, *finishing]
        jobs = {name: chains[name].jobs() for name in names}
        adder = ring_add if t < 6 else plain_add
        summed = list(adder([j for name in names for j in jobs[name]])) if names else []
        for name in active:
            sends[name + "r"] = (summed.pop(0), right)
            if len(jobs[name]) > 1:
                sends[name + "l"] = (summed.pop(0), left)
        for name in finishing:
            mine = summed.pop(0)
            finals[name + "mine"] = mine
            sends[name + "y"] = (mine, swap_y)
            if name != "f":
                sends[name + "c"] = (mine, swap_core)
        for name in ("f", "g"):
            if name + "late" in finals and name + "sent" not in finals:
                sends[name + "d"] = (finals[name + "late"], swap_core)
                finals[name + "sent"] = True
        if t == 0:
            work = lambda g_whole, up, season, *grads: back_of(grads, g_whole, up, season)
            given = (g_whole, up_other, season_other, *back_got)
            sends["f0"] = (f_give, swap_core)
        elif t == 1:
            work = lambda *v: grow_weight(lay, where, spot, *v, g_outlet)
            given = (mixed, pre_own, pre_other)
        elif t == 2:
            work = lambda *v: shrink_backward(lay, where, *v, age, gain_b)
            given = (si_whole, mixed_back_own, mixed_back_other, shrunk, iso)
            sends["g"] = (g_give, swap_core)
        elif t == 3:
            work = lambda *v: shrink_weight(lay, where, spot, *v, s_outlet)
            given = (iso_pre, shrink_pre, stacked_rows, low_own, low_other, grad_gains)
        elif t == 4:
            work = lambda *v: season_backward(lay, where, *v, order)
            given = (si_whole, shrink_pre, sum_own, sum_other)
            sends["s0"] = (s_give, swap_core)
        if t in (5, 6):
            sends["x"] = (tail_sends[t - 5], swap_y)
        if "s" in finishing:
            work = lambda *v: (*finish(*v[6:]), *grow_out(*v[2:6]), *dense_out(*v[:2]))
            given = tuple(finals[k] for k in ("flate", "fd", "gmine", "gy", "gc", "gd"))
            given += (season_mine, own_counts, *trend_back, *tail)
        arrived, done = slot(sends, work, given)
        if t == 0:
            pre_other, mixed_back_other, sum_other, gains_other = done
            chains["f"] = Chain(f_keep, arrived["f0"], False)
        elif t == 1:
            *g_keep, g_give = done
            chains["g"] = None
        elif t == 2:
            shrink_pre, iso_pre, gains_si = done
            chains["g"] = Chain(g_keep, arrived["g"])
            grad_gains = jnp.concatenate(
                [gains_own + gains_other + gains_si, dense_gains, jnp.zeros((29, width), F32)]
            )
        elif t == 3:
            *s_keep, s_give = done
        elif t == 4:
            season_mine, *tail_sends = done
            tail = []
            chains["s"] = Chain(s_keep, arrived["s0"])

            def finish(season_mine, own_counts, *rest):
                backs, tail = rest[:groups], rest[groups:]
                total = season_mine.astype(F32) + jnp.concatenate(tail).astype(F32)
                rest = jnp.stack(backs) - total
                spread = (rest * (1.0 / WINDOW)).astype(BF)
                averaged = jnp.einsum(
                    "gij,gid->gjd", own_counts, spread, preferred_element_type=F32
                )
                return ((total + averaged).astype(BF),)

            def both(mine, other):
                return jnp.where(core == 0, mine, other), jnp.where(core == 0, other, mine)

            def grow_out(mine, over_y, sibling, sibling_over_y):
                found = []
                for b in range(2):
                    here = (y == 0) if b == 0 else (y == 1)
                    lo, hi = both(
                        jnp.where(here, mine, over_y), jnp.where(here, sibling, sibling_over_y)
                    )
                    cols = [v[r : r + k] for v in (lo, hi) for r, k, _ in lay.g_parts(b)]
                    found.append(jnp.concatenate(cols, axis=1).astype(F32))
                return found

            def dense_out(mine, other):
                lo, hi = both(mine, other)
                z = lay.g_half
                first = [lo[r - z : r - z + k].astype(F32) for r, k, _, _ in lay.f_parts(0)]
                rest = [hi[r - z : r - z + k].astype(F32) for r, k, _, _ in lay.f_parts(1)]
                return (*first, rest[0], jnp.concatenate(rest[1:], axis=1))

        if "x" in arrived:
            tail.append(arrived["x"])
        for name, chain in active.items():
            chain.r, chain.l = arrived[name + "r"], arrived.get(name + "l")
            chain.step -= 1
        for name in ("f", "g"):
            if name + "d" in arrived:
                finals[name + "d"] = arrived[name + "d"]
        for name in finishing:
            finals[name + "y"] = arrived[name + "y"]
            if name != "f":
                finals[name + "c"] = arrived[name + "c"]
            if name == "f":
                mine = finals["fmine"].astype(F32) + arrived["fy"].astype(F32)
                finals["flate"] = mine.astype(BF)
            elif name == "g":
                finals["glate"] = arrived["gy"]
            else:
                series_grad, *others = done
        if chains.get("g", 0) is None:
            del chains["g"]
        t += 1
    s_mine, s_y = finals["smine"], finals["sy"]
    s_core = (finals["sc"], swap_core(s_y))
    fine_grow_grad, coarse_grow_grad, contract_grad, merge_grad, trend_grad, expand_grad = others

    fine_shrink_grad, coarse_shrink_grad, fine_iso_grad, coarse_iso_grad = give_out(
        lay, member_ids, s_mine, s_y, *s_core
    )
    at = lay.si_half
    gain_grads = s_mine[at : at + 3].astype(F32) + s_y[at : at + 3].astype(F32)
    gain_grads = lax.dynamic_slice(gain_grads, (jnp.int32(0), ring.me * share), (3, share))
    return (
        series_out,
        series_grad.reshape(series_in.shape),
        fine_shrink_grad,
        coarse_shrink_grad,
        fine_iso_grad,
        coarse_iso_grad,
        fine_grow_grad,
        coarse_grow_grad,
        merge_grad,
        expand_grad,
        contract_grad,
        trend_grad,
        gain_grads[0],
        gain_grads[1],
        gain_grads[2],
    )


def solution(mesh):
    n = mesh.shape["dp"]
    rows = P(("dp", "group"), None)
    weight = P("dp", None)
    return jax.shard_map(
        lambda *args: on_device(n, *args),
        mesh=mesh,
        in_specs=(rows, P(("dp", "group")), rows) + (weight,) * 10 + (P("dp"),) * 3,
        out_specs=(rows, rows) + (weight,) * 10 + (P("dp"),) * 3,
        check_vma=False,
    )
```

```python
import functools
import math

import jax
import jax.numpy as jnp
from jax import lax
from jax.experimental import pallas as pl
from jax.experimental.pallas import tpu as pltpu
from jax.sharding import PartitionSpec as P

STRIDES = (12, 16)
WINDOW = 25
HALF = WINDOW // 2
GROUP = 4
BF = jnp.bfloat16
F32 = jnp.float32
MIB = 1024 * 1024
VMEM = 127 * MIB // 2
CORE_SWAP = ((0, 1), (1, 0), (2, 3), (3, 2))
Y_SWAP = ((0, 2), (2, 0), (1, 3), (3, 1))


class Layout:
    def __init__(self, n, width, block_len, ff):
        self.n, self.width, self.block_len = n, width, block_len
        self.length = GROUP * block_len
        self.taps = tuple(block_len // s for s in STRIDES)
        self.shrink = tuple(s * width for s in STRIDES)
        self.iso = tuple(p * width for p in self.taps)
        self.si_half = (self.shrink[0] + self.iso[0]) // (2 * n)
        self.k = width // n
        self.g_half = max(STRIDES) // 2 * self.k
        self.chunks = ff // width
        self.merge, self.contract = 2 * width // n, ff // n
        self.f_half = max(self.contract + self.merge, self.k * (1 + self.chunks))
        self.npos = tuple(GROUP * p for p in self.taps)

    def si_parts(self, b):
        s, i = self.shrink[b] // self.n, self.iso[b] // self.n
        return [(0, s // 2, 0, s), (s // 2, i // 2, self.shrink[b], i)]

    def g_parts(self, b):
        return [(j * self.k, self.k, j) for j in range(STRIDES[b] // 2)]

    def f_parts(self, h):
        base = self.g_half
        if h == 0:
            return [
                (base, self.contract, "contract", 0),
                (base + self.contract, self.merge, "merge", 0),
            ]
        found = [(base, self.k, "trend", 0)]
        for j in range(self.chunks):
            found.append((base + (1 + j) * self.k, self.k, "expand", j))
        return found


def held(*values):
    return lax.optimization_barrier(values)


class Ring:
    def __init__(self, n):
        self.n = n
        order = list(range(0, n, 2)) + list(range(n - 1, 0, -2))
        self.right = [(order[k], order[(k + 1) % n]) for k in range(n)]
        self.left = [(b, a) for a, b in self.right]
        d = lax.axis_index("dp")
        self.me = d
        self.pos = jnp.where(d % 2 == 0, d // 2, n - 1 - d // 2)

    def index(self, offset):
        if offset == 0:
            return self.me
        r = (self.pos + offset) % self.n
        return jnp.where(r < self.n // 2, 2 * r, 2 * (self.n - 1 - r) + 1)


def slot(sends, work=None, given=(), free=()):
    names = [k for k in sends if k not in free]
    loose = [sends[k][1](sends[k][0]) for k in free]
    tied = held(*[sends[k][0] for k in names], *given)
    moved = [sends[k][1](v) for k, v in zip(names, tied)]
    done = tuple(work(*tied[len(names) :])) if work is not None else ()
    names += free
    out = held(*moved, *loose, *done)
    return dict(zip(names, out[: len(names)])), out[len(names) :]


def swap_core(v):
    return lax.ppermute(v, "group", CORE_SWAP)


def swap_y(v):
    return lax.ppermute(v, "group", Y_SWAP)


def dot(a, b):
    return jnp.dot(a, b, preferred_element_type=F32)


def dot_t(a, b):
    return lax.dot_general(a, b, (((1,), (1,)), ((), ())), preferred_element_type=F32)


def dot_w(a, b):
    return lax.dot_general(a, b, (((0,), (0,)), ((), ())), preferred_element_type=F32)


def normal(v):
    center = jnp.mean(v, axis=-1, keepdims=True)
    centered = v - center
    inverse = lax.rsqrt(jnp.mean(centered * centered, axis=-1, keepdims=True) + 1e-05)
    return centered * inverse, inverse


def normal_back(grad, hat, inverse, gain):
    g = grad * gain
    a = jnp.mean(g, axis=-1, keepdims=True)
    b = jnp.mean(g * hat, axis=-1, keepdims=True)
    return inverse * (g - a - hat * b)


def erf_pair(h):
    d = 1.0 + (0.3275911 / math.sqrt(2.0)) * jnp.abs(h)
    t = pl.reciprocal(d, approx=True)
    t = t * (2.0 - d * t)
    e = jnp.exp(-0.5 * (h * h))
    p = 0.5 * -1.453152027 + t * (0.5 * 1.061405429)
    p = 0.5 * 1.421413741 + t * p
    p = 0.5 * -0.284496736 + t * p
    q = (0.5 * 0.254829592 + t * p) * (t * e)
    return jnp.where(h >= 0, 1.0 - q, q), (h * e) * (1.0 / math.sqrt(2.0 * math.pi))


def over(parts, first, rows):
    for part in parts:
        lo, hi = max(first, part[0]), min(first + rows, part[0] + part[1])
        if lo < hi:
            yield lo - first, hi - lo, lo - part[0], part


def start_copy(piece, row, rows, whole, at, sem):
    at = at if isinstance(at, int) else pl.multiple_of(at, 16)
    pltpu.make_async_copy(
        piece.at[pl.ds(row, rows)], whole.at[pl.ds(at, rows)], sem
    ).start()


def wait_rows(whole, first, rows, sem):
    view = whole.at[pl.ds(first, rows)]
    pltpu.make_async_copy(view, view, sem).wait()


class Pieces:
    def __init__(self):
        self.meta, self.arrays = [], []

    def add(self, source, other, first, array):
        self.meta.append((source, other, first, array.shape[0]))
        self.arrays.append(array)


def load_si(lay, b, where, meta, refs, whole, sems):
    core = where[1]
    for (source, other, first, rows), ref in zip(meta, refs):
        src = where[2 + source]
        h = 1 - core if other else core
        for row, count, inside, part in over(lay.si_parts(b), first, rows):
            _, half, base, shard = part
            at = base + src * shard + h * half + inside
            start_copy(ref, row, count, whole, at, sems.at[0 if base == 0 else 1])


def load_g(lay, b, where, meta, refs, whole, sem):
    core = where[1]
    for (source, other, first, rows), ref in zip(meta, refs):
        src = where[2 + source]
        h = 1 - core if other else core
        for row, count, inside, part in over(lay.g_parts(b), first - lay.si_half, rows):
            at = (h * (STRIDES[b] // 2) + part[2]) * lay.width + src * lay.k + inside
            start_copy(ref, row, count, whole, at, sem)


def load_f(lay, c, where, meta, refs, wholes, sems):
    names = ("merge", "contract", "trend", "expand")
    width = lay.width
    for (source, other, first, rows), ref in zip(meta, refs):
        src = where[2 + source]
        h = 1 - c if other else c
        for row, count, inside, part in over(lay.f_parts(h), first - lay.si_half, rows):
            t = names.index(part[2])
            at = pl.multiple_of(src * part[1] + inside, 16)
            target = wholes[t].at[pl.ds(at, count), pl.ds(part[3] * width, width)]
            pltpu.make_async_copy(ref.at[pl.ds(row, count)], target, sems.at[t]).start()


def any_spec():
    return pl.BlockSpec(memory_space=pl.ANY)


def vmem_spec():
    return pl.BlockSpec(memory_space=pltpu.VMEM)


def smem_spec():
    return pl.BlockSpec(memory_space=pltpu.SMEM)


def cost(flops, moved):
    return pl.CostEstimate(flops=int(flops), bytes_accessed=int(moved), transcendentals=0)


def by_branch(where, body):
    for b in range(2):
        pl.when(where[0] == b)(functools.partial(body, b))


def half_of(lay, where, sibling, fs, cs, fi, ci, fg, cg, weights):
    width, k = lay.width, lay.k
    base = lay.si_half
    rows = base + lay.g_half + lay.f_half

    def kernel(where, fs, cs, fi, ci, fg, cg, contract, merge, trend, expand, out, sems):
        def moves(b, h):
            found = []
            for i, (first, half, _, _) in enumerate(lay.si_parts(b)):
                source = ((fs, fi), (cs, ci))[b][i]
                found.append((source.at[pl.ds(h * half, half)], out.at[pl.ds(first, half)]))
            for first, count, j in lay.g_parts(b):
                col = (h * (STRIDES[b] // 2) + j) * width
                source = (fg, cg)[b].at[:, pl.ds(col, width)]
                found.append((source, out.at[pl.ds(base + first, count)]))
            named = {"contract": contract, "merge": merge, "trend": trend}
            for first, count, name, j in lay.f_parts(h):
                source = expand.at[:, pl.ds(j * width, width)] if name == "expand" else named[name]
                found.append((source, out.at[pl.ds(base + first, count)]))
            return [(x, y, sems.at[i]) for i, (x, y) in enumerate(found)]

        for b in range(2):
            for h in range(2):

                @pl.when((where[0] == b) & (where[1] == (1 - h if sibling else h)))
                def _(b=b, h=h):
                    used = lay.g_parts(b)[-1][0] + k
                    if used < lay.g_half:
                        out[base + used : base + lay.g_half, :] = jnp.zeros(
                            (lay.g_half - used, width), BF
                        )
                    used = lay.f_parts(h)[-1][0] + lay.f_parts(h)[-1][1]
                    if used < lay.g_half + lay.f_half:
                        out[base + used :, :] = jnp.zeros((rows - base - used, width), BF)
                    for x, y, sem in moves(b, h):
                        pltpu.make_async_copy(x, y, sem).start()
                    for x, y, sem in moves(b, h):
                        pltpu.make_async_copy(x, y, sem).wait()

    return pl.pallas_call(
        kernel,
        out_shape=jax.ShapeDtypeStruct((rows, width), BF),
        in_specs=[smem_spec()] + [any_spec()] * 10,
        out_specs=vmem_spec(),
        scratch_shapes=[pltpu.SemaphoreType.DMA((8 + max(STRIDES),))],
        compiler_params=pltpu.CompilerParams(vmem_limit_bytes=VMEM),
        cost_estimate=cost(0, 4 * rows * width),
        name="sibling_half" if sibling else "own_half",
    )(where, fs, cs, fi, ci, fg, cg, *weights)


def bounds_of(kinds, base):
    firsts, lasts = [jnp.int32(0)], [jnp.int32(GROUP - 1)]
    for b in range(1, GROUP):
        firsts.append(jnp.where(kinds[base + b] == 2, firsts[-1], b))
    for b in reversed(range(GROUP - 1)):
        lasts.insert(0, jnp.where(kinds[base + b + 1] == 2, lasts[0], b))
    return firsts, lasts


def counts_of(lay, kinds, base, step):
    firsts, lasts = bounds_of(kinds, base)
    length = lay.length
    first = jnp.zeros_like(step)
    last = jnp.full_like(step, length - 1)
    for b in range(GROUP):
        inside = (step >= b * lay.block_len) & (step < (b + 1) * lay.block_len)
        first = jnp.where(inside, firsts[b] * lay.block_len, first)
        last = jnp.where(inside, lasts[b] * lay.block_len + (lay.block_len - 1), last)
    j = lax.broadcasted_iota(jnp.int32, (length, length), 1)
    low = jnp.maximum(step - HALF, first)
    high = jnp.minimum(step + HALF, last)
    count = jnp.where((j >= low) & (j <= high), 1.0, 0.0)
    before = jnp.maximum(first - step + HALF, 0).astype(F32)
    after = jnp.maximum(step + HALF - last, 0).astype(F32)
    count += jnp.where(j == first, before, 0.0)
    count += jnp.where(j == last, after, 0.0)
    return count.astype(BF)


def season_kernel(lay, kinds, step, x, with_trend):
    width, length = lay.width, lay.length
    groups = x.shape[0]

    def kernel(kinds_ref, step_ref, x_ref, season_ref, low_ref, *refs):
        base = pl.program_id(0) * GROUP
        step = step_ref[...]
        x = x_ref[0]
        j = lax.broadcasted_iota(jnp.int32, (length, length), 1)
        order = jnp.where(j == step, 1.0, 0.0).astype(BF)
        season = dot(order, x) - dot(counts_of(lay, kinds_ref, base, step), x) * (1.0 / WINDOW)
        season_ref[0] = season
        low_ref[0] = season.astype(BF)
        if with_trend:
            counts_ref, trend_ref, order_ref = refs
            order_ref[...] = order
            plain = lax.broadcasted_iota(jnp.int32, (length, 1), 0)
            counts = counts_of(lay, kinds_ref, base, plain)
            counts_ref[0] = counts
            trend_ref[0] = (dot(counts, x) * (1.0 / WINDOW)).astype(BF)

    group = pl.BlockSpec((1, length, width), lambda g: (g, 0, 0))
    square = pl.BlockSpec((1, length, length), lambda g: (g, 0, 0))
    shapes = [
        jax.ShapeDtypeStruct((groups, length, width), F32),
        jax.ShapeDtypeStruct((groups, length, width), BF),
    ]
    specs = [group, group]
    if with_trend:
        shapes += [
            jax.ShapeDtypeStruct((groups, length, length), BF),
            jax.ShapeDtypeStruct((groups, length, width), BF),
            jax.ShapeDtypeStruct((length, length), BF),
        ]
        specs += [square, group, pl.BlockSpec((length, length), lambda g: (0, 0))]
    return pl.pallas_call(
        kernel,
        grid=(groups,),
        out_shape=shapes,
        in_specs=[smem_spec(), pl.BlockSpec((length, 1), lambda g: (0, 0)), group],
        out_specs=specs,
        compiler_params=pltpu.CompilerParams(vmem_limit_bytes=VMEM),
        cost_estimate=cost(6 * groups * length * length * width, 12 * groups * length * width),
        name="season_trend" if with_trend else "season",
    )(kinds, step, x)


def all_taps(x, age, taps):
    rolled = [x] + [pltpu.roll(x, k, 0) for k in range(1, min(8, taps))]
    for k in range(taps):
        v = rolled[k % 8]
        if k >= 8:
            v = jnp.concatenate([jnp.zeros_like(v[: k - k % 8]), v[: v.shape[0] - (k - k % 8)]])
        yield k, jnp.where(age >= k, v, 0.0) if k else v


def step_rows(own, other, s, npos):
    cut = slice(s * npos, (s + 1) * npos)
    x = jnp.concatenate([own[:, cut, :], other[:, cut, :]], axis=0)
    return x.reshape(x.shape[0] * npos, x.shape[2])


def filled(x, rows):
    if x.shape[0] == rows:
        return x
    return jnp.concatenate([x, jnp.zeros((rows - x.shape[0], x.shape[1]), x.dtype)], axis=0)


def shrink_forward(lay, where, si, low_own, low_other, kinds_own, kinds_other, gain):
    n, width = lay.n, lay.width
    groups = 2 * low_own.shape[0]
    most = groups * max(lay.npos)
    count = len(si.arrays)
    total = lay.shrink[0] + lay.iso[0]

    def kernel(where, kinds_own, kinds_other, gain_ref, own_ref, other_ref, *refs):
        pieces, rest = refs[:count], refs[count:]
        shrunk_ref, iso_ref, mixed_ref, age_ref, taps_out, whole_out, whole, taps_ref, sems = rest

        def body(b):
            load_si(lay, b, where, si.meta, pieces, whole, sems)
            npos = lay.npos[b]
            m = groups * npos
            wait_rows(whole, 0, lay.shrink[b], sems.at[0])
            z = jnp.zeros((m, width), F32)
            for s in range(STRIDES[b]):
                z += dot(step_rows(own_ref, other_ref, s, npos), whole[s * width : (s + 1) * width])
            shrunk = jnp.tanh(z)
            shrunk_ref[:m] = shrunk
            low = shrunk.astype(BF).astype(F32)
            wait_rows(whole, lay.shrink[b], lay.iso[b], sems.at[1])
            pltpu.make_async_copy(whole, whole_out, sems.at[2]).start()
            taps = lay.taps[b]
            base = lay.shrink[b]
            row = lax.broadcasted_iota(jnp.int32, (m, 1), 0)
            age = jnp.zeros_like(row)
            for g in range(groups):
                own = g < groups // 2
                kinds = kinds_own if own else kinds_other
                firsts, _ = bounds_of(kinds, (g if own else g - groups // 2) * GROUP)
                for i in range(GROUP):
                    lo = g * npos + i * taps
                    inside = (row >= lo) & (row < lo + taps)
                    age = jnp.where(inside, row - lo + (i - firsts[i]) * taps, age)
            age_ref[:m] = age
            e = jnp.zeros((m, width), F32)
            for k, x in all_taps(low, age, taps):
                at = base + (taps - 1 - k) * width
                x = x.astype(BF)
                taps_ref[k, :m, :] = x
                if m < most:
                    taps_ref[k, m:, :] = jnp.zeros((most - m, width), BF)
                e += dot(x, whole[at : at + width])
            keep = pltpu.make_async_copy(taps_ref, taps_out, sems.at[3])
            keep.start()
            iso = jnp.tanh(e)
            iso_ref[:m] = iso
            hat, _ = normal(iso + shrunk)
            mixed_ref[:m] = (hat * gain_ref[...]).astype(BF)
            pltpu.make_async_copy(whole, whole_out, sems.at[2]).wait()
            keep.wait()

        by_branch(where, body)

    return pl.pallas_call(
        kernel,
        out_shape=[
            jax.ShapeDtypeStruct((most, width), F32),
            jax.ShapeDtypeStruct((most, width), F32),
            jax.ShapeDtypeStruct((most, width), BF),
            jax.ShapeDtypeStruct((most, 1), jnp.int32),
            jax.ShapeDtypeStruct((max(lay.taps), most, width), BF),
            jax.ShapeDtypeStruct((total, width), BF),
        ],
        in_specs=[smem_spec()] * 3 + [vmem_spec()] * 3 + [any_spec()] * count,
        out_specs=[vmem_spec()] * 4 + [any_spec()] * 2,
        scratch_shapes=[
            pltpu.VMEM((total, width), BF),
            pltpu.VMEM((max(lay.taps), most, width), BF),
            pltpu.SemaphoreType.DMA((4,)),
        ],
        compiler_params=pltpu.CompilerParams(vmem_limit_bytes=VMEM),
        cost_estimate=cost(2 * most * width * total, 4 * total * width),
        name="shrink_forward",
    )(where, kinds_own, kinds_other, gain, low_own, low_other, *si.arrays)


def stage(lay, b, copies):
    def view(ref, first, rows, middle):
        return ref.at[:, pl.ds(first, rows), :] if middle else ref.at[pl.ds(first, rows)]

    def run(i):
        for source, target, rows, sems, middle in copies:
            yield pltpu.make_async_copy(
                view(source, i * 4 * rows, 4 * rows, middle),
                view(target, i * 4 * rows, 4 * rows, middle),
                sems.at[i],
            )

    def start(i):
        for c in run(i):
            c.start()

    def wait(i):
        for c in run(i):
            c.wait()

    return start, wait


def grow_forward(lay, where, gf, part, mixed, season, order, gain):
    width = lay.width
    groups = season.shape[0]
    length = lay.length
    pieces_in = isinstance(gf, Pieces)
    arrays = gf.arrays if pieces_in else [gf]
    count = len(arrays)
    most = max(STRIDES) * width
    runs = max(STRIDES) // 4

    def kernel(where, gain_ref, order_ref, mixed_ref, season_in, *refs):
        pieces, rest = refs[:count], refs[count:]
        outs, up_out = rest[:groups], rest[groups]
        scratch = rest[groups + 1 + pieces_in :]
        rows_ref, whole, season_ref, up_ref, in_sems, w_sems, up_sems, sems = scratch

        def body(b):
            npos = lay.npos[b]
            m = groups * npos
            copies = [(season_in, season_ref, npos, in_sems, True)]
            if not pieces_in:
                copies.append((pieces[0], whole, width, w_sems, False))
            start, wait = stage(lay, b, copies)
            up_start, up_wait = stage(lay, b, [(up_ref, up_out, npos, up_sems, True)])
            if pieces_in:
                load_g(lay, b, where, gf.meta, pieces, whole, sems.at[0])
            for i in range(STRIDES[b] // 4):
                start(i)
            if pieces_in:
                wait_rows(whole, 0, STRIDES[b] * width, sems.at[0])
                pltpu.make_async_copy(whole, rest[groups + 1], sems.at[1]).start()
            x = mixed_ref[part * m : (part + 1) * m]
            gain = gain_ref[...]
            for s in range(STRIDES[b]):
                if s % 4 == 0:
                    wait(s // 4)
                cut = slice(s * npos, (s + 1) * npos)
                up = jnp.tanh(dot(x, whole[s * width : (s + 1) * width]))
                up_ref[:, cut, :] = up.reshape(groups, npos, width)
                hat, _ = normal(up + season_ref[:, cut, :].reshape(m, width))
                rows_ref[:, cut, :] = (hat * gain).astype(BF).reshape(groups, npos, width)
                if s % 4 == 3:
                    up_start(s // 4)
            for g in range(groups):
                outs[g][0] = dot_w(order_ref[...], rows_ref[g]).astype(BF)
            for i in range(STRIDES[b] // 4):
                up_wait(i)
            if pieces_in:
                pltpu.make_async_copy(whole, rest[groups + 1], sems.at[1]).wait()

        by_branch(where, body)

    shapes = [jax.ShapeDtypeStruct((1, length, width), BF)] * groups
    shapes.append(jax.ShapeDtypeStruct((groups, length, width), F32))
    if pieces_in:
        shapes.append(jax.ShapeDtypeStruct((most, width), BF))
    return pl.pallas_call(
        kernel,
        out_shape=shapes,
        in_specs=[smem_spec()] + [vmem_spec()] * 3 + [any_spec()] * (1 + count),
        out_specs=[vmem_spec()] * groups + [any_spec()] * (1 + pieces_in),
        scratch_shapes=[
            pltpu.VMEM((groups, length, width), BF),
            pltpu.VMEM((most, width), BF),
            pltpu.VMEM((groups, length, width), F32),
            pltpu.VMEM((groups, length, width), F32),
        ]
        + [pltpu.SemaphoreType.DMA((runs,))] * 3
        + [pltpu.SemaphoreType.DMA((2,))],
        compiler_params=pltpu.CompilerParams(vmem_limit_bytes=VMEM),
        cost_estimate=cost(
            2 * groups * length * width * (width + length),
            2 * most * width + 14 * groups * length * width,
        ),
        name="grow_forward",
    )(where, gain, order, mixed, season, *arrays)


def grow_backward(lay, where, whole, grads, up, season, order, gain):
    width = lay.width
    groups = season.shape[0]
    length = lay.length
    most = groups * max(lay.npos)
    runs = max(STRIDES) // 4

    def kernel(where, gain_ref, order_ref, up_in, season_in, whole_in, *refs):
        grad_refs, rest = refs[:groups], refs[groups:]
        pre_ref, back_ref, sum_out, gain_grad_ref = rest[:4]
        rows_ref, whole, up_ref, season_ref, sum_ref = rest[4:9]
        sems, sum_sems = rest[9:12], rest[12]

        def body(b):
            npos = lay.npos[b]
            m = groups * npos
            start, wait = stage(
                lay,
                b,
                [
                    (up_in, up_ref, npos, sems[0], True),
                    (season_in, season_ref, npos, sems[1], True),
                    (whole_in, whole, width, sems[2], False),
                ],
            )
            sum_start, sum_wait = stage(lay, b, [(sum_ref, sum_out, npos, sum_sems, True)])
            for i in range(STRIDES[b] // 4):
                start(i)
            for g in range(groups):
                rows_ref[g] = dot(order_ref[...], grad_refs[g][...]).astype(BF)
            total = jnp.zeros((m, width), F32)
            gains = jnp.zeros((1, width), F32)
            for s in range(STRIDES[b]):
                if s % 4 == 0:
                    wait(s // 4)
                cut = slice(s * npos, (s + 1) * npos)
                up = up_ref[:, cut, :].reshape(m, width)
                hat, inverse = normal(up + season_ref[:, cut, :].reshape(m, width))
                g = rows_ref[:, cut, :].reshape(m, width).astype(F32)
                gains += jnp.sum(g * hat, axis=0, keepdims=True)
                d = normal_back(g, hat, inverse, gain_ref[...])
                sum_ref[:, cut, :] = d.reshape(groups, npos, width)
                pre = (d * (1.0 - up * up)).astype(BF)
                pre_ref[:, cut, :] = pre.reshape(groups, npos, width)
                total += dot_t(pre, whole[s * width : (s + 1) * width])
                if s % 4 == 3:
                    sum_start(s // 4)
            back_ref[:m] = total
            gain_grad_ref[...] = gains
            for i in range(STRIDES[b] // 4):
                sum_wait(i)

        by_branch(where, body)

    return pl.pallas_call(
        kernel,
        out_shape=[
            jax.ShapeDtypeStruct((groups, length, width), BF),
            jax.ShapeDtypeStruct((most, width), F32),
            jax.ShapeDtypeStruct((groups, length, width), F32),
            jax.ShapeDtypeStruct((1, width), F32),
        ],
        in_specs=[smem_spec()] + [vmem_spec()] * 2 + [any_spec()] * 3 + [vmem_spec()] * groups,
        out_specs=[vmem_spec(), vmem_spec(), any_spec(), vmem_spec()],
        scratch_shapes=[
            pltpu.VMEM((groups, length, width), BF),
            pltpu.VMEM((whole.shape[0], width), BF),
            pltpu.VMEM((groups, length, width), F32),
            pltpu.VMEM((groups, length, width), F32),
            pltpu.VMEM((groups, length, width), F32),
        ]
        + [pltpu.SemaphoreType.DMA((runs,))] * 4,
        compiler_params=pltpu.CompilerParams(vmem_limit_bytes=VMEM),
        cost_estimate=cost(
            2 * groups * length * width * (width + length),
            2 * whole.shape[0] * width + 18 * groups * length * width,
        ),
        name="grow_backward",
    )(where, gain, order, up, season, whole, *grads)


class Outlet:
    def __init__(self, n, rows, width):
        self.n, self.rows, self.width = n, rows, width
        self.bounds = [(0, 1)] + [(i, i + 2) for i in range(1, n - 1, 2)] + [(n - 1, n)]

    def shapes(self):
        sizes = [hi - lo for lo, hi in self.bounds] + [self.n]
        return [jax.ShapeDtypeStruct((c, self.rows, self.width), BF) for c in sizes]

    def scratch(self):
        return [
            pltpu.VMEM((2, self.n, self.rows, self.width), BF),
            pltpu.SemaphoreType.DMA((1 + len(self.bounds),)),
        ]

    def copies(self, held_ref, outs, sems):
        found = []
        for i, (lo, hi) in enumerate(self.bounds):
            source = held_ref.at[0, pl.ds(lo, hi - lo)]
            found.append(pltpu.make_async_copy(source, outs[i], sems.at[i]))
        last = len(self.bounds)
        found.append(pltpu.make_async_copy(held_ref.at[1], outs[last], sems.at[last]))
        return found

    def flush(self, held_ref, outs, sems):
        for c in self.copies(held_ref, outs, sems):
            c.start()
        for c in self.copies(held_ref, outs, sems):
            c.wait()


def grow_weight(lay, where, places, mixed, pre_own, pre_other, outlet):
    n, width, k = lay.n, lay.width, lay.k
    groups = pre_own.shape[0]
    made = len(outlet.shapes())

    def kernel(where, places_ref, mixed_ref, own_ref, other_ref, *refs):
        outs, (out_ref, sems) = refs[:made], refs[made:]

        def body(b):
            npos = lay.npos[b]
            most = 2 * groups * max(lay.npos)
            x = filled(mixed_ref[: 2 * groups * npos], most)
            steps = STRIDES[b] // 2
            for s in range(STRIDES[b]):
                d = dot_w(x, filled(step_rows(own_ref, other_ref, s, npos), most)).astype(BF)
                side = jnp.where(where[1] == s // steps, 0, 1)
                at = (s % steps) * k
                for shard in range(n):
                    out_ref[side, places_ref[shard], at : at + k, :] = d[shard * k : (shard + 1) * k]
            rest = lay.g_half - steps * k
            if rest:
                out_ref[:, :, steps * k :, :] = jnp.zeros((2, n, rest, width), BF)

        by_branch(where, body)
        outlet.flush(out_ref, outs, sems)

    return pl.pallas_call(
        kernel,
        out_shape=outlet.shapes(),
        in_specs=[smem_spec(), smem_spec()] + [vmem_spec()] * 3,
        out_specs=[any_spec()] * made,
        scratch_shapes=outlet.scratch(),
        compiler_params=pltpu.CompilerParams(vmem_limit_bytes=VMEM),
        cost_estimate=cost(4 * groups * lay.length * width * width, 2 * 2 * n * lay.g_half * width),
        name="grow_weight",
    )(where, places, mixed, pre_own, pre_other)


def shrink_backward(lay, where, whole, back_own, back_other, shrunk, iso, age, gain):
    width = lay.width
    most = shrunk.shape[0]

    def kernel(where, age_ref, gain_ref, b0, b1, shrunk_ref, iso_ref, whole_in, *refs):
        pre_ref, iso_pre_ref, gain_grad_ref, whole, sem = refs

        def body(b):
            npos, taps = lay.npos[b], lay.taps[b]
            base = lay.shrink[b]
            source = whole_in.at[pl.ds(base, lay.iso[b])]
            fetch = pltpu.make_async_copy(source, whole.at[pl.ds(0, lay.iso[b])], sem)
            fetch.start()
            m = (most // max(lay.npos)) * npos
            mixed_back = jnp.concatenate([b0[: m // 2], b1[: m // 2]], axis=0)
            shrunk, iso = shrunk_ref[:m], iso_ref[:m]
            hat, inverse = normal(iso + shrunk)
            gain_grad_ref[...] = jnp.sum(mixed_back * hat, axis=0, keepdims=True)
            joint = normal_back(mixed_back, hat, inverse, gain_ref[...])
            iso_pre = (joint * (1.0 - iso * iso)).astype(BF)
            iso_pre_ref[:m] = iso_pre
            age = age_ref[:m]
            total = joint
            fetch.wait()
            for r in range(min(8, taps)):
                both = None
                for k in range(r, taps, 8):
                    tap = taps - 1 - k
                    back = dot_t(iso_pre, whole[tap * width : (tap + 1) * width])
                    if k:
                        back = jnp.where(age >= k, back, 0.0)
                    if k >= 8:
                        back = jnp.concatenate([back[k - r :], jnp.zeros_like(back[: k - r])])
                    both = back if both is None else both + back
                total += pltpu.roll(both, m - r, 0) if r else both
            pre_ref[:m] = (total * (1.0 - shrunk * shrunk)).astype(BF)

        by_branch(where, body)

    return pl.pallas_call(
        kernel,
        out_shape=[
            jax.ShapeDtypeStruct((most, width), BF),
            jax.ShapeDtypeStruct((most, width), BF),
            jax.ShapeDtypeStruct((1, width), F32),
        ],
        in_specs=[smem_spec()] + [vmem_spec()] * 6 + [any_spec()],
        out_specs=[vmem_spec()] * 3,
        scratch_shapes=[pltpu.VMEM((max(lay.iso), width), BF), pltpu.SemaphoreType.DMA],
        compiler_params=pltpu.CompilerParams(vmem_limit_bytes=VMEM),
        cost_estimate=cost(2 * most * width * lay.iso[0], 2 * lay.iso[0] * width),
        name="shrink_backward",
    )(where, age, gain, back_own, back_other, shrunk, iso, whole)


def shrink_weight(lay, where, places, iso_pre, pre, stacked, low_own, low_other, gains, outlet):
    width = lay.width
    most = stacked.shape[1]
    made = len(outlet.shapes())

    def kernel(where, places_ref, gains_ref, iso_pre_ref, pre_ref, own_ref, other_ref, *refs):
        stacked_in, outs = refs[0], refs[1 : 1 + made]
        grad_ref, sems, taps_ref, taps_sem = refs[1 + made :]
        fetch = pltpu.make_async_copy(stacked_in, taps_ref, taps_sem)
        fetch.start()
        extra = gains_ref[...].astype(BF)
        for side in range(2):
            for place in range(lay.n):
                grad_ref[side, place, lay.si_half :, :] = extra

        def body(b):
            npos, taps = lay.npos[b], lay.taps[b]
            m = (most // max(lay.npos)) * npos

            def store(part, row, d):
                first, half, _, shard = part
                d = d.astype(BF)
                lo = row
                while lo < row + width:
                    dp, h, r = lo // shard, (lo % shard) // half, lo % half
                    rows = min(half - r, row + width - lo)
                    side = jnp.where(where[1] == h, 0, 1)
                    grad_ref[side, places_ref[dp], first + r : first + r + rows, :] = d[
                        lo - row : lo - row + rows
                    ]
                    lo += rows

            part_s, part_i = lay.si_parts(b)
            iso_pre, pre = filled(iso_pre_ref[:m], most), filled(pre_ref[:m], most)
            for s in range(STRIDES[b]):
                x = filled(step_rows(own_ref, other_ref, s, npos), most)
                store(part_s, s * width, dot_w(x, pre))
            fetch.wait()
            for k in range(taps):
                store(part_i, (taps - 1 - k) * width, dot_w(taps_ref[k], iso_pre))

        by_branch(where, body)
        outlet.flush(grad_ref, outs, sems)

    return pl.pallas_call(
        kernel,
        out_shape=outlet.shapes(),
        in_specs=[smem_spec(), smem_spec()] + [vmem_spec()] * 5 + [any_spec()],
        out_specs=[any_spec()] * made,
        scratch_shapes=outlet.scratch()
        + [pltpu.VMEM(stacked.shape, BF), pltpu.SemaphoreType.DMA],
        compiler_params=pltpu.CompilerParams(vmem_limit_bytes=VMEM),
        cost_estimate=cost(2 * most * width * (lay.iso[0] + lay.shrink[0]), 30 * MIB),
        name="shrink_weight",
    )(where, places, gains, iso_pre, pre, low_own, low_other, stacked)


def season_backward(lay, where, whole, pre, sum_own, sum_other, order):
    width, length = lay.width, lay.length
    groups = sum_own.shape[0]
    most = max(lay.shrink)

    def kernel(where, order_ref, pre_ref, own_ref, other_ref, whole_in, *refs):
        outs, (whole, rows_ref, sem) = refs[:3], refs[3:]

        def body(b):
            fetch = pltpu.make_async_copy(
                whole_in.at[pl.ds(0, lay.shrink[b])], whole.at[pl.ds(0, lay.shrink[b])], sem
            )
            fetch.start()
            npos = lay.npos[b]
            m = groups * npos
            fetch.wait()
            for s in range(STRIDES[b]):
                cut = slice(s * npos, (s + 1) * npos)
                d = dot_t(pre_ref[: 2 * m], whole[s * width : (s + 1) * width])
                rows_ref[:groups, cut, :] = (
                    d[:m].reshape(groups, npos, width) + own_ref[:, cut, :]
                ).astype(BF)
                rows_ref[groups:, cut, :] = (
                    d[m:].reshape(groups, npos, width) + other_ref[:, cut, :]
                ).astype(BF)

        by_branch(where, body)
        for g in range(groups):
            outs[0][g] = dot_w(order_ref[...], rows_ref[g]).astype(BF)
            ref, i = (outs[1], 0) if g == 0 else (outs[2], g - 1)
            ref[i] = dot_w(order_ref[...], rows_ref[groups + g]).astype(BF)

    return pl.pallas_call(
        kernel,
        out_shape=[
            jax.ShapeDtypeStruct((c, length, width), BF) for c in (groups, 1, groups - 1)
        ],
        in_specs=[smem_spec()] + [vmem_spec()] * 4 + [any_spec()],
        out_specs=[vmem_spec()] * 3,
        scratch_shapes=[
            pltpu.VMEM((most, width), BF),
            pltpu.VMEM((2 * groups, length, width), BF),
            pltpu.SemaphoreType.DMA,
        ],
        compiler_params=pltpu.CompilerParams(vmem_limit_bytes=VMEM),
        cost_estimate=cost(
            4 * groups * length * width * (width + length),
            2 * most * width + 24 * groups * length * width,
        ),
        name="season_backward",
    )(where, order, pre, sum_own, sum_other, whole)


def ring_add(jobs):
    specs, arrays, shapes = [], [], []
    for first, rows, terms in jobs:
        width = terms[0][0].shape[-1]
        shapes.append(jax.ShapeDtypeStruct((rows, width), BF))
        for array, place, _ in terms:
            arrays.append(array)
            if place is None:
                specs.append(vmem_spec())
            else:
                index = functools.partial(lambda p, q, g: (p, q, 0), place, first // rows)
                specs.append(pl.BlockSpec((1, rows, width), index))

    def kernel(*refs):
        ins, outs = list(refs[: len(arrays)]), refs[len(arrays) :]
        for (first, rows, terms), out in zip(jobs, outs):
            mine = [ins.pop(0) for _ in terms]
            for r in range(0, rows, 16):
                total = None
                for (array, place, at), ref in zip(terms, mine):
                    count = rows if place is not None else array.shape[0]
                    if not at <= r < at + count:
                        continue
                    v = ref[0, r : r + 16, :] if place is not None else ref[r - at : r - at + 16, :]
                    v = v.astype(F32)
                    total = v if total is None else total + v
                out[r : r + 16, :] = total.astype(BF)

    moved = sum(2 * s.shape[0] * s.shape[1] for s in shapes) * 4
    return pl.pallas_call(
        kernel,
        grid=(1,),
        out_shape=shapes,
        in_specs=specs,
        out_specs=[vmem_spec()] * len(shapes),
        compiler_params=pltpu.CompilerParams(vmem_limit_bytes=VMEM),
        cost_estimate=cost(0, moved),
        name="ring_add",
    )(*arrays)


def plain_add(jobs):
    found = []
    for first, rows, terms in jobs:
        total, late = None, None
        for array, place, at in terms:
            v = array if place is None else array[place, first : first + rows]
            v = v.astype(F32)
            if v.shape[0] < rows:
                late = (v, at)
            else:
                total = v if total is None else total + v
        if late is not None:
            v, at = late
            lo, hi = total[:at], total[at + v.shape[0] :]
            total = jnp.concatenate([lo, total[at : at + v.shape[0]] + v, hi])
        found.append(total.astype(BF))
    return found


def give_out(lay, member_ids, mine, over_y, sibling, sibling_over_y):
    n, width = lay.n, lay.width

    def kernel(where, mine, over_y, sibling, sibling_over_y, *outs):
        for y in range(2):
            for core in range(2):

                @pl.when((where[0] == y) & (where[1] == core))
                def _(y=y, core=core):
                    for b in range(2):
                        own, other = (mine, sibling) if b == y else (over_y, sibling_over_y)
                        for i, (first, half, _, _) in enumerate(lay.si_parts(b)):
                            for h in range(2):
                                source = own if h == core else other
                                outs[2 * i + b][h * half : (h + 1) * half, :] = source[
                                    first : first + half, :
                                ].astype(F32)

    return pl.pallas_call(
        kernel,
        out_shape=[
            jax.ShapeDtypeStruct((rows // n, width), F32) for rows in (*lay.shrink, *lay.iso)
        ],
        in_specs=[smem_spec()] + [vmem_spec()] * 4,
        out_specs=[vmem_spec()] * 4,
        compiler_params=pltpu.CompilerParams(vmem_limit_bytes=VMEM),
        cost_estimate=cost(0, 12 * MIB),
        name="give_out",
    )(member_ids, mine, over_y, sibling, sibling_over_y)


def dense_whole(lay, where, gf):
    width, ff = lay.width, lay.width * lay.chunks
    count = len(gf.arrays)
    shapes = ((2 * width, width), (ff, width), (width, width), (width, ff))

    def kernel(where, *refs):
        pieces, wholes, sems = refs[:count], refs[count:-1], refs[-1]
        for c in range(2):
            pl.when(where[1] == c)(
                functools.partial(load_f, lay, c, where, gf.meta, pieces, wholes, sems)
            )
        for t in range(4):
            wait_rows(wholes[t], 0, shapes[t][0], sems.at[t])

    return pl.pallas_call(
        kernel,
        out_shape=[jax.ShapeDtypeStruct(v, BF) for v in shapes],
        in_specs=[smem_spec()] + [any_spec()] * count,
        out_specs=[vmem_spec()] * 4,
        scratch_shapes=[pltpu.SemaphoreType.DMA((4,))],
        compiler_params=pltpu.CompilerParams(vmem_limit_bytes=VMEM),
        cost_estimate=cost(0, 4 * sum(r * c for r, c in shapes)),
        name="dense_whole",
    )(where, *gf.arrays)


def dense(lay, where, tile, wholes, mine, received, trend_low, out_grad, gain_middle, gain_output):
    width, length, chunks = lay.width, lay.length, lay.chunks
    cuts = 2
    part = length // cuts
    ff = width * chunks
    strip = 32

    def kernel(where, tile_ref, gm_ref, go_ref, merge, contract, trend, expand, *refs):
        mine_ref, got_ref, trend_ref, grad_ref = refs[:4]
        (hid_ref, hg_ref, ml_ref, ll_ref, mg_ref, tb_ref, out_ref, jm_ref, js_ref) = refs[4:13]
        gains_ref, h_ref, slope_ref, a_ref, b_ref, c_ref = refs[13:]
        b = where[0]
        gm, go = gm_ref[...], go_ref[...]
        at_mine = pl.multiple_of(b * width, width)
        at_other = pl.multiple_of((1 - b) * width, width)

        def strips(body):
            for r in range(0, part, strip):
                body(slice(r, r + strip))

        a_ref[...] = dot(mine_ref[...], merge[pl.ds(at_mine, width)]) + dot(
            got_ref[...], merge[pl.ds(at_other, width)]
        )
        inverses = {}

        def middle_norm(r):
            hat, inverses[r.start] = normal(a_ref[r, :])
            a_ref[r, :] = hat
            ml_ref[r, :] = (hat * gm).astype(BF)

        strips(middle_norm)
        for j in range(chunks):
            cols = slice(j * width, (j + 1) * width)
            h_ref[:, cols] = dot(ml_ref[...], expand[:, cols])

            def gelu(r, cols=cols):
                h = h_ref[r, cols]
                phi, dens = erf_pair(h)
                hid_ref[r, cols] = (h * phi).astype(BF)
                slope_ref[r, cols] = phi + dens

            strips(gelu)
        b_ref[...] = dot(hid_ref[...], contract[...])
        c_ref[...] = dot(trend_ref[0], trend[...])
        sums = [jnp.zeros((8, width), F32), jnp.zeros((8, width), F32)]

        def rows8(v):
            return jnp.sum(v.reshape(strip // 8, 8, width), axis=0)

        def output_norm(r):
            hat, inverse = normal(a_ref[r, :] * gm + b_ref[r, :])
            out_ref[r, :] = (hat * go + c_ref[r, :]).astype(BF)
            g = grad_ref[0, r, :].astype(F32)
            sums[1] += rows8(g * hat)
            d = normal_back(g, hat, inverse, go)
            b_ref[r, :] = d
            ll_ref[r, :] = d.astype(BF)

        strips(output_norm)
        tb_ref[...] = dot_t(grad_ref[0], trend[...])
        for j in range(chunks):
            cols = slice(j * width, (j + 1) * width)
            h_ref[:, cols] = dot_t(ll_ref[...], contract[cols])

            def gelu_back(r, cols=cols):
                hg_ref[r, cols] = (h_ref[r, cols] * slope_ref[r, cols]).astype(BF)

            strips(gelu_back)
        c_ref[...] = dot_t(hg_ref[...], expand[...])

        def middle_back(r):
            hat = a_ref[r, :]
            back = b_ref[r, :] + c_ref[r, :]
            sums[0] += rows8(back * hat)
            mg_ref[r, :] = normal_back(back, hat, inverses[r.start], gm).astype(BF)

        strips(middle_back)
        jm_ref[...] = dot_t(mg_ref[...], merge[pl.ds(at_mine, width)]).astype(BF)
        js_ref[...] = dot_t(mg_ref[...], merge[pl.ds(at_other, width)]).astype(BF)

        @pl.when(pl.program_id(0) == 0)
        def _():
            gains_ref[...] = jnp.zeros_like(gains_ref)

        gains_ref[0:1, :] += jnp.sum(sums[0], axis=0, keepdims=True)
        gains_ref[1:2, :] += jnp.sum(sums[1], axis=0, keepdims=True)

    of_tile = pl.BlockSpec((1, part, width), lambda i, w, t: (t[0], i, 0))
    alone = pl.BlockSpec((part, width), lambda i, w, t: (i, 0))
    shapes = [(ff, BF)] * 2 + [(width, BF)] * 3 + [(width, F32)] + [(width, BF)] * 3
    return pl.pallas_call(
        kernel,
        grid_spec=pltpu.PrefetchScalarGridSpec(
            num_scalar_prefetch=2,
            grid=(cuts,),
            in_specs=[vmem_spec()] * 6 + [alone, alone, of_tile, of_tile],
            out_specs=[pl.BlockSpec((part, c), lambda i, w, t: (i, 0)) for c, _ in shapes]
            + [pl.BlockSpec((2, width), lambda i, w, t: (0, 0))],
            scratch_shapes=[pltpu.VMEM((part, ff), F32)] * 2 + [pltpu.VMEM((part, width), F32)] * 3,
        ),
        out_shape=[jax.ShapeDtypeStruct((length, w), t) for w, t in shapes]
        + [jax.ShapeDtypeStruct((2, width), F32)],
        compiler_params=pltpu.CompilerParams(vmem_limit_bytes=VMEM),
        cost_estimate=cost(
            2 * length * width * (4 * width + 4 * ff + 2 * width), 12 * MIB + 20 * MIB
        ),
        name="dense",
    )(where, tile, gain_middle, gain_output, *wholes, mine, received, trend_low, out_grad)


def dense_weights(lay, where, places, mine, received, trend_low, out_grad, saved, outlet):
    n, width, chunks, length = lay.n, lay.width, lay.chunks, lay.length
    groups = len(saved)
    made = len(outlet.shapes())
    base = lay.g_half
    (_, contract, _, _), (merge_at, merge, _, _) = lay.f_parts(0)
    merge_at -= base

    def kernel(where, places_ref, *refs):
        refs = list(refs)

        def take(count):
            out = refs[:count]
            del refs[:count]
            return out

        middle, lifted = take(groups), take(groups)
        hidden, slopes = take(groups), take(groups)
        late = take(3 * groups) + take(2)
        outs = take(made)
        out_ref, sems, mine_ref, got_ref, grad_ref, trend_ref, up_ref, late_sems = refs
        core, q = where[1], pl.program_id(0)

        def fetches():
            targets = [r.at[g] for r in (mine_ref, got_ref, grad_ref) for g in range(groups)]
            targets += [trend_ref, up_ref]
            return [
                pltpu.make_async_copy(x, y, late_sems.at[i])
                for i, (x, y) in enumerate(zip(late, targets))
            ]

        def side(h):
            return jnp.where(core == h, 0, 1)

        def total(xs, gs):
            d = None
            for x, g in zip(xs, gs):
                v = dot_w(x, g)
                d = v if d is None else d + v
            return d.astype(BF)

        @pl.when(q == 0)
        def _():
            for f in fetches():
                f.start()
            if merge_at + merge < lay.f_half:
                out_ref[side(0), :, merge_at + merge :, :] = jnp.zeros(
                    (n, lay.f_half - merge_at - merge, width), BF
                )

        d = total([r[...] for r in hidden], [r[...] for r in lifted])
        each = width // contract
        for i in range(each):
            out_ref[side(0), places_ref[q * each + i], 0:contract, :] = d[
                i * contract : (i + 1) * contract
            ]
        d = total([r[...] for r in middle], [r[...] for r in slopes])
        at = pl.ds(pl.multiple_of((1 + q) * lay.k, 16), lay.k)
        for dp in range(n):
            out_ref[side(1), places_ref[dp], at, :] = d[dp * lay.k : (dp + 1) * lay.k]

        @pl.when(q == chunks - 1)
        def _():
            for f in fetches():
                f.wait()
            d = total([trend_ref[g] for g in range(groups)], [up_ref[g] for g in range(groups)])
            for dp in range(n):
                out_ref[side(1), places_ref[dp], 0 : lay.k, :] = d[dp * lay.k : (dp + 1) * lay.k]
            each = width // merge
            for ref, first in ((mine_ref, where[0]), (got_ref, 1 - where[0])):
                d = total([ref[g] for g in range(groups)], [grad_ref[g] for g in range(groups)])
                for i in range(each):
                    out_ref[side(0), places_ref[first * each + i], merge_at : merge_at + merge, :] = d[
                        i * merge : (i + 1) * merge
                    ]
            used = (1 + chunks) * lay.k
            if used < lay.f_half:
                out_ref[side(1), :, used:, :] = jnp.zeros((n, lay.f_half - used, width), BF)
            outlet.flush(out_ref, outs, sems)

    whole = pl.BlockSpec((length, width), lambda q: (0, 0))
    column = pl.BlockSpec((length, width), lambda q: (0, q))
    arrays = [k[0] for k in saved] + [k[3] for k in saved]
    arrays += [k[1] for k in saved] + [k[2] for k in saved]
    arrays += [v.reshape(length, width) for v in mine] + list(received) + [k[4] for k in saved]
    arrays += [trend_low, out_grad]
    ff = chunks * width
    square = pltpu.VMEM((groups, length, width), BF)
    return pl.pallas_call(
        kernel,
        grid=(chunks,),
        out_shape=outlet.shapes(),
        in_specs=[smem_spec(), smem_spec()]
        + [whole] * (2 * groups)
        + [column] * (2 * groups)
        + [any_spec()] * (3 * groups + 2),
        out_specs=[any_spec()] * made,
        scratch_shapes=outlet.scratch()
        + [square] * 5
        + [pltpu.SemaphoreType.DMA((3 * groups + 2,))],
        compiler_params=pltpu.CompilerParams(vmem_limit_bytes=VMEM),
        cost_estimate=cost(
            2 * groups * length * width * (2 * width + 2 * ff + width), 45 * MIB
        ),
        name="dense_weights",
    )(where, places, *arrays)


def exchange(axis, size, step):
    return lambda v: lax.ppermute(v, axis, [(i, i ^ step) for i in range(size)])


def on_device(
    n,
    series_in,
    block_kinds,
    out_grad,
    fine_shrink,
    coarse_shrink,
    fine_isometric,
    coarse_isometric,
    fine_grow,
    coarse_grow,
    merge_weight,
    expand_weight,
    contract_weight,
    trend_weight,
    branch_gain,
    middle_gain,
    output_gain,
):
    ring = Ring(n)
    member = lax.axis_index("group")
    core, y = member % 2, member // 2
    block_count = block_kinds.shape[0]
    width = series_in.shape[1]
    block_len = series_in.shape[0] // block_count
    groups = block_count // GROUP
    lay = Layout(n, width, block_len, expand_weight.shape[1])
    length = lay.length
    share = branch_gain.shape[0]
    fine = y == 0

    def right(v):
        return lax.ppermute(v, "dp", ring.right)

    def left(v):
        return lax.ppermute(v, "dp", ring.left)

    shards = (fine_shrink, coarse_shrink, fine_isometric, coarse_isometric)
    shards += (fine_grow, coarse_grow)
    dense_shards = (contract_weight, merge_weight, trend_weight, expand_weight)
    member_ids = jnp.stack([y, core]).astype(jnp.int32)
    own = half_of(lay, member_ids, False, *shards, dense_shards)
    offsets = [0]
    pieces = Pieces()
    for k in range(1, n // 2):
        offsets += [-k, k]
    offsets.append(n // 2)

    def source(offset):
        return offsets.index(offset if abs(offset) < n // 2 else n // 2)

    where = jnp.stack([y, core] + [ring.index(o) for o in offsets]).astype(jnp.int32)

    x_own = series_in.reshape(groups, length, width)
    x_other = []
    last = n // 2

    def prepare_own(kinds, x):
        rows = jnp.arange(length, dtype=jnp.int32)
        npos = jnp.where(fine, lay.npos[0], lay.npos[1])
        stride = jnp.where(fine, STRIDES[0], STRIDES[1])
        step = ((rows % npos) * stride + rows // npos)[:, None]
        return (step, *season_kernel(lay, kinds, step, x, True))

    def prepare_other(step, kinds, *xs):
        kinds = kinds.astype(jnp.int32)
        return (kinds, *season_kernel(lay, kinds, step, jnp.stack(xs), False))

    def spread_gains(*parts):
        parts = jnp.stack(parts).astype(F32)
        return lax.dynamic_update_slice(
            jnp.zeros((3, width), F32), parts, (jnp.int32(0), ring.me * share)
        )

    doublings = []
    size = 1
    while size < n:
        doublings.append(size)
        size *= 2
    gains = spread_gains(branch_gain, middle_gain, output_gain)
    hops = [exchange("dp", n, d) for d in doublings]

    def hop(sends):
        if hops:
            sends["gain"] = (gains, hops.pop(0))

    whole_r = whole_l = own
    half_rows = (lay.g_half + lay.f_half) // 2
    si_rows = lay.si_half // 2
    for t in range(1, last):
        sends = {"r": (whole_r, right), "l": (whole_l, left)}
        if t > 1:
            sends["cr"], sends["cl"] = (whole_r, swap_core), (whole_l, swap_core)
        if t <= groups:
            sends["x"] = (x_own[t - 1], swap_y)
        work, given = None, ()
        if t == 1:
            sends["k"] = (block_kinds.astype(F32), swap_y)
            hop(sends)
            work = lambda *v: (half_of(lay, member_ids, True, *v[:6], v[6:]),)
            given = (*shards, *dense_shards)
        elif t == 2:
            work, given = prepare_own, (block_kinds, x_own)
        arrived, done = slot(sends, work, given, ("r", "l") if t == 1 else ())
        if t == 1:
            kinds_other = arrived["k"]
            pieces.add(0, 0, 0, own)
            pieces.add(0, 1, 0, done[0])
        elif t == 2:
            step, season_own, low_own, own_counts, trend_low, order = done
        if "x" in arrived:
            x_other.append(arrived["x"])
        if "gain" in arrived:
            gains = gains + arrived["gain"]
        if t > 1:
            pieces.add(source(1 - t), 1, 0, arrived["cr"])
            pieces.add(source(t - 1), 1, 0, arrived["cl"])
        whole_r, whole_l = arrived["r"], arrived["l"]
        pieces.add(source(-t), 0, 0, whole_r)
        pieces.add(source(t), 0, 0, whole_l)
    middle = lay.si_half
    sends = {"r": (whole_r[:si_rows], right), "l": (whole_l[si_rows:middle], left)}
    sends["cr"], sends["cl"] = (whole_r, swap_core), (whole_l, swap_core)
    hop(sends)
    arrived, done = slot(sends, prepare_other, (step, kinds_other, *x_other))
    kinds_other, season_other, low_other = done
    if "gain" in arrived:
        gains = gains + arrived["gain"]
    pieces.add(source(1 - last), 1, 0, arrived["cr"])
    pieces.add(source(last - 1), 1, 0, arrived["cl"])
    si_r, si_l = arrived["r"], arrived["l"]
    pieces.add(source(last), 0, 0, si_r)
    pieces.add(source(last), 0, si_rows, si_l)
    sends = {"cr": (si_r, swap_core), "cl": (si_l, swap_core)}
    hop(sends)
    arrived, _ = slot(sends)
    if "gain" in arrived:
        gains = gains + arrived["gain"]
    pieces.add(source(last), 1, 0, arrived["cr"])
    pieces.add(source(last), 1, si_rows, arrived["cl"])
    for move_gains in hops:
        gains = gains + move_gains(gains)
    gain_b, gain_m, gain_o = gains[0:1], gains[1:2], gains[2:3]

    def run_shrink(low_own, low_other, *arrays):
        pieces.arrays = list(arrays)
        return shrink_forward(
            lay, where, pieces, low_own, low_other, block_kinds, kinds_other, gain_b
        )

    cut_at = middle + half_rows
    sends = {"r": (whole_r[middle:cut_at], right), "l": (whole_l[cut_at:], left)}
    arrived, done = slot(sends, run_shrink, (low_own, low_other, *pieces.arrays))
    shrunk, iso, mixed, age, stacked_rows, si_whole = done
    gf_r, gf_l = arrived["r"], arrived["l"]
    pieces.add(source(last), 0, middle, gf_r)
    pieces.add(source(last), 0, cut_at, gf_l)
    arrived, _ = slot({"cr": (gf_r, swap_core), "cl": (gf_l, swap_core)})
    pieces.add(source(last), 1, middle, arrived["cr"])
    pieces.add(source(last), 1, cut_at, arrived["cl"])
    gf = pieces

    *branch_other, up_other, g_whole = grow_forward(
        lay, where, gf, 1, mixed, season_other, order, gain_b
    )
    branch_other = [v.reshape(length, width) for v in branch_other]
    grads_in = out_grad.reshape(groups, length, width)

    def grow_own(mixed, g_whole, season_own, *arrays):
        gf.arrays = list(arrays)
        made = grow_forward(lay, where, g_whole, 0, mixed, season_own, order, gain_b)
        return (*made, *dense_whole(lay, where, gf))

    arrived, done = slot(
        {"b": (branch_other[0], swap_y)}, grow_own, (mixed, g_whole, season_own, *gf.arrays)
    )
    branch_own = [v.reshape(length, width) for v in done[:groups]]
    up_own, wholes = done[groups], done[groups + 1 :]
    received = [arrived["b"]]
    outs, back_own, back_got, waiting, trend_back, saved, dense_gains = [], [], [], [], [], [], None
    for g in range(groups):
        sends = {}
        if g + 1 < groups:
            sends["b"] = (branch_other[g + 1], swap_y)
        elif waiting:
            sends["j"] = (waiting.pop(0), swap_y)

        def run_dense(mine, got, *wholes, g=g):
            tile = jnp.full((1,), g, jnp.int32)
            return dense(
                lay, where, tile, wholes, mine, got, trend_low, grads_in, gain_m, gain_o
            )

        arrived, made = slot(sends, run_dense, (branch_own[g], received[g], *wholes))
        if "b" in arrived:
            received.append(arrived["b"])
        if "j" in arrived:
            back_got.append(arrived["j"])
        outs.append(made[6])
        back_own.append(made[7])
        waiting.append(made[8])
        trend_back.append(made[5])
        saved.append((made[2], made[0], made[1], made[3], made[4]))
        dense_gains = made[9] if dense_gains is None else dense_gains + made[9]
    series_out = jnp.concatenate(outs)

    ring_order = [n // 2]
    for k in range(n // 2 - 1, 0, -1):
        ring_order += [k, -k]
    ring_order.append(0)
    spot = jnp.zeros((n,), jnp.int32)
    for place, offset in enumerate(ring_order):
        spot = jnp.where(jnp.arange(n) == ring.index(offset), place, spot)

    f_outlet = Outlet(n, lay.f_half, width)
    g_outlet = Outlet(n, lay.g_half, width)
    s_outlet = Outlet(n, lay.si_half + 32, width)

    def run_dense_weights(*arrays):
        mine, got, flat = arrays[:groups], arrays[groups : 2 * groups], arrays[2 * groups :]
        kept = [flat[5 * g : 5 * g + 5] for g in range(groups)]
        return dense_weights(
            lay, where, spot, mine, list(got), trend_low, grads_in, kept, f_outlet
        )

    class Chain:
        def __init__(self, keep, got, halved=True):
            self.keep, self.got, self.halved = keep, got, halved
            self.step = last
            self.r = self.l = None
            self.half = got.shape[1] // 2

        def here(self, place, first=0, rows=None):
            array, i = (place + 1) // 2, 0 if place == 0 else (place - 1) % 2
            rows = self.got.shape[1] if rows is None else rows
            return (first, rows, [(self.keep[array], i, 0), (self.got, place, 0)])

        def jobs(self):
            k, h = self.step, self.half
            if k == 0:
                job = self.here(n - 1)
                job[2].extend([(self.r, None, 0), (self.l, None, 0)])
                return [job]
            if k == last:
                return [self.here(0, 0, h), self.here(0, h, h)] if self.halved else [self.here(0)]
            place = 1 + 2 * (last - 1 - k)
            a, b = self.here(place), self.here(place + 1)
            a[2].append((self.r, None, 0))
            if self.l is not None:
                b[2].append((self.l, None, h if k == last - 1 else 0))
            return [a, b]

    def back_of(grads, g_whole, up, season):
        return grow_backward(lay, where, g_whole, grads, up, season, order, gain_b)

    def weights_and_own(g_whole, up, season, *rest):
        return (
            *run_dense_weights(*rest[groups:]),
            *back_of(rest[:groups], g_whole, up, season),
        )

    sends = {"j%d" % i: (v, swap_y) for i, v in enumerate(waiting)}
    arrived, done = slot(
        sends,
        weights_and_own,
        (g_whole, up_own, season_own, *back_own, *branch_own, *received)
        + tuple(v for k in saved for v in k),
    )
    back_got += [arrived[k] for k in sends]
    steps = last + 1
    f_keep, f_give = done[:steps], done[steps]
    pre_own, mixed_back_own, sum_own, gains_own = done[steps + 1 :]
    chains = {}
    kept = {}
    finals = {}
    t = 0
    while True:
        active = {k: c for k, c in chains.items() if c.step > 0}
        finishing = [k for k, c in chains.items() if c.step == 0 and k + "mine" not in finals]
        if len(active) > 1:
            finishing = []
        if not active and not finishing and "smine" in finals:
            break
        sends, work, given = {}, None, ()
        names = [*active, *finishing]
        jobs = {name: chains[name].jobs() for name in names}
        adder = ring_add if t < 6 else plain_add
        summed = list(adder([j for name in names for j in jobs[name]])) if names else []
        for name in active:
            sends[name + "r"] = (summed.pop(0), right)
            if len(jobs[name]) > 1:
                sends[name + "l"] = (summed.pop(0), left)
        for name in finishing:
            mine = summed.pop(0)
            finals[name + "mine"] = mine
            sends[name + "y"] = (mine, swap_y)
            if name != "f":
                sends[name + "c"] = (mine, swap_core)
        for name in ("f", "g"):
            if name + "late" in finals and name + "sent" not in finals:
                sends[name + "d"] = (finals[name + "late"], swap_core)
                finals[name + "sent"] = True
        if t == 0:
            work = lambda g_whole, up, season, *grads: back_of(grads, g_whole, up, season)
            given = (g_whole, up_other, season_other, *back_got)
            sends["f0"] = (f_give, swap_core)
        elif t == 1:
            work = lambda *v: grow_weight(lay, where, spot, *v, g_outlet)
            given = (mixed, pre_own, pre_other)
        elif t == 2:
            work = lambda *v: shrink_backward(lay, where, *v, age, gain_b)
            given = (si_whole, mixed_back_own, mixed_back_other, shrunk, iso)
            sends["g"] = (g_give, swap_core)
        elif t == 3:
            work = lambda *v: shrink_weight(lay, where, spot, *v, s_outlet)
            given = (iso_pre, shrink_pre, stacked_rows, low_own, low_other, grad_gains)
        elif t == 4:
            work = lambda *v: season_backward(lay, where, *v, order)
            given = (si_whole, shrink_pre, sum_own, sum_other)
            sends["s0"] = (s_give, swap_core)
        if t in (5, 6):
            sends["x"] = (tail_sends[t - 5], swap_y)
        if "s" in finishing:
            work = lambda *v: (*finish(*v[6:]), *grow_out(*v[2:6]), *dense_out(*v[:2]))
            given = tuple(finals[k] for k in ("flate", "fd", "gmine", "gy", "gc", "gd"))
            given += (season_mine, own_counts, *trend_back, *tail)
        arrived, done = slot(sends, work, given)
        if t == 0:
            pre_other, mixed_back_other, sum_other, gains_other = done
            chains["f"] = Chain(f_keep, arrived["f0"], False)
        elif t == 1:
            *g_keep, g_give = done
            chains["g"] = None
        elif t == 2:
            shrink_pre, iso_pre, gains_si = done
            chains["g"] = Chain(g_keep, arrived["g"])
            grad_gains = jnp.concatenate(
                [gains_own + gains_other + gains_si, dense_gains, jnp.zeros((29, width), F32)]
            )
        elif t == 3:
            *s_keep, s_give = done
        elif t == 4:
            season_mine, *tail_sends = done
            tail = []
            chains["s"] = Chain(s_keep, arrived["s0"])

            def finish(season_mine, own_counts, *rest):
                backs, tail = rest[:groups], rest[groups:]
                total = season_mine.astype(F32) + jnp.concatenate(tail).astype(F32)
                rest = jnp.stack(backs) - total
                spread = (rest * (1.0 / WINDOW)).astype(BF)
                averaged = jnp.einsum(
                    "gij,gid->gjd", own_counts, spread, preferred_element_type=F32
                )
                return ((total + averaged).astype(BF),)

            def both(mine, other):
                return jnp.where(core == 0, mine, other), jnp.where(core == 0, other, mine)

            def grow_out(mine, over_y, sibling, sibling_over_y):
                found = []
                for b in range(2):
                    here = (y == 0) if b == 0 else (y == 1)
                    lo, hi = both(
                        jnp.where(here, mine, over_y), jnp.where(here, sibling, sibling_over_y)
                    )
                    cols = [v[r : r + k] for v in (lo, hi) for r, k, _ in lay.g_parts(b)]
                    found.append(jnp.concatenate(cols, axis=1).astype(F32))
                return found

            def dense_out(mine, other):
                lo, hi = both(mine, other)
                z = lay.g_half
                first = [lo[r - z : r - z + k].astype(F32) for r, k, _, _ in lay.f_parts(0)]
                rest = [hi[r - z : r - z + k].astype(F32) for r, k, _, _ in lay.f_parts(1)]
                return (*first, rest[0], jnp.concatenate(rest[1:], axis=1))

        if "x" in arrived:
            tail.append(arrived["x"])
        for name, chain in active.items():
            chain.r, chain.l = arrived[name + "r"], arrived.get(name + "l")
            chain.step -= 1
        for name in ("f", "g"):
            if name + "d" in arrived:
                finals[name + "d"] = arrived[name + "d"]
        for name in finishing:
            finals[name + "y"] = arrived[name + "y"]
            if name != "f":
                finals[name + "c"] = arrived[name + "c"]
            if name == "f":
                mine = finals["fmine"].astype(F32) + arrived["fy"].astype(F32)
                finals["flate"] = mine.astype(BF)
            elif name == "g":
                finals["glate"] = arrived["gy"]
            else:
                series_grad, *others = done
        if chains.get("g", 0) is None:
            del chains["g"]
        t += 1
    s_mine, s_y = finals["smine"], finals["sy"]
    s_core = (finals["sc"], swap_core(s_y))
    fine_grow_grad, coarse_grow_grad, contract_grad, merge_grad, trend_grad, expand_grad = others

    fine_shrink_grad, coarse_shrink_grad, fine_iso_grad, coarse_iso_grad = give_out(
        lay, member_ids, s_mine, s_y, *s_core
    )
    at = lay.si_half
    gain_grads = s_mine[at : at + 3].astype(F32) + s_y[at : at + 3].astype(F32)
    gain_grads = lax.dynamic_slice(gain_grads, (jnp.int32(0), ring.me * share), (3, share))
    return (
        series_out,
        series_grad.reshape(series_in.shape),
        fine_shrink_grad,
        coarse_shrink_grad,
        fine_iso_grad,
        coarse_iso_grad,
        fine_grow_grad,
        coarse_grow_grad,
        merge_grad,
        expand_grad,
        contract_grad,
        trend_grad,
        gain_grads[0],
        gain_grads[1],
        gain_grads[2],
    )


def solution(mesh):
    n = mesh.shape["dp"]
    rows = P(("dp", "group"), None)
    weight = P("dp", None)
    return jax.shard_map(
        lambda *args: on_device(n, *args),
        mesh=mesh,
        in_specs=(rows, P(("dp", "group")), rows) + (weight,) * 10 + (P("dp"),) * 3,
        out_specs=(rows, rows) + (weight,) * 10 + (P("dp"),) * 3,
        check_vma=False,
    )
```
